32 devices in a mesh: groups: 2 (over x), inst: 8 (over z, y), tp: 2 (over core).
Axes of the slice: x: 2, y: 2, z: 4, core: 2. Of those that a mesh axis runs over, the one named last changes fastest.
Arguments:
- queries: bfloat16 [4, 512, 3072], P(None, ('groups', 'inst'), 'tp'), parts along dimension 1, may hold values from -130 to 130
- new_kv: bfloat16 [4, 512, 256], P(None, ('groups', 'inst')), parts along dimension 1, may hold values from -4.5 to 4.5
- cache_pool: bfloat16 [98304, 256], P(('groups', 'inst')), parts along dimension 0, may hold values from -6 to 6
- lengths: int32 [16, 32], P('groups'), parts along dimension 0, may hold values from 1 to 2, as said below
- anchor: int32 [16, 32], P('groups'), parts along dimension 0, may hold values from 0 to 7, as said below
- out_weight: bfloat16 [3072, 3072], P('tp'), may hold values from -0.875 to 0.875
Outputs:
- attended: bfloat16 [4, 512, 3072], P(None, ('groups', 'inst'), 'tp'), parts along dimension 1
The draws below stay inside these ranges and needn't reach their ends.
There are 2 independent parts, one for each index of `groups`. The reference program is written for one: setup_inputs(seed, part) draws one part's arguments, and reference() takes and returns one part's arrays. A program takes and returns all parts, laid end to end along the dimension named above; an argument that names none is the same for every part. Nothing has to cross between parts.
Inputs may be any that keep to these rules, and one draw needn't show every extreme that they name: `lengths`: in every instance exactly 16 requests hold 2 blocks and the others one; the requests' blocks lie in the instance's pool in slot order, each right after the one before, filling its 48 blocks. anchor[d, j] is the instance whose request in slot j moves to slot j of instance d, or d where the slot stays. Exactly 7 slots move; for each of them the source is the destination rotated by one amount, nonzero and different for each moving slot, and one of these amounts is half the number of instances, rounded down; so every instance sends and receives exactly 7 requests, at most one to or from any other instance.
All inputs are finite; a program needn't handle non-finite values.
Results may differ from the reference program's by a relative error of at most 0.009.
Values may be sent and summed in bfloat16 or wider, within the bound.
No kernel may reach another device: no remote copies, remote signals or barrier semaphores. Data moves between devices by JAX's collectives and lax.ppermute only.
A program may use at most 128 MiB of HBM per device.

```python
import math
import jax
import jax.numpy as jnp
from jax import lax

D = 3072
HEADS = 24
HDIM = 128
BLK = 128
MAXB = 2
STEPS = 4
R = 32
KVW = 256
CAPB = 48
MIG = 7
N_INST = 8


def plan_parts(key):
    base = jax.random.fold_in(key, 7)
    key_slots, key_shift, key_len = jax.random.split(base, 3)
    order = jax.random.permutation(key_slots, R).astype(jnp.int32)
    half_turn = N_INST // 2
    others = (jax.random.permutation(key_shift, N_INST - 2) + 1).astype(jnp.int32)
    others = others + (others >= half_turn).astype(jnp.int32)
    rotations = jnp.concatenate([jnp.full((1,), half_turn, jnp.int32), others])
    moving = order[:MIG]
    shift_slot = jnp.zeros((R,), jnp.int32).at[moving].set(rotations[:MIG])
    dest_index = jnp.arange(N_INST, dtype=jnp.int32)
    anchor = (dest_index[:, None] - shift_slot[None, :]) % N_INST
    row_keys = jax.random.split(key_len, N_INST)
    ranks = jax.vmap(lambda row_key: jax.random.permutation(row_key, R))(row_keys)
    lengths = 1 + (ranks < R // 2).astype(jnp.int32)
    return (anchor.astype(jnp.int32), lengths.astype(jnp.int32))


def draw_lengths(key, part):
    return plan_parts(key)[1]


def draw_anchor(key, part):
    return plan_parts(key)[0]


def token_parts(key):
    base = jax.random.fold_in(key, 11)
    key_query, key_keys, key_values = jax.random.split(base, 3)
    total_rows = N_INST * R
    keys_new = jax.random.truncated_normal(key_keys, -4.5, 4.5, (STEPS, total_rows, HDIM), jnp.float32)
    values_new = jax.random.truncated_normal(key_values, -4.5, 4.5, (STEPS, total_rows, HDIM), jnp.float32)
    noise = jax.random.truncated_normal(key_query, -4.5, 4.5, (STEPS, total_rows, HEADS, HDIM), jnp.float32)
    queries = noise + 0.27 * keys_new[:, :, None, :]
    return (queries.reshape(STEPS, total_rows, HEADS * HDIM), jnp.concatenate([keys_new, values_new], axis=-1))


def draw_queries(key, part):
    return token_parts(key)[0].astype(jnp.bfloat16)


def draw_new_kv(key, part):
    return token_parts(key)[1].astype(jnp.bfloat16)


def shard_levels(own_key, dims, cuts, low, largest):
    def one(position, parts):
        draws = jax.random.uniform(jax.random.fold_in(jax.random.fold_in(own_key, 6), position), (parts,), jnp.float32, low / len(cuts), largest / len(cuts))
        return jnp.repeat(jnp.exp(draws), dims[position] // parts).reshape((-1,) + (1,) * (len(dims) - position - 1))

    level = one(*cuts[0])
    for cut in cuts[1:]:
        level = level * one(*cut)
    return level


def bell_draw(own_key, extent, spread, most, shards=(), held_as=jnp.bfloat16):
    loudness = shard_levels(own_key, extent, shards, -0.22, 0.18) if shards else 1.0
    entries = jax.random.normal(own_key, extent, jnp.float32) * spread * loudness
    return jnp.minimum(jnp.maximum(entries, -most), most).astype(held_as)


def setup_inputs(seed: int = 0, part: int = 0) -> dict:
    arg_keys = jax.random.split(jax.random.key(seed), 7)
    own_keys = jax.random.split(jax.random.fold_in(arg_keys[6], part), 7)
    return {
        "queries": draw_queries(jax.random.fold_in(jax.random.fold_in(arg_keys[6], part), 71), part),
        "new_kv": draw_new_kv(jax.random.fold_in(jax.random.fold_in(arg_keys[6], part), 71), part),
        "cache_pool": bell_draw(own_keys[2], (N_INST * CAPB * BLK, KVW), 1.0, 6.0, ((0, 8),)),
        "lengths": draw_lengths(jax.random.fold_in(jax.random.fold_in(arg_keys[6], part), 71), part),
        "anchor": draw_anchor(jax.random.fold_in(jax.random.fold_in(arg_keys[6], part), 71), part),
        "out_weight": bell_draw(arg_keys[5], (HEADS * HDIM, D), (HEADS * HDIM // 64) ** -0.5, 0.875, ((0, 2),)),
    }


def reference(queries, new_kv, cache_pool, lengths, anchor, out_weight):
    window_rows = MAXB * BLK
    pool_rows = CAPB * BLK
    slot_ids = jnp.arange(R, dtype=jnp.int32)
    within = jnp.arange(window_rows, dtype=jnp.int32)
    step_ids = jnp.arange(STEPS, dtype=jnp.int32)
    offsets = (jnp.cumsum(lengths, axis=1) - lengths).astype(jnp.int32)
    score_scale = 1.0 / math.sqrt(HDIM)
    causal = step_ids[:, None] >= step_ids[None, :]

    def per_instance(dest):
        source = anchor[dest]
        start_row = (source * pool_rows + offsets[source, slot_ids] * BLK).astype(jnp.int32)
        row_count = lengths[source, slot_ids] * BLK
        row_index = jnp.minimum(start_row[:, None] + within[None, :], cache_pool.shape[0] - 1)
        cached = cache_pool[row_index]
        valid_rows = within[None, :] < row_count[:, None]
        query_part = lax.dynamic_slice_in_dim(queries, (dest * R).astype(jnp.int32), R, 1)
        fresh_rows = lax.dynamic_slice_in_dim(new_kv, (dest * R).astype(jnp.int32), R, 1)
        query_heads = query_part.astype(jnp.float32).reshape(STEPS, R, HEADS, HDIM)
        cache_keys = cached[:, :, :HDIM].astype(jnp.float32)
        cache_values = cached[:, :, HDIM:].astype(jnp.float32)
        fresh_keys = fresh_rows[:, :, :HDIM].astype(jnp.float32)
        fresh_values = fresh_rows[:, :, HDIM:].astype(jnp.float32)
        cache_scores = jnp.einsum('srhe,rte->srht', query_heads, cache_keys) * score_scale
        cache_scores = jnp.where(valid_rows[None, :, None, :], cache_scores, -jnp.inf)
        fresh_scores = jnp.einsum('srhe,ure->srhu', query_heads, fresh_keys) * score_scale
        fresh_scores = jnp.where(causal[:, None, None, :], fresh_scores, -jnp.inf)
        row_max = jnp.maximum(lax.optimization_barrier(jnp.max(cache_scores, axis=-1)), lax.optimization_barrier(jnp.max(fresh_scores, axis=-1)))
        exp_cache = jnp.exp(cache_scores - row_max[..., None])
        exp_fresh = jnp.exp(fresh_scores - row_max[..., None])
        denominator = lax.optimization_barrier(jnp.sum(exp_cache, axis=-1)) + lax.optimization_barrier(jnp.sum(exp_fresh, axis=-1))
        weight_cache = (exp_cache / denominator[..., None]).astype(jnp.bfloat16).astype(jnp.float32)
        weight_fresh = (exp_fresh / denominator[..., None]).astype(jnp.bfloat16).astype(jnp.float32)
        head_out = jnp.einsum('srht,rte->srhe', weight_cache, cache_values)
        head_out = head_out + jnp.einsum('srhu,ure->srhe', weight_fresh, fresh_values)
        attn = head_out.reshape(STEPS * R, HEADS * HDIM).astype(jnp.bfloat16)
        projected = jnp.dot(attn, out_weight, preferred_element_type=jnp.float32)
        return projected.reshape(STEPS, R, D).astype(jnp.bfloat16)
    per_dest = lax.map(per_instance, jnp.arange(N_INST, dtype=jnp.int32))
    return jnp.transpose(per_dest, (1, 0, 2, 3)).reshape(STEPS, N_INST * R, D)
```

```python
import functools
import math

import jax
import jax.numpy as jnp
from jax import lax
from jax.experimental import pallas as pl
from jax.experimental.pallas import tpu as pltpu
from jax.sharding import PartitionSpec as P

HDIM = 128
BLK = 128
MAXB = 2
WIN = MAXB * BLK
PAD = 8
MIB = 1024 * 1024


def plan_kernel(ops, place, anchor, lengths, pool, table, *refs):
    sends, half, offs, sems = refs[:ops], refs[ops], refs[ops + 1], refs[ops + 2]
    insts, slots = anchor.shape
    blocks = pool.shape[0] // BLK
    own, core = place[0], place[1]
    for m in range(insts):
        table[0, m] = slots
        table[1, m] = 1
        offs[m] = 0
    start = jnp.int32(0)
    for j in range(slots):
        source = anchor[own, j]
        dest = (2 * own - source) & (insts - 1)
        table[0, own ^ source] = j
        table[1, own ^ source] = lengths[source, j]
        offs[own ^ dest] = start
        start = start + lengths[own, j]

    def block(at, to, sem):
        row = pl.multiple_of(jnp.minimum(at, blocks - 1) * BLK, BLK)
        copy = pltpu.make_async_copy(pool.at[pl.ds(row, BLK)], to, sem)
        copy.start()
        return copy

    copies = []
    for i in range(ops):
        at = offs[insts - 1 - 2 * i - core]
        for b in range(MAXB):
            copies.append(block(at + b, sends[i].at[pl.ds(b * BLK, BLK)], sems.at[i * MAXB + b]))
    copies.append(block(offs[1] + core, half, sems.at[ops * MAXB]))
    for copy in copies:
        copy.wait()


def attend(query, keys, values, fresh_keys, fresh_values, cached_ok, fresh_ok):
    contract = (((1,), (1,)), ((), ()))
    scale = math.log2(math.e) / math.sqrt(HDIM)
    cached = lax.dot_general(query, keys, contract, preferred_element_type=jnp.float32)
    fresh = lax.dot_general(query, fresh_keys, contract, preferred_element_type=jnp.float32)
    cached = jnp.where(cached_ok, cached, -jnp.inf)
    fresh = jnp.where(fresh_ok, fresh, -jnp.inf)
    top = jnp.maximum(
        jnp.max(cached, axis=1, keepdims=True), jnp.max(fresh, axis=1, keepdims=True)
    )
    cached = jnp.exp2((cached - top) * scale)
    fresh = jnp.exp2((fresh - top) * scale)
    total = jnp.sum(cached, axis=1, keepdims=True) + jnp.sum(fresh, axis=1, keepdims=True)
    mixed = jnp.dot(
        cached.astype(jnp.bfloat16), values, preferred_element_type=jnp.float32
    ) + jnp.dot(fresh.astype(jnp.bfloat16), fresh_values, preferred_element_type=jnp.float32)
    return mixed / total


def masks(rows, heads, slots, fresh_count):
    step = lax.broadcasted_iota(jnp.int32, (rows, fresh_count), 0) // heads
    col = lax.broadcasted_iota(jnp.int32, (rows, fresh_count), 1)
    owner = jnp.where(col // slots <= step, col % slots, -1)
    within = lax.broadcasted_iota(jnp.int32, (rows, WIN), 1)
    return owner, within


def stay_kernel(
    stride, group, place, table, lengths, queries, fresh, pool, attn, moved_q, held, spread, sem
):
    steps, slots, width = queries.shape
    heads = width // HDIM
    rows = steps * heads
    pool_rows = pool.shape[0]
    own = place[0]
    copy = pltpu.make_async_copy(pool, held.at[pl.ds(0, pool_rows)], sem.at[0])
    copy.start()
    held[pl.ds(pool_rows, BLK), :] = jnp.zeros((BLK, held.shape[1]), held.dtype)
    for s in range(steps):
        for h in range(heads):
            spread[pl.ds((s * heads + h) * stride, slots), :] = queries[
                s, :, h * HDIM : (h + 1) * HDIM
            ].astype(jnp.float32)
    for m in range(moved_q.shape[0]):
        moved_q[m] = spread[pl.ds(table[0, m], rows, stride=stride), :].astype(jnp.bfloat16)
    owner, within = masks(rows, heads, slots, fresh.shape[0])
    copy.wait()

    def some(g, start):
        for u in range(group):
            j = g * group + u
            count = lengths[own, j]
            query = spread[pl.ds(j, rows, stride=stride), :].astype(jnp.bfloat16)
            window = pl.ds(pl.multiple_of(start * BLK, BLK), WIN)
            attn[pl.ds(j, rows, stride=stride), :] = attend(
                query,
                held[window, :HDIM],
                held[window, HDIM:],
                fresh[:, :HDIM],
                fresh[:, HDIM:],
                within < count * BLK,
                owner == j,
            )
            start = start + count
        return start

    lax.fori_loop(0, slots // group, some, jnp.int32(0))


def move_kernel(
    stride, ops, chunks, place, table, moved_q, fresh, attn, weight, *refs
):
    mine, peers = refs[: ops + 1], refs[ops + 1 : 2 * ops + 2]
    partial, lhs, held, q_v, fresh_v, attn_v, weight_v, sems, weight_sems = refs[2 * ops + 2 :]
    insts, rows = moved_q.shape[0], moved_q.shape[1]
    slots = stride - PAD
    steps = lhs.shape[0] // slots
    heads = rows // steps
    half = partial.shape[1]
    core = place[1]
    other = 1 - core
    copies = []

    def bring(source, to):
        copy = pltpu.make_async_copy(source, to, sems.at[len(copies)])
        copy.start()
        copies.append(copy)

    for i in range(ops):
        bring(mine[i], held.at[insts - 1 - 2 * i - core])
        bring(peers[i], held.at[insts - 1 - 2 * i - other])
    bring(mine[ops], held.at[1, pl.ds(pl.multiple_of(core * BLK, BLK), BLK)])
    bring(peers[ops], held.at[1, pl.ds(pl.multiple_of(other * BLK, BLK), BLK)])
    bring(moved_q, q_v)
    bring(fresh, fresh_v)
    bring(attn, attn_v)
    tile = half // chunks
    first = other * half
    loads = []
    for n in range(chunks):
        load = pltpu.make_async_copy(
            weight.at[:, pl.ds(pl.multiple_of(first + n * tile, HDIM), tile)],
            weight_v.at[n],
            weight_sems.at[n],
        )
        load.start()
        loads.append(load)
    owner, within = masks(rows, heads, slots, fresh_v.shape[0])
    for copy in copies:
        copy.wait()
    for m in range(1, insts):
        j = table[0, m]
        attn_v[pl.ds(j, rows, stride=stride), :] = attend(
            q_v[m],
            held[m, :, :HDIM],
            held[m, :, HDIM:],
            fresh_v[:, :HDIM],
            fresh_v[:, HDIM:],
            within < table[1, m] * BLK,
            owner == j,
        )
    for s in range(steps):
        for h in range(heads):
            lhs[s * slots : (s + 1) * slots, h * HDIM : (h + 1) * HDIM] = attn_v[
                pl.ds((s * heads + h) * stride, slots), :
            ].astype(jnp.bfloat16)
    for n in range(chunks):
        loads[n].wait()
        partial[:, n * tile : (n + 1) * tile] = jnp.dot(
            lhs[...], weight_v[n], preferred_element_type=jnp.float32
        ).astype(jnp.bfloat16)


def own_kernel(chunks, place, lhs, weight, out, weight_v, weight_sems):
    half = out.shape[1]
    tile = half // chunks
    first = place[1] * half
    loads = []
    for n in range(chunks):
        load = pltpu.make_async_copy(
            weight.at[:, pl.ds(pl.multiple_of(first + n * tile, HDIM), tile)],
            weight_v.at[n],
            weight_sems.at[n],
        )
        load.start()
        loads.append(load)
    for n in range(chunks):
        loads[n].wait()
        out[:, n * tile : (n + 1) * tile] = jnp.dot(
            lhs[...], weight_v[n], preferred_element_type=jnp.float32
        )


def spec(space):
    return pl.BlockSpec(memory_space=space)


def body(queries, new_kv, cache_pool, lengths, anchor, out_weight):
    steps, slots, width = queries.shape
    heads = width // HDIM
    rows = steps * heads
    insts = lax.axis_size("inst")
    cores = lax.axis_size("tp")
    kvw = cache_pool.shape[1]
    depth, columns = out_weight.shape
    half = columns // cores
    ops = (insts - 2) // 2
    stride = slots + PAD
    smem, vmem, hbm = spec(pltpu.SMEM), spec(pltpu.VMEM), spec(pl.ANY)
    place = jnp.stack([lax.axis_index("inst"), lax.axis_index("tp")]).astype(jnp.int32)
    fresh = new_kv.reshape(steps * slots, kvw)
    sends = pl.pallas_call(
        functools.partial(plan_kernel, ops),
        out_shape=[jax.ShapeDtypeStruct((2, insts), jnp.int32)]
        + [jax.ShapeDtypeStruct((WIN, kvw), jnp.bfloat16)] * ops
        + [jax.ShapeDtypeStruct((BLK, kvw), jnp.bfloat16)],
        in_specs=[smem, smem, smem, hbm],
        out_specs=[smem] + [hbm] * (ops + 1),
        scratch_shapes=[pltpu.SMEM((insts,), jnp.int32), pltpu.SemaphoreType.DMA((ops * MAXB + 1,))],
    )(place, anchor, lengths, cache_pool)
    table, sends = sends[0], sends[1:]

    mine = [None] * (ops + 1)
    for i in reversed(range(ops + 1)):
        pairs = []
        for a in range(insts):
            for c in range(cores):
                m = insts - 1 - 2 * i - c if i < ops else 1
                pairs.append((a * cores + c, (a ^ m) * cores + c))
        mine[i] = lax.ppermute(sends[i], ("inst", "tp"), pairs)
    swap = [(c, cores - 1 - c) for c in range(cores)]
    peers = [lax.ppermute(block, "tp", swap) for block in mine]

    attn, moved_q = pl.pallas_call(
        functools.partial(stay_kernel, stride, 4),
        out_shape=[
            jax.ShapeDtypeStruct((rows * stride, HDIM), jnp.float32),
            jax.ShapeDtypeStruct((insts, rows, HDIM), jnp.bfloat16),
        ],
        in_specs=[smem, smem, smem, vmem, vmem, hbm],
        out_specs=[vmem, vmem],
        scratch_shapes=[
            pltpu.VMEM((cache_pool.shape[0] + BLK, kvw), jnp.bfloat16),
            pltpu.VMEM((rows * stride, HDIM), jnp.float32),
            pltpu.SemaphoreType.DMA((1,)),
        ],
        compiler_params=pltpu.CompilerParams(vmem_limit_bytes=24 * MIB),
        cost_estimate=pl.CostEstimate(
            flops=4 * slots * rows * WIN * HDIM, bytes_accessed=16 * MIB, transcendentals=0
        ),
    )(place, table, lengths, queries, fresh, cache_pool)

    chunks = 4
    tile = half // chunks
    partial, lhs = pl.pallas_call(
        functools.partial(move_kernel, stride, ops, chunks),
        out_shape=[
            jax.ShapeDtypeStruct((steps * slots, half), jnp.bfloat16),
            jax.ShapeDtypeStruct((steps * slots, width), jnp.bfloat16),
        ],
        in_specs=[smem, smem] + [hbm] * (4 + 2 * (ops + 1)),
        out_specs=[vmem, vmem],
        scratch_shapes=[
            pltpu.VMEM((insts, WIN, kvw), jnp.bfloat16),
            pltpu.VMEM((insts, rows, HDIM), jnp.bfloat16),
            pltpu.VMEM((steps * slots, kvw), jnp.bfloat16),
            pltpu.VMEM((rows * stride, HDIM), jnp.float32),
            pltpu.VMEM((chunks, depth, tile), jnp.bfloat16),
            pltpu.SemaphoreType.DMA((2 * (ops + 1) + 3,)),
            pltpu.SemaphoreType.DMA((chunks,)),
        ],
        compiler_params=pltpu.CompilerParams(vmem_limit_bytes=32 * MIB),
    )(place, table, moved_q, fresh, attn, out_weight, *mine, *peers)

    arrived = lax.ppermute(partial, "tp", swap)
    own = pl.pallas_call(
        functools.partial(own_kernel, chunks),
        out_shape=jax.ShapeDtypeStruct((steps * slots, half), jnp.float32),
        in_specs=[smem, vmem, hbm],
        out_specs=vmem,
        scratch_shapes=[
            pltpu.VMEM((chunks, depth, tile), jnp.bfloat16),
            pltpu.SemaphoreType.DMA((chunks,)),
        ],
        compiler_params=pltpu.CompilerParams(vmem_limit_bytes=24 * MIB),
        cost_estimate=pl.CostEstimate(
            flops=2 * steps * slots * width * half, bytes_accessed=6 * MIB, transcendentals=0
        ),
    )(place, lhs, out_weight)
    result = (own + arrived.astype(jnp.float32)).astype(jnp.bfloat16)
    return result.reshape(steps, slots, half)


def solution(mesh):
    placed = (
        P(None, ("groups", "inst"), "tp"),
        P(None, ("groups", "inst"), None),
        P(("groups", "inst"), None),
        P("groups", None),
        P("groups", None),
        P("tp", None),
    )
    return jax.shard_map(
        body,
        mesh=mesh,
        in_specs=placed,
        out_specs=P(None, ("groups", "inst"), "tp"),
        check_vma=False,
    )
```

```python
import functools
import math

import jax
import jax.numpy as jnp
from jax import lax
from jax.experimental import pallas as pl
from jax.experimental.pallas import tpu as pltpu
from jax.sharding import PartitionSpec as P

HDIM = 128
BLK = 128
MAXB = 2
WIN = MAXB * BLK
PAD = 8
MIB = 1024 * 1024


def partner(insts, ops, i, core):
    return jnp.int32(1) if i == ops - 1 else insts - 1 - 2 * i - core


def start_copies(pairs, sems):
    copies = [pltpu.make_async_copy(a, b, sems.at[n]) for n, (a, b) in enumerate(pairs)]
    for copy in copies:
        copy.start()
    return copies


def plan_kernel(ops, anchor_h, lengths_h, pool, table, *refs):
    sends, (anchor, lengths, offs, sems) = refs[:ops], refs[ops:]
    insts, slots = anchor.shape
    blocks = pool.shape[0] // BLK
    own, core = lax.axis_index("inst"), lax.axis_index("tp")
    for copy in start_copies([(anchor_h, anchor), (lengths_h, lengths)], sems):
        copy.wait()
    for m in range(insts):
        table[0, m] = slots
        table[1, m] = 1
        offs[m] = 0
    start = jnp.int32(0)
    for j in range(slots):
        source = anchor[own, j]
        dest = (2 * own - source) & (insts - 1)
        table[0, own ^ source] = j
        table[1, own ^ source] = lengths[source, j]
        offs[own ^ dest] = start
        start = start + lengths[own, j]
    pairs = []
    for i in range(ops):
        at = offs[partner(insts, ops, i, core)]
        for b in range(MAXB):
            row = pl.multiple_of(jnp.minimum(at + b, blocks - 1) * BLK, BLK)
            pairs.append((pool.at[pl.ds(row, BLK)], sends[i].at[pl.ds(b * BLK, BLK)]))
    for copy in start_copies(pairs, sems):
        copy.wait()


def attend(query, keys, values, fresh, fresh_ok, cached_ok=None):
    contract = (((1,), (1,)), ((), ()))
    scale = math.log2(math.e) / math.sqrt(HDIM)
    cached = lax.dot_general(query, keys, contract, preferred_element_type=jnp.float32)
    recent = lax.dot_general(
        query, fresh[:, :HDIM], contract, preferred_element_type=jnp.float32
    )
    if cached_ok is not None:
        cached = jnp.where(cached_ok, cached, -jnp.inf)
    recent = jnp.where(fresh_ok, recent, -jnp.inf)
    top = jnp.maximum(
        jnp.max(cached, axis=1, keepdims=True), jnp.max(recent, axis=1, keepdims=True)
    )
    cached = jnp.exp2((cached - top) * scale)
    recent = jnp.exp2((recent - top) * scale)
    total = jnp.sum(cached, axis=1, keepdims=True) + jnp.sum(recent, axis=1, keepdims=True)
    mixed = jnp.dot(
        cached.astype(jnp.bfloat16), values, preferred_element_type=jnp.float32
    ) + jnp.dot(recent.astype(jnp.bfloat16), fresh[:, HDIM:], preferred_element_type=jnp.float32)
    return mixed / total


def owners(parts, steps, heads, slots):
    shape = (parts * steps * heads, steps * slots)
    step = lax.broadcasted_iota(jnp.int32, shape, 0) // heads % steps
    col = lax.broadcasted_iota(jnp.int32, shape, 1)
    return jnp.where(col // slots <= step, col % slots, -1)


def stay_kernel(
    stride, group, ops, table, queries_h, fresh_h, pool_h, lengths_h, weight_h,
    attn, own_q, sent_q, fresh, peer_w, own_w,
    queries, pool, lengths, order, starts, spread, sems,
):
    steps, slots, width = queries.shape
    insts = lengths.shape[0]
    heads = width // HDIM
    rows = steps * heads
    half = own_w.shape[1]
    own, core = lax.axis_index("inst"), lax.axis_index("tp")
    own_cols = pl.ds(pl.multiple_of(core * half, HDIM), half)
    peer_cols = pl.ds(pl.multiple_of((1 - core) * half, HDIM), half)
    loads = start_copies(
        [
            (lengths_h, lengths),
            (queries_h, queries),
            (fresh_h, fresh),
            (pool_h, pool),
            (weight_h.at[:, peer_cols], peer_w),
            (weight_h.at[:, own_cols], own_w),
        ],
        sems,
    )
    loads[0].wait()
    longer = pool.shape[0] // BLK - slots
    start, found = jnp.int32(0), jnp.int32(0)
    for j in range(slots):
        count = lengths[own, j]
        more = count - 1
        place = jnp.where(more > 0, found, longer + j - found)
        order[place] = j
        starts[place] = start
        start = start + count
        found = found + more
    loads[1].wait()
    for s in range(steps):
        for h in range(heads):
            spread[pl.ds((s * heads + h) * stride, slots), :] = queries[
                s, :, h * HDIM : (h + 1) * HDIM
            ].astype(jnp.float32)

    def rows_of(j):
        return spread[pl.ds(j, rows, stride=stride), :].astype(jnp.bfloat16)

    for i in range(ops):
        own_q[i] = rows_of(table[0, partner(insts, ops, i, core)])
    for i in range(ops - 1):
        sent_q[i] = rows_of(table[0, partner(insts, ops, i, 1 - core)])
    owner = owners(1, steps, heads, slots)
    loads[2].wait()
    loads[3].wait()

    def some(first, size, g, _):
        found = []
        for u in range(group):
            at = first + g * group + u
            j = order[at]
            window = pl.ds(pl.multiple_of(starts[at] * BLK, BLK), size)
            out = attend(
                rows_of(j), pool[window, :HDIM], pool[window, HDIM:], fresh[...], owner == j
            )
            found.append((j, out))
        for j, out in found:
            attn[pl.ds(j, rows, stride=stride), :] = out
        return 0

    lax.fori_loop(0, longer // group, functools.partial(some, 0, WIN), 0)
    lax.fori_loop(0, (slots - longer) // group, functools.partial(some, longer, BLK), 0)
    loads[4].wait()
    loads[5].wait()


def move_kernel(ops, steps, slots, table, own_q, peer_q, fresh, *refs):
    blocks, (found, sent) = refs[:ops], refs[ops:]
    rows = own_q.shape[1]
    heads = rows // steps
    insts = table.shape[1]
    core = lax.axis_index("tp")
    within = lax.broadcasted_iota(jnp.int32, (2 * rows, WIN), 1)
    owner = owners(2, steps, heads, slots)
    for i in range(ops):
        m = partner(insts, ops, i, core)
        both = i < ops - 1
        count = 2 * rows if both else rows
        query = jnp.concatenate([own_q[i], peer_q[i]]) if both else own_q[i]
        out = attend(
            query,
            blocks[i][:, :HDIM],
            blocks[i][:, HDIM:],
            fresh[...],
            owner[:count] == table[0, m],
            within[:count] < table[1, m] * BLK,
        )
        found[i] = out[:rows]
        if both:
            sent[i] = out[rows:].astype(jnp.bfloat16)


def project_kernel(ops, stride, chunks, table, attn, found, arrived, weight, partial, lhs, merged):
    rows = found.shape[1]
    insts = table.shape[1]
    slots = stride - PAD
    steps = lhs.shape[0] // slots
    heads = rows // steps
    core = lax.axis_index("tp")
    merged[...] = attn[...]
    for i in range(ops):
        j = table[0, partner(insts, ops, i, core)]
        merged[pl.ds(j, rows, stride=stride), :] = found[i]
    for i in range(ops - 1):
        j = table[0, partner(insts, ops, i, 1 - core)]
        merged[pl.ds(j, rows, stride=stride), :] = arrived[i].astype(jnp.float32)
    for s in range(steps):
        for h in range(heads):
            lhs[s * slots : (s + 1) * slots, h * HDIM : (h + 1) * HDIM] = merged[
                pl.ds((s * heads + h) * stride, slots), :
            ].astype(jnp.bfloat16)
    tile = partial.shape[1] // chunks
    for n in range(chunks):
        cols = slice(n * tile, (n + 1) * tile)
        partial[:, cols] = jnp.dot(
            lhs[...], weight[:, cols], preferred_element_type=jnp.float32
        ).astype(jnp.bfloat16)


def own_kernel(chunks, lhs, weight, out):
    tile = out.shape[1] // chunks
    for n in range(chunks):
        cols = slice(n * tile, (n + 1) * tile)
        out[:, cols] = jnp.dot(lhs[...], weight[:, cols], preferred_element_type=jnp.float32)


def call(kernel, operands, outs, scratch=(), limit=8, cost=None):
    specs = [pl.BlockSpec(memory_space=space) for space, _ in operands]
    return pl.pallas_call(
        kernel,
        out_shape=[space(shape.shape, shape.dtype) for space, shape in outs],
        in_specs=specs,
        out_specs=[pl.BlockSpec(memory_space=space) for space, _ in outs],
        scratch_shapes=list(scratch),
        compiler_params=pltpu.CompilerParams(vmem_limit_bytes=limit * MIB),
        cost_estimate=cost,
    )(*[pltpu.with_memory_space_constraint(array, space) for space, array in operands])


def body(queries, new_kv, cache_pool, lengths, anchor, out_weight):
    steps, slots, width = queries.shape
    heads = width // HDIM
    rows = steps * heads
    insts = lax.axis_size("inst")
    cores = lax.axis_size("tp")
    kvw = cache_pool.shape[1]
    depth, columns = out_weight.shape
    half = columns // cores
    ops = insts // 2
    stride = slots + PAD
    hbm, vmem, smem = pltpu.HBM, pltpu.VMEM, pltpu.SMEM
    dma = pltpu.SemaphoreType.DMA

    def bf16(*shape):
        return jax.ShapeDtypeStruct(shape, jnp.bfloat16)

    def f32(*shape):
        return jax.ShapeDtypeStruct(shape, jnp.float32)

    table, *sends = call(
        functools.partial(plan_kernel, ops),
        [(hbm, anchor), (hbm, lengths), (hbm, cache_pool)],
        [(smem, jax.ShapeDtypeStruct((2, insts), jnp.int32))] + [(vmem, bf16(WIN, kvw))] * ops,
        [
            smem(anchor.shape, jnp.int32),
            smem(lengths.shape, jnp.int32),
            smem((insts,), jnp.int32),
            dma((ops * MAXB,)),
        ],
    )
    blocks = [None] * ops
    for i in reversed(range(ops)):
        pairs = []
        for a in range(insts):
            for c in range(cores):
                m = 1 if i == ops - 1 else insts - 1 - 2 * i - c
                pairs.append((a * cores + c, (a ^ m) * cores + c))
        blocks[i] = lax.ppermute(sends[i], ("inst", "tp"), pairs)

    attn, own_q, sent_q, fresh, peer_w, own_w = call(
        functools.partial(stay_kernel, stride, 4, ops),
        [
            (smem, table),
            (hbm, queries),
            (hbm, new_kv.reshape(steps * slots, kvw)),
            (hbm, cache_pool),
            (hbm, lengths),
            (hbm, out_weight),
        ],
        [
            (vmem, f32(rows * stride, HDIM)),
            (vmem, bf16(ops, rows, HDIM)),
            (vmem, bf16(ops - 1, rows, HDIM)),
            (vmem, bf16(steps * slots, kvw)),
            (vmem, bf16(depth, half)),
            (vmem, bf16(depth, half)),
        ],
        [
            vmem(queries.shape, jnp.bfloat16),
            vmem(cache_pool.shape, jnp.bfloat16),
            smem(lengths.shape, jnp.int32),
            smem((slots,), jnp.int32),
            smem((slots,), jnp.int32),
            vmem((rows * stride, HDIM), jnp.float32),
            dma((6,)),
        ],
        limit=12,
        cost=pl.CostEstimate(
            flops=4 * slots * rows * WIN * HDIM, bytes_accessed=24 * MIB, transcendentals=0
        ),
    )
    swap = [(c, cores - 1 - c) for c in range(cores)]
    peer_q = lax.ppermute(sent_q, "tp", swap)

    found, sent = call(
        functools.partial(move_kernel, ops, steps, slots),
        [(smem, table), (vmem, own_q), (vmem, peer_q), (vmem, fresh)]
        + [(vmem, block) for block in blocks],
        [(vmem, f32(ops, rows, HDIM)), (vmem, bf16(ops - 1, rows, HDIM))],
    )
    arrived = lax.ppermute(sent, "tp", swap)
    chunks = 4
    partial, lhs = call(
        functools.partial(project_kernel, ops, stride, chunks),
        [(smem, table), (vmem, attn), (vmem, found), (vmem, arrived), (vmem, peer_w)],
        [(vmem, bf16(steps * slots, half)), (vmem, bf16(steps * slots, width))],
        [vmem((rows * stride, HDIM), jnp.float32)],
    )
    others = lax.ppermute(partial, "tp", swap)
    (own,) = call(
        functools.partial(own_kernel, chunks),
        [(vmem, lhs), (vmem, own_w)],
        [(vmem, f32(steps * slots, half))],
        cost=pl.CostEstimate(
            flops=2 * steps * slots * width * half, bytes_accessed=6 * MIB, transcendentals=0
        ),
    )
    result = (own + others.astype(jnp.float32)).astype(jnp.bfloat16)
    return result.reshape(steps, slots, half)


def solution(mesh):
    placed = (
        P(None, ("groups", "inst"), "tp"),
        P(None, ("groups", "inst"), None),
        P(("groups", "inst"), None),
        P("groups", None),
        P("groups", None),
        P("tp", None),
    )
    return jax.shard_map(
        body,
        mesh=mesh,
        in_specs=placed,
        out_specs=P(None, ("groups", "inst"), "tp"),
        check_vma=False,
    )
```

```python
import functools
import math

import jax
import jax.numpy as jnp
from jax import lax
from jax.experimental import pallas as pl
from jax.experimental.pallas import tpu as pltpu
from jax.sharding import PartitionSpec as P

HDIM = 128
BLK = 128
MAXB = 2
WIN = MAXB * BLK
PAD = 8
MIB = 1024 * 1024


def partner(insts, ops, i, core):
    return jnp.int32(1) if i == ops - 1 else insts - 1 - 2 * i - core


def start_copies(pairs, sems):
    copies = [pltpu.make_async_copy(a, b, sems.at[n]) for n, (a, b) in enumerate(pairs)]
    for copy in copies:
        copy.start()
    return copies


def plan_kernel(ops, anchor_h, lengths_h, pool, table, *refs):
    sends, (anchor, lengths, offs, sems) = refs[:ops], refs[ops:]
    insts, slots = anchor.shape
    blocks = pool.shape[0] // BLK
    own, core = lax.axis_index("inst"), lax.axis_index("tp")
    for copy in start_copies([(anchor_h, anchor), (lengths_h, lengths)], sems):
        copy.wait()
    for m in range(insts):
        table[0, m] = slots
        table[1, m] = 1
        offs[m] = 0
    start = jnp.int32(0)
    for j in range(slots):
        source = anchor[own, j]
        dest = (2 * own - source) & (insts - 1)
        table[0, own ^ source] = j
        table[1, own ^ source] = lengths[source, j]
        offs[own ^ dest] = start
        start = start + lengths[own, j]
    pairs = []
    for i in range(ops):
        at = offs[partner(insts, ops, i, core)]
        for b in range(MAXB):
            row = pl.multiple_of(jnp.minimum(at + b, blocks - 1) * BLK, BLK)
            pairs.append((pool.at[pl.ds(row, BLK)], sends[i].at[pl.ds(b * BLK, BLK)]))
    for copy in start_copies(pairs, sems):
        copy.wait()


def contract_last(a, b):
    return lax.dot_general(a, b, (((1,), (1,)), ((), ())), preferred_element_type=jnp.float32)


def widest(score):
    return functools.reduce(
        jnp.maximum, [score[:, k : k + HDIM] for k in range(0, score.shape[1], HDIM)]
    )


def attend_all(scores, recents, values):
    scale = math.log2(math.e) / math.sqrt(HDIM)
    weights = []
    for score, recent in zip(scores, recents):
        top = jnp.max(jnp.maximum(widest(score), recent), axis=1, keepdims=True)
        cached = jnp.exp2((score - top) * scale)
        late = jnp.exp2((recent - top) * scale)
        folded = sum([cached[:, k : k + HDIM] for k in range(0, cached.shape[1], HDIM)], late)
        share = 1.0 / jnp.sum(folded, axis=1, keepdims=True)
        weights.append((cached.astype(jnp.bfloat16), late * share, share))
    return [
        (jnp.dot(cached, value, preferred_element_type=jnp.float32) * share, late)
        for (cached, late, share), value in zip(weights, values)
    ]


def query_kernel(stride, ops, table, queries_h, spread, own_q, sent_q, queries, sems):
    steps, slots, width = queries.shape
    insts = table.shape[1]
    heads = width // HDIM
    rows = steps * heads
    core = lax.axis_index("tp")
    start_copies([(queries_h, queries)], sems)[0].wait()
    for s in range(steps):
        for h in range(heads):
            spread[pl.ds((s * heads + h) * stride, slots), :] = queries[
                s, :, h * HDIM : (h + 1) * HDIM
            ].astype(jnp.float32)
    for i in range(ops):
        j = table[0, partner(insts, ops, i, core)]
        own_q[i] = spread[pl.ds(j, rows, stride=stride), :].astype(jnp.bfloat16)
    for i in range(ops - 1):
        j = table[0, partner(insts, ops, i, 1 - core)]
        sent_q[i] = spread[pl.ds(j, rows, stride=stride), :].astype(jnp.bfloat16)


def stay_kernel(
    stride, steps, group, spread, fresh_h, pool_h, lengths_h, weight_h,
    attn, fresh, peer_w, own_w,
    pool, lengths, order, starts, recent, late, sems,
):
    slots = lengths.shape[1]
    rows = spread.shape[0] // stride
    heads = rows // steps
    half = own_w.shape[1]
    own, core = lax.axis_index("inst"), lax.axis_index("tp")
    own_cols = pl.ds(pl.multiple_of(core * half, HDIM), half)
    peer_cols = pl.ds(pl.multiple_of((1 - core) * half, HDIM), half)
    loads = start_copies(
        [
            (lengths_h, lengths),
            (fresh_h, fresh),
            (pool_h, pool),
            (weight_h.at[:, peer_cols], peer_w),
            (weight_h.at[:, own_cols], own_w),
        ],
        sems,
    )
    loads[0].wait()
    longer = pool.shape[0] // BLK - slots
    group = math.gcd(group, longer, slots - longer)
    start, found = jnp.int32(0), jnp.int32(0)
    for j in range(slots):
        count = lengths[own, j]
        place = jnp.where(count > 1, found, longer + j - found)
        order[place] = j
        starts[place] = start
        start = start + count
        found = found + count - 1
    loads[1].wait()
    slot = lax.broadcasted_iota(jnp.int32, (slots, steps * slots), 0)
    col = lax.broadcasted_iota(jnp.int32, (slots, steps * slots), 1)
    for i in range(rows):
        at = pl.ds(i * stride, slots)
        score = contract_last(spread[at, :].astype(jnp.bfloat16), fresh[:, :HDIM])
        mine = (col % slots == slot) & (col // slots <= i // heads)
        recent[at, :] = jnp.where(mine, score, -jnp.inf)
    loads[2].wait()

    def some(first, size, g, _):
        places = [first + g * group + u for u in range(group)]
        picked = [pl.ds(order[at], rows, stride=stride) for at in places]
        windows = [pl.ds(pl.multiple_of(starts[at] * BLK, BLK), size) for at in places]
        queries = [spread[at, :].astype(jnp.bfloat16) for at in picked]
        recents = [recent[at, :] for at in picked]
        scores = [contract_last(q, pool[w, :HDIM]) for q, w in zip(queries, windows)]
        done = attend_all(scores, recents, [pool[w, HDIM:] for w in windows])
        for at, (mixed, weight) in zip(picked, done):
            attn[at, :] = mixed
            late[at, :] = weight
        return 0

    lax.fori_loop(0, longer // group, functools.partial(some, 0, WIN), 0)
    lax.fori_loop(0, (slots - longer) // group, functools.partial(some, longer, BLK), 0)
    for i in range(rows):
        at = pl.ds(i * stride, slots)
        attn[at, :] = attn[at, :] + jnp.dot(
            late[at, :].astype(jnp.bfloat16), fresh[:, HDIM:], preferred_element_type=jnp.float32
        )
    loads[3].wait()
    loads[4].wait()


def move_kernel(ops, steps, slots, group, table, own_q, peer_q, fresh, *refs):
    blocks, (found, sent) = refs[:ops], refs[ops:]
    rows = own_q.shape[1]
    heads = rows // steps
    insts = table.shape[1]
    core = lax.axis_index("tp")
    shape = (2 * rows, steps * slots)
    step = lax.broadcasted_iota(jnp.int32, shape, 0) // heads % steps
    col = lax.broadcasted_iota(jnp.int32, shape, 1)
    owner = jnp.where(col // slots <= step, col % slots, -1)
    within = lax.broadcasted_iota(jnp.int32, (2 * rows, WIN), 1)
    for first in range(0, ops, group):
        batch = range(first, min(first + group, ops))
        queries, recents, scores = [], [], []
        for i in batch:
            query = own_q[i]
            if i < ops - 1:
                query = jnp.concatenate([query, peer_q[i]])
            queries.append(query)
        for i, query in zip(batch, queries):
            m = partner(insts, ops, i, core)
            score = contract_last(query, blocks[i][:, :HDIM])
            limit = table[1, m] * BLK
            scores.append(jnp.where(within[: query.shape[0]] < limit, score, -jnp.inf))
        for i, query in zip(batch, queries):
            recent = contract_last(query, fresh[:, :HDIM])
            j = table[0, partner(insts, ops, i, core)]
            recents.append(jnp.where(owner[: query.shape[0]] == j, recent, -jnp.inf))
        done = attend_all(scores, recents, [blocks[i][:, HDIM:] for i in batch])
        for i, (mixed, weight) in zip(batch, done):
            out = mixed + jnp.dot(
                weight.astype(jnp.bfloat16), fresh[:, HDIM:], preferred_element_type=jnp.float32
            )
            found[i] = out[:rows]
            if i < ops - 1:
                sent[i] = out[rows:].astype(jnp.bfloat16)


def project_kernel(ops, stride, chunks, table, attn, found, arrived, weight, partial, lhs, merged):
    rows = found.shape[1]
    insts = table.shape[1]
    slots = stride - PAD
    steps = lhs.shape[0] // slots
    heads = rows // steps
    core = lax.axis_index("tp")
    merged[...] = attn[...]
    for i in range(ops):
        j = table[0, partner(insts, ops, i, core)]
        merged[pl.ds(j, rows, stride=stride), :] = found[i]
    for i in range(ops - 1):
        j = table[0, partner(insts, ops, i, 1 - core)]
        merged[pl.ds(j, rows, stride=stride), :] = arrived[i].astype(jnp.float32)
    for s in range(steps):
        for h in range(heads):
            lhs[s * slots : (s + 1) * slots, h * HDIM : (h + 1) * HDIM] = merged[
                pl.ds((s * heads + h) * stride, slots), :
            ].astype(jnp.bfloat16)
    tile = partial.shape[1] // chunks
    for n in range(chunks):
        cols = slice(n * tile, (n + 1) * tile)
        partial[:, cols] = jnp.dot(
            lhs[...], weight[:, cols], preferred_element_type=jnp.float32
        ).astype(jnp.bfloat16)


def own_kernel(chunks, lhs, weight, out):
    tile = out.shape[1] // chunks
    for n in range(chunks):
        cols = slice(n * tile, (n + 1) * tile)
        out[:, cols] = jnp.dot(lhs[...], weight[:, cols], preferred_element_type=jnp.float32)


def call(kernel, operands, outs, scratch=(), limit=8, cost=None):
    specs = [pl.BlockSpec(memory_space=space) for space, _ in operands]
    return pl.pallas_call(
        kernel,
        out_shape=[space(shape.shape, shape.dtype) for space, shape in outs],
        in_specs=specs,
        out_specs=[pl.BlockSpec(memory_space=space) for space, _ in outs],
        scratch_shapes=list(scratch),
        compiler_params=pltpu.CompilerParams(vmem_limit_bytes=limit * MIB),
        cost_estimate=cost,
    )(*[pltpu.with_memory_space_constraint(array, space) for space, array in operands])


def body(queries, new_kv, cache_pool, lengths, anchor, out_weight):
    steps, slots, width = queries.shape
    heads = width // HDIM
    rows = steps * heads
    insts = lax.axis_size("inst")
    cores = lax.axis_size("tp")
    kvw = cache_pool.shape[1]
    depth, columns = out_weight.shape
    half = columns // cores
    ops = insts // 2
    stride = slots + PAD
    hbm, vmem, smem = pltpu.HBM, pltpu.VMEM, pltpu.SMEM
    dma = pltpu.SemaphoreType.DMA

    def bf16(*shape):
        return jax.ShapeDtypeStruct(shape, jnp.bfloat16)

    def f32(*shape):
        return jax.ShapeDtypeStruct(shape, jnp.float32)

    table, *sends = call(
        functools.partial(plan_kernel, ops),
        [(hbm, anchor), (hbm, lengths), (hbm, cache_pool)],
        [(smem, jax.ShapeDtypeStruct((2, insts), jnp.int32))] + [(vmem, bf16(WIN, kvw))] * ops,
        [
            smem(anchor.shape, jnp.int32),
            smem(lengths.shape, jnp.int32),
            smem((insts,), jnp.int32),
            dma((ops * MAXB,)),
        ],
    )
    blocks = [None] * ops
    for i in reversed(range(ops)):
        pairs = []
        for a in range(insts):
            for c in range(cores):
                m = 1 if i == ops - 1 else insts - 1 - 2 * i - c
                pairs.append((a * cores + c, (a ^ m) * cores + c))
        blocks[i] = lax.ppermute(sends[i], ("inst", "tp"), pairs)

    spread, own_q, sent_q = call(
        functools.partial(query_kernel, stride, ops),
        [(smem, table), (hbm, queries)],
        [
            (vmem, f32(rows * stride, HDIM)),
            (vmem, bf16(ops, rows, HDIM)),
            (vmem, bf16(ops - 1, rows, HDIM)),
        ],
        [vmem(queries.shape, jnp.bfloat16), dma((1,))],
        cost=pl.CostEstimate(flops=0, bytes_accessed=MIB, transcendentals=0),
    )
    swap = [(c, cores - 1 - c) for c in range(cores)]
    peer_q = lax.ppermute(sent_q, "tp", swap)

    attn, fresh, peer_w, own_w = call(
        functools.partial(stay_kernel, stride, steps, 8),
        [
            (vmem, spread),
            (hbm, new_kv.reshape(steps * slots, kvw)),
            (hbm, cache_pool),
            (hbm, lengths),
            (hbm, out_weight),
        ],
        [
            (vmem, f32(rows * stride, HDIM)),
            (vmem, bf16(steps * slots, kvw)),
            (vmem, bf16(depth, half)),
            (vmem, bf16(depth, half)),
        ],
        [
            vmem(cache_pool.shape, jnp.bfloat16),
            smem(lengths.shape, jnp.int32),
            smem((slots,), jnp.int32),
            smem((slots,), jnp.int32),
            vmem((rows * stride, HDIM), jnp.float32),
            vmem((rows * stride, HDIM), jnp.float32),
            dma((5,)),
        ],
        limit=16,
        cost=pl.CostEstimate(
            flops=4 * slots * rows * WIN * HDIM, bytes_accessed=24 * MIB, transcendentals=0
        ),
    )

    found, sent = call(
        functools.partial(move_kernel, ops, steps, slots, 4),
        [(smem, table), (vmem, own_q), (vmem, peer_q), (vmem, fresh)]
        + [(vmem, block) for block in blocks],
        [(vmem, f32(ops, rows, HDIM)), (vmem, bf16(ops - 1, rows, HDIM))],
    )
    arrived = lax.ppermute(sent, "tp", swap)
    chunks = 4
    partial, lhs = call(
        functools.partial(project_kernel, ops, stride, chunks),
        [(smem, table), (vmem, attn), (vmem, found), (vmem, arrived), (vmem, peer_w)],
        [(vmem, bf16(steps * slots, half)), (vmem, bf16(steps * slots, width))],
        [vmem((rows * stride, HDIM), jnp.float32)],
    )
    others = lax.ppermute(partial, "tp", swap)
    (own,) = call(
        functools.partial(own_kernel, chunks),
        [(vmem, lhs), (vmem, own_w)],
        [(vmem, f32(steps * slots, half))],
        cost=pl.CostEstimate(
            flops=2 * steps * slots * width * half, bytes_accessed=6 * MIB, transcendentals=0
        ),
    )
    result = (own + others.astype(jnp.float32)).astype(jnp.bfloat16)
    return result.reshape(steps, slots, half)


def solution(mesh):
    placed = (
        P(None, ("groups", "inst"), "tp"),
        P(None, ("groups", "inst"), None),
        P(("groups", "inst"), None),
        P("groups", None),
        P("groups", None),
        P("tp", None),
    )
    return jax.shard_map(
        body,
        mesh=mesh,
        in_specs=placed,
        out_specs=P(None, ("groups", "inst"), "tp"),
        check_vma=False,
    )
```

```python
import functools
import math

import jax
import jax.numpy as jnp
from jax import lax
from jax.experimental import pallas as pl
from jax.experimental.pallas import tpu as pltpu
from jax.sharding import PartitionSpec as P

HDIM = 128
BLK = 128
MAXB = 2
WIN = MAXB * BLK
PAD = 8
MIB = 1024 * 1024


def partner(insts, ops, i, core):
    return jnp.int32(1) if i == ops - 1 else insts - 1 - 2 * i - core


def start_copies(pairs, sems):
    copies = [pltpu.make_async_copy(a, b, sems.at[n]) for n, (a, b) in enumerate(pairs)]
    for copy in copies:
        copy.start()
    return copies


def plan_kernel(
    ops, stride, anchor_h, lengths_h, queries_h, pool_h,
    table, pool, spread, own_q, sent_q, *refs,
):
    sends, (anchor, lengths, offs, queries, sems) = refs[:ops], refs[ops:]
    insts, slots = anchor.shape
    steps, _, width = queries.shape
    heads = width // HDIM
    rows = steps * heads
    blocks = pool.shape[0] // BLK
    own, core = lax.axis_index("inst"), lax.axis_index("tp")
    loads = start_copies(
        [(anchor_h, anchor), (lengths_h, lengths), (queries_h, queries), (pool_h, pool)], sems
    )
    loads[0].wait()
    loads[1].wait()
    for m in range(insts):
        table[0, m] = slots
        table[1, m] = 1
        offs[m] = 0
    start = jnp.int32(0)
    for j in range(slots):
        source = anchor[own, j]
        dest = (2 * own - source) & (insts - 1)
        table[0, own ^ source] = j
        table[1, own ^ source] = lengths[source, j]
        offs[own ^ dest] = start
        start = start + lengths[own, j]
    loads[2].wait()
    for s in range(steps):
        for h in range(heads):
            spread[pl.ds((s * heads + h) * stride, slots), :] = queries[
                s, :, h * HDIM : (h + 1) * HDIM
            ].astype(jnp.float32)
    for i in range(ops):
        j = table[0, partner(insts, ops, i, core)]
        own_q[i] = spread[pl.ds(j, rows, stride=stride), :].astype(jnp.bfloat16)
    for i in range(ops - 1):
        j = table[0, partner(insts, ops, i, 1 - core)]
        sent_q[i] = spread[pl.ds(j, rows, stride=stride), :].astype(jnp.bfloat16)
    loads[3].wait()
    for i in range(ops):
        at = offs[partner(insts, ops, i, core)]
        for b in range(MAXB):
            row = pl.multiple_of(jnp.minimum(at + b, blocks - 1) * BLK, BLK)
            sends[i][b * BLK : (b + 1) * BLK, :] = pool[pl.ds(row, BLK), :]


def contract_last(a, b):
    return lax.dot_general(a, b, (((1,), (1,)), ((), ())), preferred_element_type=jnp.float32)


def widest(score):
    return functools.reduce(
        jnp.maximum, [score[:, k : k + HDIM] for k in range(0, score.shape[1], HDIM)]
    )


def attend_all(scores, recents, values):
    scale = math.log2(math.e) / math.sqrt(HDIM)
    weights = []
    for score, recent in zip(scores, recents):
        top = jnp.max(jnp.maximum(widest(score), recent), axis=1, keepdims=True)
        cached = jnp.exp2((score - top) * scale)
        late = jnp.exp2((recent - top) * scale)
        folded = sum([cached[:, k : k + HDIM] for k in range(0, cached.shape[1], HDIM)], late)
        share = 1.0 / jnp.sum(folded, axis=1, keepdims=True)
        weights.append((cached.astype(jnp.bfloat16), late * share, share))
    return [
        (jnp.dot(cached, value, preferred_element_type=jnp.float32) * share, late)
        for (cached, late, share), value in zip(weights, values)
    ]


def stay_kernel(
    stride, steps, group, spread, pool, fresh_h, lengths_h, weight_h,
    attn, fresh, peer_w, own_w,
    lengths, order, starts, recent, late, sems,
):
    slots = lengths.shape[1]
    rows = spread.shape[0] // stride
    heads = rows // steps
    half = own_w.shape[1]
    own, core = lax.axis_index("inst"), lax.axis_index("tp")
    own_cols = pl.ds(pl.multiple_of(core * half, HDIM), half)
    peer_cols = pl.ds(pl.multiple_of((1 - core) * half, HDIM), half)
    loads = start_copies(
        [
            (lengths_h, lengths),
            (fresh_h, fresh),
            (weight_h.at[:, peer_cols], peer_w),
            (weight_h.at[:, own_cols], own_w),
        ],
        sems,
    )
    loads[0].wait()
    longer = pool.shape[0] // BLK - slots
    group = math.gcd(group, longer, slots - longer)
    start, found = jnp.int32(0), jnp.int32(0)
    for j in range(slots):
        count = lengths[own, j]
        place = jnp.where(count > 1, found, longer + j - found)
        order[place] = j
        starts[place] = start
        start = start + count
        found = found + count - 1
    loads[1].wait()
    slot = lax.broadcasted_iota(jnp.int32, (slots, steps * slots), 0)
    col = lax.broadcasted_iota(jnp.int32, (slots, steps * slots), 1)
    for i in range(rows):
        at = pl.ds(i * stride, slots)
        score = contract_last(spread[at, :].astype(jnp.bfloat16), fresh[:, :HDIM])
        mine = (col % slots == slot) & (col // slots <= i // heads)
        recent[at, :] = jnp.where(mine, score, -jnp.inf)

    def some(first, size, g, _):
        places = [first + g * group + u for u in range(group)]
        picked = [pl.ds(order[at], rows, stride=stride) for at in places]
        windows = [pl.ds(pl.multiple_of(starts[at] * BLK, BLK), size) for at in places]
        queries = [spread[at, :].astype(jnp.bfloat16) for at in picked]
        recents = [recent[at, :] for at in picked]
        scores = [contract_last(q, pool[w, :HDIM]) for q, w in zip(queries, windows)]
        done = attend_all(scores, recents, [pool[w, HDIM:] for w in windows])
        for at, (mixed, weight) in zip(picked, done):
            attn[at, :] = mixed
            late[at, :] = weight
        return 0

    lax.fori_loop(0, longer // group, functools.partial(some, 0, WIN), 0)
    lax.fori_loop(0, (slots - longer) // group, functools.partial(some, longer, BLK), 0)
    for i in range(rows):
        at = pl.ds(i * stride, slots)
        attn[at, :] = attn[at, :] + jnp.dot(
            late[at, :].astype(jnp.bfloat16), fresh[:, HDIM:], preferred_element_type=jnp.float32
        )
    loads[2].wait()
    loads[3].wait()


def move_kernel(ops, steps, slots, group, table, own_q, peer_q, fresh, *refs):
    blocks, (found, sent) = refs[:ops], refs[ops:]
    rows = own_q.shape[1]
    heads = rows // steps
    insts = table.shape[1]
    core = lax.axis_index("tp")
    shape = (2 * rows, steps * slots)
    step = lax.broadcasted_iota(jnp.int32, shape, 0) // heads % steps
    col = lax.broadcasted_iota(jnp.int32, shape, 1)
    owner = jnp.where(col // slots <= step, col % slots, -1)
    within = lax.broadcasted_iota(jnp.int32, (2 * rows, WIN), 1)
    for first in range(0, ops, group):
        batch = range(first, min(first + group, ops))
        queries, recents, scores = [], [], []
        for i in batch:
            query = own_q[i]
            if i < ops - 1:
                query = jnp.concatenate([query, peer_q[i]])
            queries.append(query)
        for i, query in zip(batch, queries):
            m = partner(insts, ops, i, core)
            score = contract_last(query, blocks[i][:, :HDIM])
            limit = table[1, m] * BLK
            scores.append(jnp.where(within[: query.shape[0]] < limit, score, -jnp.inf))
        for i, query in zip(batch, queries):
            recent = contract_last(query, fresh[:, :HDIM])
            j = table[0, partner(insts, ops, i, core)]
            recents.append(jnp.where(owner[: query.shape[0]] == j, recent, -jnp.inf))
        done = attend_all(scores, recents, [blocks[i][:, HDIM:] for i in batch])
        for i, (mixed, weight) in zip(batch, done):
            out = mixed + jnp.dot(
                weight.astype(jnp.bfloat16), fresh[:, HDIM:], preferred_element_type=jnp.float32
            )
            found[i] = out[:rows]
            if i < ops - 1:
                sent[i] = out[rows:].astype(jnp.bfloat16)


def project_kernel(ops, stride, chunks, table, attn, found, arrived, weight, partial, lhs, merged):
    rows = found.shape[1]
    insts = table.shape[1]
    slots = stride - PAD
    steps = lhs.shape[0] // slots
    heads = rows // steps
    core = lax.axis_index("tp")
    for i in range(ops):
        j = table[0, partner(insts, ops, i, core)]
        merged[pl.ds(j, rows, stride=stride), :] = found[i]
    for i in range(ops - 1):
        j = table[0, partner(insts, ops, i, 1 - core)]
        merged[pl.ds(j, rows, stride=stride), :] = arrived[i].astype(jnp.float32)
    for s in range(steps):
        for h in range(heads):
            lhs[s * slots : (s + 1) * slots, h * HDIM : (h + 1) * HDIM] = merged[
                pl.ds((s * heads + h) * stride, slots), :
            ].astype(jnp.bfloat16)
    tile = partial.shape[1] // chunks
    for n in range(chunks):
        cols = slice(n * tile, (n + 1) * tile)
        partial[:, cols] = jnp.dot(
            lhs[...], weight[:, cols], preferred_element_type=jnp.float32
        ).astype(jnp.bfloat16)


def own_kernel(chunks, lhs, weight, out):
    tile = out.shape[1] // chunks
    for n in range(chunks):
        cols = slice(n * tile, (n + 1) * tile)
        out[:, cols] = jnp.dot(lhs[...], weight[:, cols], preferred_element_type=jnp.float32)


def add_kernel(chunks, own, others, out_h, out, sems):
    part = out.shape[0] // chunks
    copies = []
    for n in range(chunks):
        at = pl.ds(n * part, part)
        out[at, :] = (own[at, :] + others[at, :].astype(jnp.float32)).astype(jnp.bfloat16)
        copies.append(pltpu.make_async_copy(out.at[at], out_h.at[at], sems.at[n]))
        copies[-1].start()
    for copy in copies:
        copy.wait()


def call(kernel, operands, outs, scratch=(), limit=8, cost=None, aliases=None):
    specs = [pl.BlockSpec(memory_space=space) for space, _ in operands]
    return pl.pallas_call(
        kernel,
        out_shape=[space(shape.shape, shape.dtype) for space, shape in outs],
        in_specs=specs,
        out_specs=[pl.BlockSpec(memory_space=space) for space, _ in outs],
        scratch_shapes=list(scratch),
        compiler_params=pltpu.CompilerParams(vmem_limit_bytes=limit * MIB),
        cost_estimate=cost,
        input_output_aliases=aliases or {},
    )(*[pltpu.with_memory_space_constraint(array, space) for space, array in operands])


def body(queries, new_kv, cache_pool, lengths, anchor, out_weight):
    steps, slots, width = queries.shape
    heads = width // HDIM
    rows = steps * heads
    insts = lax.axis_size("inst")
    cores = lax.axis_size("tp")
    kvw = cache_pool.shape[1]
    depth, columns = out_weight.shape
    half = columns // cores
    ops = insts // 2
    stride = slots + PAD
    hbm, vmem, smem = pltpu.HBM, pltpu.VMEM, pltpu.SMEM
    dma = pltpu.SemaphoreType.DMA

    def bf16(*shape):
        return jax.ShapeDtypeStruct(shape, jnp.bfloat16)

    def f32(*shape):
        return jax.ShapeDtypeStruct(shape, jnp.float32)

    table, pool, spread, own_q, sent_q, *sends = call(
        functools.partial(plan_kernel, ops, stride),
        [(hbm, anchor), (hbm, lengths), (hbm, queries), (hbm, cache_pool)],
        [
            (smem, jax.ShapeDtypeStruct((2, insts), jnp.int32)),
            (vmem, bf16(*cache_pool.shape)),
            (vmem, f32(rows * stride, HDIM)),
            (vmem, bf16(ops, rows, HDIM)),
            (vmem, bf16(ops - 1, rows, HDIM)),
        ]
        + [(vmem, bf16(WIN, kvw))] * ops,
        [
            smem(anchor.shape, jnp.int32),
            smem(lengths.shape, jnp.int32),
            smem((insts,), jnp.int32),
            vmem(queries.shape, jnp.bfloat16),
            dma((4,)),
        ],
    )
    blocks = [None] * ops
    for i in reversed(range(ops)):
        pairs = []
        for a in range(insts):
            for c in range(cores):
                m = 1 if i == ops - 1 else insts - 1 - 2 * i - c
                pairs.append((a * cores + c, (a ^ m) * cores + c))
        blocks[i] = lax.ppermute(sends[i], ("inst", "tp"), pairs)

    swap = [(c, cores - 1 - c) for c in range(cores)]
    peer_q = lax.ppermute(sent_q, "tp", swap)

    attn, fresh, peer_w, own_w = call(
        functools.partial(stay_kernel, stride, steps, 8),
        [
            (vmem, spread),
            (vmem, pool),
            (hbm, new_kv.reshape(steps * slots, kvw)),
            (hbm, lengths),
            (hbm, out_weight),
        ],
        [
            (vmem, f32(rows * stride, HDIM)),
            (vmem, bf16(steps * slots, kvw)),
            (vmem, bf16(depth, half)),
            (vmem, bf16(depth, half)),
        ],
        [
            smem(lengths.shape, jnp.int32),
            smem((slots,), jnp.int32),
            smem((slots,), jnp.int32),
            vmem((rows * stride, HDIM), jnp.float32),
            vmem((rows * stride, HDIM), jnp.float32),
            dma((4,)),
        ],
        limit=16,
        cost=pl.CostEstimate(
            flops=4 * slots * rows * WIN * HDIM, bytes_accessed=24 * MIB, transcendentals=0
        ),
    )

    found, sent = call(
        functools.partial(move_kernel, ops, steps, slots, 4),
        [(smem, table), (vmem, own_q), (vmem, peer_q), (vmem, fresh)]
        + [(vmem, block) for block in blocks],
        [(vmem, f32(ops, rows, HDIM)), (vmem, bf16(ops - 1, rows, HDIM))],
    )
    arrived = lax.ppermute(sent, "tp", swap)
    chunks = half // WIN
    partial, lhs, _ = call(
        functools.partial(project_kernel, ops, stride, chunks),
        [(smem, table), (vmem, attn), (vmem, found), (vmem, arrived), (vmem, peer_w)],
        [
            (vmem, bf16(steps * slots, half)),
            (vmem, bf16(steps * slots, width)),
            (vmem, f32(rows * stride, HDIM)),
        ],
        aliases={1: 2},
    )
    others = lax.ppermute(partial, "tp", swap)
    (own,) = call(
        functools.partial(own_kernel, chunks),
        [(vmem, lhs), (vmem, own_w)],
        [(vmem, f32(steps * slots, half))],
        cost=pl.CostEstimate(
            flops=2 * steps * slots * width * half, bytes_accessed=6 * MIB, transcendentals=0
        ),
    )
    (result,) = call(
        functools.partial(add_kernel, 4),
        [(vmem, own), (vmem, others)],
        [(hbm, bf16(steps * slots, half))],
        [vmem((steps * slots, half), jnp.bfloat16), dma((4,))],
    )
    return result.reshape(steps, slots, half)


def solution(mesh):
    placed = (
        P(None, ("groups", "inst"), "tp"),
        P(None, ("groups", "inst"), None),
        P(("groups", "inst"), None),
        P("groups", None),
        P("groups", None),
        P("tp", None),
    )
    return jax.shard_map(
        body,
        mesh=mesh,
        in_specs=placed,
        out_specs=P(None, ("groups", "inst"), "tp"),
        check_vma=False,
    )
```

```python
import functools
import math

import jax
import jax.numpy as jnp
from jax import lax
from jax.experimental import pallas as pl
from jax.experimental.pallas import tpu as pltpu
from jax.sharding import PartitionSpec as P

HDIM = 128
BLK = 128
MAXB = 2
WIN = MAXB * BLK
PAD = 8
MIB = 1024 * 1024


def partner(insts, ops, i, core):
    return jnp.int32(1) if i == ops - 1 else insts - 2 - 2 * i + core


def start_copies(pairs, sems):
    copies = [pltpu.make_async_copy(a, b, sems.at[n]) for n, (a, b) in enumerate(pairs)]
    for copy in copies:
        copy.start()
    return copies


def plan_kernel(
    ops, stride, anchor_h, lengths_h, queries_h, pool_h,
    table, pool, spread, own_q, sent_q, *refs,
):
    sends, (anchor, lengths, offs, queries, sems) = refs[:ops], refs[ops:]
    insts, slots = anchor.shape
    steps, _, width = queries.shape
    heads = width // HDIM
    rows = steps * heads
    blocks = pool.shape[0] // BLK
    own, core = lax.axis_index("inst"), lax.axis_index("tp")
    loads = start_copies(
        [(anchor_h, anchor), (lengths_h, lengths), (queries_h, queries), (pool_h, pool)], sems
    )
    loads[0].wait()
    loads[1].wait()
    for m in range(insts):
        table[0, m] = slots
        table[1, m] = 1
        offs[m] = 0
    start = jnp.int32(0)
    for j in range(slots):
        source = anchor[own, j]
        dest = (2 * own - source) & (insts - 1)
        table[0, own ^ source] = j
        table[1, own ^ source] = lengths[source, j]
        offs[own ^ dest] = start
        start = start + lengths[own, j]
    loads[2].wait()
    for s in range(steps):
        for h in range(heads):
            spread[pl.ds((s * heads + h) * stride, slots), :] = queries[
                s, :, h * HDIM : (h + 1) * HDIM
            ].astype(jnp.float32)
    for i in range(ops):
        j = table[0, partner(insts, ops, i, core)]
        own_q[i] = spread[pl.ds(j, rows, stride=stride), :].astype(jnp.bfloat16)
    for i in range(ops - 1):
        j = table[0, partner(insts, ops, i, 1 - core)]
        sent_q[i] = spread[pl.ds(j, rows, stride=stride), :].astype(jnp.bfloat16)
    loads[3].wait()
    for i in range(ops):
        at = offs[partner(insts, ops, i, core)]
        for b in range(MAXB):
            row = pl.multiple_of(jnp.minimum(at + b, blocks - 1) * BLK, BLK)
            sends[i][b * BLK : (b + 1) * BLK, :] = pool[pl.ds(row, BLK), :]


def contract_last(a, b):
    return lax.dot_general(a, b, (((1,), (1,)), ((), ())), preferred_element_type=jnp.float32)


def widest(score):
    return functools.reduce(
        jnp.maximum, [score[:, k : k + HDIM] for k in range(0, score.shape[1], HDIM)]
    )


def attend_all(scores, recents, values):
    scale = math.log2(math.e) / math.sqrt(HDIM)
    weights = []
    for score, recent in zip(scores, recents):
        top = jnp.max(jnp.maximum(widest(score), recent), axis=1, keepdims=True)
        cached = jnp.exp2((score - top) * scale)
        late = jnp.exp2((recent - top) * scale)
        folded = sum([cached[:, k : k + HDIM] for k in range(0, cached.shape[1], HDIM)], late)
        share = 1.0 / jnp.sum(folded, axis=1, keepdims=True)
        weights.append((cached.astype(jnp.bfloat16), late * share, share))
    return [
        (jnp.dot(cached, value, preferred_element_type=jnp.float32) * share, late)
        for (cached, late, share), value in zip(weights, values)
    ]


def stay_kernel(
    stride, steps, group, spread, pool, fresh_h, lengths_h, weight_h,
    attn, fresh, peer_w, own_w,
    lengths, order, starts, recent, late, sems,
):
    slots = lengths.shape[1]
    rows = spread.shape[0] // stride
    heads = rows // steps
    half = own_w.shape[1]
    own, core = lax.axis_index("inst"), lax.axis_index("tp")
    own_cols = pl.ds(pl.multiple_of(core * half, HDIM), half)
    peer_cols = pl.ds(pl.multiple_of((1 - core) * half, HDIM), half)
    loads = start_copies(
        [
            (lengths_h, lengths),
            (fresh_h, fresh),
            (weight_h.at[:, peer_cols], peer_w),
            (weight_h.at[:, own_cols], own_w),
        ],
        sems,
    )
    loads[0].wait()
    longer = pool.shape[0] // BLK - slots
    group = math.gcd(group, longer, slots - longer)
    start, found = jnp.int32(0), jnp.int32(0)
    for j in range(slots):
        count = lengths[own, j]
        place = jnp.where(count > 1, found, longer + j - found)
        order[place] = j
        starts[place] = start
        start = start + count
        found = found + count - 1
    loads[1].wait()
    slot = lax.broadcasted_iota(jnp.int32, (slots, steps * slots), 0)
    col = lax.broadcasted_iota(jnp.int32, (slots, steps * slots), 1)
    for i in range(rows):
        at = pl.ds(i * stride, slots)
        score = contract_last(spread[at, :].astype(jnp.bfloat16), fresh[:, :HDIM])
        mine = (col % slots == slot) & (col // slots <= i // heads)
        recent[at, :] = jnp.where(mine, score, -jnp.inf)

    def some(first, size, g, _):
        places = [first + g * group + u for u in range(group)]
        picked = [pl.ds(order[at], rows, stride=stride) for at in places]
        windows = [pl.ds(pl.multiple_of(starts[at] * BLK, BLK), size) for at in places]
        queries = [spread[at, :].astype(jnp.bfloat16) for at in picked]
        recents = [recent[at, :] for at in picked]
        scores = [contract_last(q, pool[w, :HDIM]) for q, w in zip(queries, windows)]
        done = attend_all(scores, recents, [pool[w, HDIM:] for w in windows])
        for at, (mixed, weight) in zip(picked, done):
            attn[at, :] = mixed
            late[at, :] = weight
        return 0

    lax.fori_loop(0, longer // group, functools.partial(some, 0, WIN), 0)
    lax.fori_loop(0, (slots - longer) // group, functools.partial(some, longer, BLK), 0)
    for i in range(rows):
        at = pl.ds(i * stride, slots)
        attn[at, :] = attn[at, :] + jnp.dot(
            late[at, :].astype(jnp.bfloat16), fresh[:, HDIM:], preferred_element_type=jnp.float32
        )
    loads[2].wait()
    loads[3].wait()


def move_kernel(ops, steps, slots, group, table, own_q, peer_q, fresh, *refs):
    blocks, (found, sent) = refs[:ops], refs[ops:]
    rows = own_q.shape[1]
    heads = rows // steps
    insts = table.shape[1]
    core = lax.axis_index("tp")
    shape = (2 * rows, steps * slots)
    step = lax.broadcasted_iota(jnp.int32, shape, 0) // heads % steps
    col = lax.broadcasted_iota(jnp.int32, shape, 1)
    owner = jnp.where(col // slots <= step, col % slots, -1)
    within = lax.broadcasted_iota(jnp.int32, (2 * rows, WIN), 1)
    for first in range(0, ops, group):
        batch = range(first, min(first + group, ops))
        queries, recents, scores = [], [], []
        for i in batch:
            query = own_q[i]
            if i < ops - 1:
                query = jnp.concatenate([query, peer_q[i]])
            queries.append(query)
        for i, query in zip(batch, queries):
            m = partner(insts, ops, i, core)
            score = contract_last(query, blocks[i][:, :HDIM])
            limit = table[1, m] * BLK
            scores.append(jnp.where(within[: query.shape[0]] < limit, score, -jnp.inf))
        for i, query in zip(batch, queries):
            recent = contract_last(query, fresh[:, :HDIM])
            j = table[0, partner(insts, ops, i, core)]
            recents.append(jnp.where(owner[: query.shape[0]] == j, recent, -jnp.inf))
        done = attend_all(scores, recents, [blocks[i][:, HDIM:] for i in batch])
        for i, (mixed, weight) in zip(batch, done):
            out = mixed + jnp.dot(
                weight.astype(jnp.bfloat16), fresh[:, HDIM:], preferred_element_type=jnp.float32
            )
            found[i] = out[:rows]
            if i < ops - 1:
                sent[i] = out[rows:].astype(jnp.bfloat16)


def project_kernel(ops, stride, chunks, table, attn, found, arrived, weight, partial, lhs, merged):
    rows = found.shape[1]
    insts = table.shape[1]
    slots = stride - PAD
    steps = lhs.shape[0] // slots
    heads = rows // steps
    core = lax.axis_index("tp")
    for i in range(ops):
        j = table[0, partner(insts, ops, i, core)]
        merged[pl.ds(j, rows, stride=stride), :] = found[i]
    for i in range(ops - 1):
        j = table[0, partner(insts, ops, i, 1 - core)]
        merged[pl.ds(j, rows, stride=stride), :] = arrived[i].astype(jnp.float32)
    for s in range(steps):
        for h in range(heads):
            lhs[s * slots : (s + 1) * slots, h * HDIM : (h + 1) * HDIM] = merged[
                pl.ds((s * heads + h) * stride, slots), :
            ].astype(jnp.bfloat16)
    tile = partial.shape[1] // chunks
    for n in range(chunks):
        cols = slice(n * tile, (n + 1) * tile)
        partial[:, cols] = jnp.dot(
            lhs[...], weight[:, cols], preferred_element_type=jnp.float32
        ).astype(jnp.bfloat16)


def own_kernel(chunks, lhs, weight, out):
    tile = out.shape[1] // chunks
    for n in range(chunks):
        cols = slice(n * tile, (n + 1) * tile)
        out[:, cols] = jnp.dot(lhs[...], weight[:, cols], preferred_element_type=jnp.float32)


def add_kernel(chunks, own, others, out_h, out, sems):
    part = out.shape[0] // chunks
    copies = []
    for n in range(chunks):
        at = pl.ds(n * part, part)
        out[at, :] = (own[at, :] + others[at, :].astype(jnp.float32)).astype(jnp.bfloat16)
        copies.append(pltpu.make_async_copy(out.at[at], out_h.at[at], sems.at[n]))
        copies[-1].start()
    for copy in copies:
        copy.wait()


def call(kernel, operands, outs, scratch=(), limit=8, cost=None, aliases=None):
    specs = [pl.BlockSpec(memory_space=space) for space, _ in operands]
    return pl.pallas_call(
        kernel,
        out_shape=[space(shape.shape, shape.dtype) for space, shape in outs],
        in_specs=specs,
        out_specs=[pl.BlockSpec(memory_space=space) for space, _ in outs],
        scratch_shapes=list(scratch),
        compiler_params=pltpu.CompilerParams(vmem_limit_bytes=limit * MIB),
        cost_estimate=cost,
        input_output_aliases=aliases or {},
    )(*[pltpu.with_memory_space_constraint(array, space) for space, array in operands])


def body(queries, new_kv, cache_pool, lengths, anchor, out_weight):
    steps, slots, width = queries.shape
    heads = width // HDIM
    rows = steps * heads
    insts = lax.axis_size("inst")
    cores = lax.axis_size("tp")
    kvw = cache_pool.shape[1]
    depth, columns = out_weight.shape
    half = columns // cores
    ops = insts // 2
    stride = slots + PAD
    hbm, vmem, smem = pltpu.HBM, pltpu.VMEM, pltpu.SMEM
    dma = pltpu.SemaphoreType.DMA

    def bf16(*shape):
        return jax.ShapeDtypeStruct(shape, jnp.bfloat16)

    def f32(*shape):
        return jax.ShapeDtypeStruct(shape, jnp.float32)

    table, pool, spread, own_q, sent_q, *sends = call(
        functools.partial(plan_kernel, ops, stride),
        [(hbm, anchor), (hbm, lengths), (hbm, queries), (hbm, cache_pool)],
        [
            (smem, jax.ShapeDtypeStruct((2, insts), jnp.int32)),
            (vmem, bf16(*cache_pool.shape)),
            (vmem, f32(rows * stride, HDIM)),
            (vmem, bf16(ops, rows, HDIM)),
            (vmem, bf16(ops - 1, rows, HDIM)),
        ]
        + [(vmem, bf16(WIN, kvw))] * ops,
        [
            smem(anchor.shape, jnp.int32),
            smem(lengths.shape, jnp.int32),
            smem((insts,), jnp.int32),
            vmem(queries.shape, jnp.bfloat16),
            dma((4,)),
        ],
    )
    blocks = [None] * ops
    for i in reversed(range(ops)):
        pairs = []
        for a in range(insts):
            for c in range(cores):
                m = 1 if i == ops - 1 else insts - 2 - 2 * i + c
                pairs.append((a * cores + c, (a ^ m) * cores + c))
        blocks[i] = lax.ppermute(sends[i], ("inst", "tp"), pairs)

    swap = [(c, cores - 1 - c) for c in range(cores)]
    peer_q = lax.ppermute(sent_q, "tp", swap)

    attn, fresh, peer_w, own_w = call(
        functools.partial(stay_kernel, stride, steps, 8),
        [
            (vmem, spread),
            (vmem, pool),
            (hbm, new_kv.reshape(steps * slots, kvw)),
            (hbm, lengths),
            (hbm, out_weight),
        ],
        [
            (vmem, f32(rows * stride, HDIM)),
            (vmem, bf16(steps * slots, kvw)),
            (vmem, bf16(depth, half)),
            (vmem, bf16(depth, half)),
        ],
        [
            smem(lengths.shape, jnp.int32),
            smem((slots,), jnp.int32),
            smem((slots,), jnp.int32),
            vmem((rows * stride, HDIM), jnp.float32),
            vmem((rows * stride, HDIM), jnp.float32),
            dma((4,)),
        ],
        limit=16,
        cost=pl.CostEstimate(
            flops=4 * slots * rows * WIN * HDIM, bytes_accessed=24 * MIB, transcendentals=0
        ),
    )

    found, sent = call(
        functools.partial(move_kernel, ops, steps, slots, 4),
        [(smem, table), (vmem, own_q), (vmem, peer_q), (vmem, fresh)]
        + [(vmem, block) for block in blocks],
        [(vmem, f32(ops, rows, HDIM)), (vmem, bf16(ops - 1, rows, HDIM))],
    )
    arrived = lax.ppermute(sent, "tp", swap)
    chunks = half // WIN
    partial, lhs, _ = call(
        functools.partial(project_kernel, ops, stride, chunks),
        [(smem, table), (vmem, attn), (vmem, found), (vmem, arrived), (vmem, peer_w)],
        [
            (vmem, bf16(steps * slots, half)),
            (vmem, bf16(steps * slots, width)),
            (vmem, f32(rows * stride, HDIM)),
        ],
        aliases={1: 2},
    )
    others = lax.ppermute(partial, "tp", swap)
    (own,) = call(
        functools.partial(own_kernel, chunks),
        [(vmem, lhs), (vmem, own_w)],
        [(vmem, f32(steps * slots, half))],
        cost=pl.CostEstimate(
            flops=2 * steps * slots * width * half, bytes_accessed=6 * MIB, transcendentals=0
        ),
    )
    (result,) = call(
        functools.partial(add_kernel, 4),
        [(vmem, own), (vmem, others)],
        [(hbm, bf16(steps * slots, half))],
        [vmem((steps * slots, half), jnp.bfloat16), dma((4,))],
    )
    return result.reshape(steps, slots, half)


def solution(mesh):
    placed = (
        P(None, ("groups", "inst"), "tp"),
        P(None, ("groups", "inst"), None),
        P(("groups", "inst"), None),
        P("groups", None),
        P("groups", None),
        P("tp", None),
    )
    return jax.shard_map(
        body,
        mesh=mesh,
        in_specs=placed,
        out_specs=P(None, ("groups", "inst"), "tp"),
        check_vma=False,
    )
```

```python
import functools
import math

import jax
import jax.numpy as jnp
from jax import lax
from jax.experimental import pallas as pl
from jax.experimental.pallas import tpu as pltpu
from jax.sharding import PartitionSpec as P

HDIM = 128
BLK = 128
MAXB = 2
WIN = MAXB * BLK
PAD = 8
FEW = 16
MIB = 1024 * 1024


def partner(insts, ops, i, core):
    return jnp.int32(1) if i == ops - 1 else insts - 2 - 2 * i + core


def start_copies(pairs, sems):
    copies = [pltpu.make_async_copy(a, b, sems.at[n]) for n, (a, b) in enumerate(pairs)]
    for copy in copies:
        copy.start()
    return copies


def plan_kernel(
    ops, asked, stride, anchor_h, lengths_h, queries_h, fresh_h, pool_h,
    table, lists, pool, spread, fresh, own_q, sent_q, asked_f, *refs,
):
    sends, (anchor, lengths, offs, queries, keys, values, few, sems) = refs[:ops], refs[ops:]
    insts, slots = anchor.shape
    steps, _, width = queries.shape
    heads = width // HDIM
    rows = steps * heads
    blocks = pool.shape[0] // BLK
    own, core = lax.axis_index("inst"), lax.axis_index("tp")
    loads = start_copies(
        [
            (anchor_h, anchor),
            (lengths_h, lengths),
            (queries_h, queries),
            (fresh_h, fresh),
            (pool_h, pool),
        ],
        sems,
    )
    loads[0].wait()
    loads[1].wait()
    for m in range(insts):
        table[0, m] = slots
        table[1, m] = 1
        table[2, m] = 1
        offs[m] = 0
    longer = blocks - slots
    start, found = jnp.int32(0), jnp.int32(0)
    for j in range(slots):
        source, count = anchor[own, j], lengths[own, j]
        dest = (2 * own - source) & (insts - 1)
        table[0, own ^ source] = j
        table[1, own ^ source] = lengths[source, j]
        table[2, own ^ dest] = count
        offs[own ^ dest] = start
        place = jnp.where(count > 1, found, longer + j - found)
        lists[0, place] = j
        lists[1, place] = start
        start = start + count
        found = found + count - 1
    loads[2].wait()
    for s in range(steps):
        for h in range(heads):
            spread[pl.ds((s * heads + h) * stride, slots), :] = queries[
                s, :, h * HDIM : (h + 1) * HDIM
            ].astype(jnp.float32)
    for i in range(ops):
        j = table[0, partner(insts, ops, i, core)]
        own_q[i] = spread[pl.ds(j, rows, stride=stride), :].astype(jnp.bfloat16)
    for i in range(ops - 1):
        j = table[0, partner(insts, ops, i, 1 - core)]
        sent_q[i] = spread[pl.ds(j, rows, stride=stride), :].astype(jnp.bfloat16)
    loads[3].wait()
    keys[0 : steps * slots, :] = fresh[:, :HDIM].astype(jnp.float32)
    values[0 : steps * slots, :] = fresh[:, HDIM:].astype(jnp.float32)
    few[...] = jnp.zeros_like(few)
    for n, i in enumerate(asked):
        j = table[0, partner(insts, ops, i, core)]
        for u in range(steps):
            few[u : u + 1, :] = keys[pl.ds(u * slots + j, 1), :]
            few[FEW + u : FEW + u + 1, :] = values[pl.ds(u * slots + j, 1), :]
        asked_f[n] = few[...].astype(jnp.bfloat16)
    loads[4].wait()
    for i in range(ops):
        at = offs[partner(insts, ops, i, core)]
        for b in range(MAXB):
            row = pl.multiple_of(jnp.minimum(at + b, blocks - 1) * BLK, BLK)
            sends[i][b * BLK : (b + 1) * BLK, :] = pool[pl.ds(row, BLK), :]


def ask_kernel(asked, own_q, peer_q, asked_f, *outs):
    rows = own_q.shape[1]
    for n, i in enumerate(asked):
        outs[n][0:rows, :] = own_q[i]
        outs[n][rows : 2 * rows, :] = peer_q[i]
        outs[n][2 * rows :, :] = asked_f[n]


def answer_kernel(ops, asked, steps, after, table, *refs):
    count = len(asked)
    questions, windows, outs = refs[:count], refs[count : 2 * count], refs[2 * count :]
    rows = outs[0].shape[0]
    heads = rows // 2 // steps
    insts = table.shape[1]
    core = lax.axis_index("tp")
    step = lax.broadcasted_iota(jnp.int32, (rows, HDIM), 0) // heads % steps
    col = lax.broadcasted_iota(jnp.int32, (rows, HDIM), 1)
    within = lax.broadcasted_iota(jnp.int32, (rows, WIN), 1)
    empty = jnp.zeros((HDIM - FEW, HDIM), jnp.bfloat16)
    scores, recents, lates = [], [], []
    for n, i in enumerate(asked):
        limit = table[2, partner(insts, ops, i, core)] * BLK
        query = questions[n][0:rows, :]
        score = contract_last(query, windows[n][:, :HDIM])
        scores.append(jnp.where(within < limit, score, -jnp.inf))
        keys = jnp.concatenate([questions[n][rows : rows + FEW, :], empty])
        lates.append(jnp.concatenate([questions[n][rows + FEW :, :], empty]))
        recents.append(jnp.where(col <= step, contract_last(query, keys), -jnp.inf))
    done = attend_all(scores, recents, [window[:, HDIM:] for window in windows])
    for n, (mixed, weight) in enumerate(done):
        out = mixed + jnp.dot(
            weight.astype(jnp.bfloat16), lates[n], preferred_element_type=jnp.float32
        )
        outs[n][...] = out.astype(jnp.bfloat16)


def contract_last(a, b):
    return lax.dot_general(a, b, (((1,), (1,)), ((), ())), preferred_element_type=jnp.float32)


def widest(score):
    return functools.reduce(
        jnp.maximum, [score[:, k : k + HDIM] for k in range(0, score.shape[1], HDIM)]
    )


def attend_all(scores, recents, values):
    scale = math.log2(math.e) / math.sqrt(HDIM)
    weights = []
    for score, recent in zip(scores, recents):
        top = jnp.max(jnp.maximum(widest(score), recent), axis=1, keepdims=True)
        cached = jnp.exp2((score - top) * scale)
        late = jnp.exp2((recent - top) * scale)
        folded = sum([cached[:, k : k + HDIM] for k in range(0, cached.shape[1], HDIM)], late)
        share = 1.0 / jnp.sum(folded, axis=1, keepdims=True)
        weights.append((cached.astype(jnp.bfloat16), late * share, share))
    return [
        (jnp.dot(cached, value, preferred_element_type=jnp.float32) * share, late)
        for (cached, late, share), value in zip(weights, values)
    ]


def stay_requests(stride, rows, group, first, count, size, lists, spread, pool, recent, attn, late):
    group = math.gcd(group, count)

    def some(g, _):
        places = [first + g * group + u for u in range(group)]
        picked = [pl.ds(lists[0, at], rows, stride=stride) for at in places]
        windows = [pl.ds(pl.multiple_of(lists[1, at] * BLK, BLK), size) for at in places]
        queries = [spread[at, :].astype(jnp.bfloat16) for at in picked]
        recents = [recent[at, :] for at in picked]
        scores = [contract_last(q, pool[w, :HDIM]) for q, w in zip(queries, windows)]
        done = attend_all(scores, recents, [pool[w, HDIM:] for w in windows])
        for at, (mixed, weight) in zip(picked, done):
            attn[at, :] = mixed
            late[at, :] = weight
        return 0

    lax.fori_loop(0, count // group, some, 0)


def long_kernel(
    stride, steps, group, after, lists, spread, pool, fresh, weight_h,
    attn, late, recent, peer_w, sems,
):
    slots = lists.shape[1]
    rows = spread.shape[0] // stride
    heads = rows // steps
    half = peer_w.shape[1]
    peer = (1 - lax.axis_index("tp")) * half
    load = start_copies([(weight_h.at[:, pl.ds(pl.multiple_of(peer, HDIM), half)], peer_w)], sems)
    slot = lax.broadcasted_iota(jnp.int32, (slots, steps * slots), 0)
    col = lax.broadcasted_iota(jnp.int32, (slots, steps * slots), 1)
    for i in range(rows):
        at = pl.ds(i * stride, slots)
        score = contract_last(spread[at, :].astype(jnp.bfloat16), fresh[:, :HDIM])
        mine = (col % slots == slot) & (col // slots <= i // heads)
        recent[at, :] = jnp.where(mine, score, -jnp.inf)
    longer = pool.shape[0] // BLK - slots
    stay_requests(stride, rows, group, 0, longer, WIN, lists, spread, pool, recent, attn, late)
    load[0].wait()


def short_kernel(
    stride, group, after, lists, spread, pool, fresh, weight_h, recent, attn_in, late_in,
    attn, late, own_w, sems,
):
    slots = lists.shape[1]
    rows = spread.shape[0] // stride
    half = own_w.shape[1]
    own = lax.axis_index("tp") * half
    load = start_copies([(weight_h.at[:, pl.ds(pl.multiple_of(own, HDIM), half)], own_w)], sems)
    longer = pool.shape[0] // BLK - slots
    stay_requests(
        stride, rows, group, longer, slots - longer, BLK, lists, spread, pool, recent, attn, late
    )
    for i in range(rows):
        at = pl.ds(i * stride, slots)
        attn[at, :] = attn[at, :] + jnp.dot(
            late[at, :].astype(jnp.bfloat16), fresh[:, HDIM:], preferred_element_type=jnp.float32
        )
    load[0].wait()


def move_kernel(ops, asked, steps, slots, group, after, table, own_q, peer_q, fresh, *refs):
    blocks, (found, sent) = refs[:ops], refs[ops:]
    rows = own_q.shape[1]
    heads = rows // steps
    insts = table.shape[1]
    core = lax.axis_index("tp")
    shape = (2 * rows, steps * slots)
    step = lax.broadcasted_iota(jnp.int32, shape, 0) // heads % steps
    col = lax.broadcasted_iota(jnp.int32, shape, 1)
    owner = jnp.where(col // slots <= step, col % slots, -1)
    within = lax.broadcasted_iota(jnp.int32, (2 * rows, WIN), 1)
    for i in asked:
        found[i] = blocks[i][0:rows, :].astype(jnp.float32)
        sent[i] = blocks[i][rows : 2 * rows, :]
    moved = [i for i in range(ops) if i not in asked]
    for first in range(0, len(moved), group):
        batch = moved[first : first + group]
        queries, recents, scores = [], [], []
        for i in batch:
            query = own_q[i]
            if i < ops - 1:
                query = jnp.concatenate([query, peer_q[i]])
            queries.append(query)
        for i, query in zip(batch, queries):
            m = partner(insts, ops, i, core)
            score = contract_last(query, blocks[i][:, :HDIM])
            limit = table[1, m] * BLK
            scores.append(jnp.where(within[: query.shape[0]] < limit, score, -jnp.inf))
        for i, query in zip(batch, queries):
            recent = contract_last(query, fresh[:, :HDIM])
            j = table[0, partner(insts, ops, i, core)]
            recents.append(jnp.where(owner[: query.shape[0]] == j, recent, -jnp.inf))
        done = attend_all(scores, recents, [blocks[i][:, HDIM:] for i in batch])
        for i, (mixed, weight) in zip(batch, done):
            out = mixed + jnp.dot(
                weight.astype(jnp.bfloat16), fresh[:, HDIM:], preferred_element_type=jnp.float32
            )
            found[i] = out[:rows]
            if i < ops - 1:
                sent[i] = out[rows:].astype(jnp.bfloat16)


def project_kernel(ops, stride, chunks, table, attn, found, arrived, weight, partial, lhs, merged):
    rows = found.shape[1]
    insts = table.shape[1]
    slots = stride - PAD
    steps = lhs.shape[0] // slots
    heads = rows // steps
    core = lax.axis_index("tp")
    for i in range(ops):
        j = table[0, partner(insts, ops, i, core)]
        merged[pl.ds(j, rows, stride=stride), :] = found[i]
    for i in range(ops - 1):
        j = table[0, partner(insts, ops, i, 1 - core)]
        merged[pl.ds(j, rows, stride=stride), :] = arrived[i].astype(jnp.float32)
    for s in range(steps):
        for h in range(heads):
            lhs[s * slots : (s + 1) * slots, h * HDIM : (h + 1) * HDIM] = merged[
                pl.ds((s * heads + h) * stride, slots), :
            ].astype(jnp.bfloat16)
    tile = partial.shape[1] // chunks
    for n in range(chunks):
        cols = slice(n * tile, (n + 1) * tile)
        partial[:, cols] = jnp.dot(
            lhs[...], weight[:, cols], preferred_element_type=jnp.float32
        ).astype(jnp.bfloat16)


def own_kernel(chunks, lhs, weight, out):
    tile = out.shape[1] // chunks
    for n in range(chunks):
        cols = slice(n * tile, (n + 1) * tile)
        out[:, cols] = jnp.dot(lhs[...], weight[:, cols], preferred_element_type=jnp.float32)


def add_kernel(chunks, own, others, out_h, out, sems):
    part = out.shape[0] // chunks
    copies = []
    for n in range(chunks):
        at = pl.ds(n * part, part)
        out[at, :] = (own[at, :] + others[at, :].astype(jnp.float32)).astype(jnp.bfloat16)
        copies.append(pltpu.make_async_copy(out.at[at], out_h.at[at], sems.at[n]))
        copies[-1].start()
    for copy in copies:
        copy.wait()


def call(kernel, operands, outs, scratch=(), limit=8, cost=None, aliases=None):
    specs = [pl.BlockSpec(memory_space=space) for space, _ in operands]
    return pl.pallas_call(
        kernel,
        out_shape=[space(shape.shape, shape.dtype) for space, shape in outs],
        in_specs=specs,
        out_specs=[pl.BlockSpec(memory_space=space) for space, _ in outs],
        scratch_shapes=list(scratch),
        compiler_params=pltpu.CompilerParams(vmem_limit_bytes=limit * MIB),
        cost_estimate=cost,
        input_output_aliases=aliases or {},
    )(*[pltpu.with_memory_space_constraint(array, space) for space, array in operands])


def body(queries, new_kv, cache_pool, lengths, anchor, out_weight):
    steps, slots, width = queries.shape
    heads = width // HDIM
    rows = steps * heads
    insts = lax.axis_size("inst")
    cores = lax.axis_size("tp")
    kvw = cache_pool.shape[1]
    depth, columns = out_weight.shape
    half = columns // cores
    ops = insts // 2
    stride = slots + PAD
    hbm, vmem, smem = pltpu.HBM, pltpu.VMEM, pltpu.SMEM
    dma = pltpu.SemaphoreType.DMA

    def bf16(*shape):
        return jax.ShapeDtypeStruct(shape, jnp.bfloat16)

    def f32(*shape):
        return jax.ShapeDtypeStruct(shape, jnp.float32)

    asked = (1,)
    table, lists, pool, spread, fresh, own_q, sent_q, asked_f, *sends = call(
        functools.partial(plan_kernel, ops, asked, stride),
        [
            (hbm, anchor),
            (hbm, lengths),
            (hbm, queries),
            (hbm, new_kv.reshape(steps * slots, kvw)),
            (hbm, cache_pool),
        ],
        [
            (smem, jax.ShapeDtypeStruct((3, insts), jnp.int32)),
            (smem, jax.ShapeDtypeStruct((2, slots), jnp.int32)),
            (vmem, bf16(*cache_pool.shape)),
            (vmem, f32(rows * stride, HDIM)),
            (vmem, bf16(steps * slots, kvw)),
            (vmem, bf16(ops, rows, HDIM)),
            (vmem, bf16(ops - 1, rows, HDIM)),
            (vmem, bf16(len(asked), 2 * FEW, HDIM)),
        ]
        + [(vmem, bf16(WIN, kvw))] * ops,
        [
            smem(anchor.shape, jnp.int32),
            smem(lengths.shape, jnp.int32),
            smem((insts,), jnp.int32),
            vmem(queries.shape, jnp.bfloat16),
            vmem((steps * slots + PAD, HDIM), jnp.float32),
            vmem((steps * slots + PAD, HDIM), jnp.float32),
            vmem((2 * FEW, HDIM), jnp.float32),
            dma((5,)),
        ],
    )
    swap = [(c, cores - 1 - c) for c in range(cores)]
    peer_q = lax.ppermute(sent_q, "tp", swap)

    def exchange(i, array):
        pairs = []
        for a in range(insts):
            for c in range(cores):
                m = 1 if i == ops - 1 else insts - 2 - 2 * i + c
                pairs.append((a * cores + c, (a ^ m) * cores + c))
        return lax.ppermute(array, ("inst", "tp"), pairs)

    blocks = [None] * ops
    for i in reversed(range(ops)):
        if i not in asked:
            blocks[i] = exchange(i, sends[i])
    questions = call(
        functools.partial(ask_kernel, asked),
        [(vmem, own_q), (vmem, peer_q), (vmem, asked_f)],
        [(vmem, bf16(2 * rows + 2 * FEW, HDIM))] * len(asked),
    )
    asking = [exchange(i, question) for i, question in zip(asked, questions)]
    half_cost = pl.CostEstimate(
        flops=2 * slots * rows * WIN * HDIM, bytes_accessed=10 * MIB, transcendentals=0
    )
    attn, late, recent, peer_w = call(
        functools.partial(long_kernel, stride, steps, 8),
        [
            (vmem, questions[0]),
            (smem, lists),
            (vmem, spread),
            (vmem, pool),
            (vmem, fresh),
            (hbm, out_weight),
        ],
        [(vmem, f32(rows * stride, HDIM))] * 3 + [(vmem, bf16(depth, half))],
        [dma((1,))],
        cost=half_cost,
    )
    answers = call(
        functools.partial(answer_kernel, ops, asked, steps),
        [(vmem, attn), (smem, table)]
        + [(vmem, question) for question in asking]
        + [(vmem, sends[i]) for i in asked],
        [(vmem, bf16(2 * rows, HDIM))] * len(asked),
    )
    for i, answer in zip(asked, answers):
        blocks[i] = exchange(i, answer)
    attn, late, own_w = call(
        functools.partial(short_kernel, stride, 8),
        [
            (vmem, answers[0]),
            (smem, lists),
            (vmem, spread),
            (vmem, pool),
            (vmem, fresh),
            (hbm, out_weight),
            (vmem, recent),
            (vmem, attn),
            (vmem, late),
        ],
        [(vmem, f32(rows * stride, HDIM))] * 2 + [(vmem, bf16(depth, half))],
        [dma((1,))],
        cost=half_cost,
        aliases={7: 0, 8: 1},
    )

    found, sent = call(
        functools.partial(move_kernel, ops, asked, steps, slots, 4),
        [(vmem, own_w), (smem, table), (vmem, own_q), (vmem, peer_q), (vmem, fresh)]
        + [(vmem, block) for block in blocks],
        [(vmem, f32(ops, rows, HDIM)), (vmem, bf16(ops - 1, rows, HDIM))],
    )
    arrived = lax.ppermute(sent, "tp", swap)
    chunks = half // WIN
    partial, lhs, _ = call(
        functools.partial(project_kernel, ops, stride, chunks),
        [(smem, table), (vmem, attn), (vmem, found), (vmem, arrived), (vmem, peer_w)],
        [
            (vmem, bf16(steps * slots, half)),
            (vmem, bf16(steps * slots, width)),
            (vmem, f32(rows * stride, HDIM)),
        ],
        aliases={1: 2},
    )
    others = lax.ppermute(partial, "tp", swap)
    (own,) = call(
        functools.partial(own_kernel, chunks),
        [(vmem, lhs), (vmem, own_w)],
        [(vmem, f32(steps * slots, half))],
        cost=pl.CostEstimate(
            flops=2 * steps * slots * width * half, bytes_accessed=6 * MIB, transcendentals=0
        ),
    )
    (result,) = call(
        functools.partial(add_kernel, 4),
        [(vmem, own), (vmem, others)],
        [(hbm, bf16(steps * slots, half))],
        [vmem((steps * slots, half), jnp.bfloat16), dma((4,))],
    )
    return result.reshape(steps, slots, half)


def solution(mesh):
    placed = (
        P(None, ("groups", "inst"), "tp"),
        P(None, ("groups", "inst"), None),
        P(("groups", "inst"), None),
        P("groups", None),
        P("groups", None),
        P("tp", None),
    )
    return jax.shard_map(
        body,
        mesh=mesh,
        in_specs=placed,
        out_specs=P(None, ("groups", "inst"), "tp"),
        check_vma=False,
    )
```

```python
import functools
import math

import jax
import jax.numpy as jnp
from jax import lax
from jax.experimental import pallas as pl
from jax.experimental.pallas import tpu as pltpu
from jax.sharding import PartitionSpec as P

HDIM = 128
BLK = 128
MAXB = 2
WIN = MAXB * BLK
PAD = 8
MIB = 1024 * 1024


def partner(insts, ops, i, core):
    return jnp.int32(1) if i == ops - 1 else insts - 2 - 2 * i + core


def start_copies(pairs, sems):
    copies = [pltpu.make_async_copy(a, b, sems.at[n]) for n, (a, b) in enumerate(pairs)]
    for copy in copies:
        copy.start()
    return copies


def plan_kernel(
    ops, stride, anchor_h, lengths_h, queries_h, fresh_h, pool_h,
    table, lists, pool, spread, fresh, own_q, sent_q, *refs,
):
    sends, (anchor, lengths, offs, queries, sems) = refs[:ops], refs[ops:]
    insts, slots = anchor.shape
    steps, _, width = queries.shape
    heads = width // HDIM
    rows = steps * heads
    blocks = pool.shape[0] // BLK
    own, core = lax.axis_index("inst"), lax.axis_index("tp")
    loads = start_copies(
        [
            (anchor_h, anchor),
            (lengths_h, lengths),
            (queries_h, queries),
            (fresh_h, fresh),
            (pool_h, pool),
        ],
        sems,
    )
    loads[0].wait()
    loads[1].wait()
    for m in range(insts):
        table[0, m] = slots
        table[1, m] = 1
        offs[m] = 0
    longer = blocks - slots
    start, found = jnp.int32(0), jnp.int32(0)
    for j in range(slots):
        source, count = anchor[own, j], lengths[own, j]
        dest = (2 * own - source) & (insts - 1)
        table[0, own ^ source] = j
        table[1, own ^ source] = lengths[source, j]
        offs[own ^ dest] = start
        place = jnp.where(count > 1, found, longer + j - found)
        lists[0, place] = j
        lists[1, place] = start
        start = start + count
        found = found + count - 1
    loads[2].wait()
    for s in range(steps):
        for h in range(heads):
            spread[pl.ds((s * heads + h) * stride, slots), :] = queries[
                s, :, h * HDIM : (h + 1) * HDIM
            ].astype(jnp.float32)
    for i in range(ops):
        j = table[0, partner(insts, ops, i, core)]
        own_q[i] = spread[pl.ds(j, rows, stride=stride), :].astype(jnp.bfloat16)
    for i in range(ops - 1):
        j = table[0, partner(insts, ops, i, 1 - core)]
        sent_q[i] = spread[pl.ds(j, rows, stride=stride), :].astype(jnp.bfloat16)
    loads[3].wait()
    loads[4].wait()
    for i in range(ops):
        at = offs[partner(insts, ops, i, core)]
        for b in range(MAXB):
            row = pl.multiple_of(jnp.minimum(at + b, blocks - 1) * BLK, BLK)
            sends[i][b * BLK : (b + 1) * BLK, :] = pool[pl.ds(row, BLK), :]


def contract_last(a, b):
    return lax.dot_general(a, b, (((1,), (1,)), ((), ())), preferred_element_type=jnp.float32)


def widest(score):
    return functools.reduce(
        jnp.maximum, [score[:, k : k + HDIM] for k in range(0, score.shape[1], HDIM)]
    )


def attend_all(scores, recents, values):
    scale = math.log2(math.e) / math.sqrt(HDIM)
    weights = []
    for score, recent in zip(scores, recents):
        top = jnp.max(jnp.maximum(widest(score), recent), axis=1, keepdims=True)
        cached = jnp.exp2((score - top) * scale)
        late = jnp.exp2((recent - top) * scale)
        folded = sum([cached[:, k : k + HDIM] for k in range(0, cached.shape[1], HDIM)], late)
        share = 1.0 / jnp.sum(folded, axis=1, keepdims=True)
        weights.append((cached.astype(jnp.bfloat16), late * share, share))
    return [
        (jnp.dot(cached, value, preferred_element_type=jnp.float32) * share, late)
        for (cached, late, share), value in zip(weights, values)
    ]


def stay_requests(stride, rows, group, first, count, size, lists, spread, pool, recent, attn, late):
    group = math.gcd(group, count)

    def some(g, _):
        places = [first + g * group + u for u in range(group)]
        picked = [pl.ds(lists[0, at], rows, stride=stride) for at in places]
        windows = [pl.ds(pl.multiple_of(lists[1, at] * BLK, BLK), size) for at in places]
        queries = [spread[at, :].astype(jnp.bfloat16) for at in picked]
        recents = [recent[at, :] for at in picked]
        scores = [contract_last(q, pool[w, :HDIM]) for q, w in zip(queries, windows)]
        done = attend_all(scores, recents, [pool[w, HDIM:] for w in windows])
        for at, (mixed, weight) in zip(picked, done):
            attn[at, :] = mixed
            late[at, :] = weight
        return 0

    lax.fori_loop(0, count // group, some, 0)


def stay_kernel(
    stride, steps, group, lists, spread, pool, fresh, weight_h,
    attn, peer_w, own_w, recent, late, sems,
):
    slots = lists.shape[1]
    rows = spread.shape[0] // stride
    heads = rows // steps
    half = peer_w.shape[1]
    core = lax.axis_index("tp")
    own_cols = pl.ds(pl.multiple_of(core * half, HDIM), half)
    peer_cols = pl.ds(pl.multiple_of((1 - core) * half, HDIM), half)
    loads = start_copies(
        [(weight_h.at[:, peer_cols], peer_w), (weight_h.at[:, own_cols], own_w)], sems
    )
    slot = lax.broadcasted_iota(jnp.int32, (slots, steps * slots), 0)
    col = lax.broadcasted_iota(jnp.int32, (slots, steps * slots), 1)
    for i in range(rows):
        at = pl.ds(i * stride, slots)
        score = contract_last(spread[at, :].astype(jnp.bfloat16), fresh[:, :HDIM])
        mine = (col % slots == slot) & (col // slots <= i // heads)
        recent[at, :] = jnp.where(mine, score, -jnp.inf)
    longer = pool.shape[0] // BLK - slots
    state = (lists, spread, pool, recent, attn, late)
    stay_requests(stride, rows, group, 0, longer, WIN, *state)
    stay_requests(stride, rows, group, longer, slots - longer, BLK, *state)
    for i in range(rows):
        at = pl.ds(i * stride, slots)
        attn[at, :] = attn[at, :] + jnp.dot(
            late[at, :].astype(jnp.bfloat16), fresh[:, HDIM:], preferred_element_type=jnp.float32
        )
    for load in loads:
        load.wait()


def move_kernel(ops, steps, slots, through, table, own_q, peer_q, fresh, *refs):
    blocks, (found, sent, _) = refs[:ops], refs[ops:]
    rows = own_q.shape[1]
    heads = rows // steps
    insts = table.shape[1]
    core = lax.axis_index("tp")
    shape = (2 * rows, steps * slots)
    step = lax.broadcasted_iota(jnp.int32, shape, 0) // heads % steps
    col = lax.broadcasted_iota(jnp.int32, shape, 1)
    owner = jnp.where(col // slots <= step, col % slots, -1)
    within = lax.broadcasted_iota(jnp.int32, (2 * rows, WIN), 1)
    for first in range(0, ops, 4):
        batch = range(first, min(first + 4, ops))
        scores, recents = [], []
        for i in batch:
            query = own_q[i]
            if i < ops - 1:
                query = jnp.concatenate([query, peer_q[i]])
            m = partner(insts, ops, i, core)
            score = contract_last(query, blocks[i][:, :HDIM])
            fits = within[: query.shape[0]] < table[1, m] * BLK
            scores.append(jnp.where(fits, score, -jnp.inf))
            recent = contract_last(query, fresh[:, :HDIM])
            recents.append(jnp.where(owner[: query.shape[0]] == table[0, m], recent, -jnp.inf))
        done = attend_all(scores, recents, [blocks[i][:, HDIM:] for i in batch])
        for i, (mixed, weight) in zip(batch, done):
            out = mixed + jnp.dot(
                weight.astype(jnp.bfloat16), fresh[:, HDIM:], preferred_element_type=jnp.float32
            )
            found[i] = out[:rows].astype(jnp.bfloat16)
            if i < ops - 1:
                sent[i] = out[rows:].astype(jnp.bfloat16)


def dot_tiles(lhs, weight, out):
    tile = math.gcd(WIN, out.shape[1])
    for n in range(0, out.shape[1], tile):
        out[:, n : n + tile] = jnp.dot(
            lhs[...], weight[:, n : n + tile], preferred_element_type=jnp.float32
        ).astype(out.dtype)


def base_kernel(ops, stride, table, attn, peer_w, own_w, partial, own, spot, lhs):
    insts = table.shape[1]
    slots = stride - PAD
    steps = lhs.shape[0] // slots
    rows = attn.shape[0] // stride
    heads = rows // steps
    width = spot.shape[1]
    slot = lax.broadcasted_iota(jnp.int32, (slots, HDIM), 0)
    stays = slot >= 0
    row = lax.broadcasted_iota(jnp.int32, spot.shape, 0)
    col = lax.broadcasted_iota(jnp.int32, spot.shape, 1)
    goes = row < 0
    for n in range(2 * ops - 1):
        m = table_place(insts, ops, n)
        j = table[0, m]
        stays = stays & (slot != j)
        goes = goes | ((col % (2 * ops) == n) & (row % slots == j))
    goes = goes & (col // (2 * ops) == row // slots)
    spot[...] = jnp.where(goes, 1.0, 0.0).astype(jnp.bfloat16)
    for s in range(steps):
        for h in range(heads):
            value = attn[pl.ds((s * heads + h) * stride, slots), :]
            lhs[s * slots : (s + 1) * slots, h * HDIM : (h + 1) * HDIM] = jnp.where(
                stays, value, 0.0
            ).astype(jnp.bfloat16)
    dot_tiles(lhs, peer_w, partial)
    dot_tiles(lhs, own_w, own)


def table_place(insts, ops, n):
    return 1 if n // 2 == ops - 1 else insts - 2 - 2 * (n // 2) + n % 2


def project_kernel(ops, steps, weight, found, arrived, partial, lhs, spread):
    rows = found.shape[1]
    heads = rows // steps
    stride = 2 * ops
    core = lax.axis_index("tp")
    spread[pl.ds(stride - 1, rows, stride=stride), :] = jnp.zeros((rows, HDIM), jnp.float32)
    for i in range(ops):
        at = stride - 2 if i == ops - 1 else 2 * i + core
        spread[pl.ds(at, rows, stride=stride), :] = found[i].astype(jnp.float32)
    for i in range(ops - 1):
        at = 2 * i + 1 - core
        spread[pl.ds(at, rows, stride=stride), :] = arrived[i].astype(jnp.float32)
    for s in range(0, steps, 2):
        for h in range(heads):
            both = [
                spread[pl.ds(((s + t) * heads + h) * stride, stride), :] for t in range(2)
            ]
            lhs[s * stride : (s + 2) * stride, h * HDIM : (h + 1) * HDIM] = jnp.concatenate(
                both
            ).astype(jnp.bfloat16)
    dot_tiles(lhs, weight, partial)


def own_kernel(lhs, weight, out):
    dot_tiles(lhs, weight, out)


def final_kernel(chunks, spot, own, others, own_m, others_m, out_h, out, sems):
    moved = (own_m[...] + others_m[...].astype(jnp.float32)).astype(jnp.bfloat16)
    part = out.shape[0] // chunks
    copies = []
    for n in range(chunks):
        at = pl.ds(n * part, part)
        placed = jnp.dot(spot[at, :], moved, preferred_element_type=jnp.float32)
        out[at, :] = (own[at, :] + others[at, :].astype(jnp.float32) + placed).astype(jnp.bfloat16)
        copies.append(pltpu.make_async_copy(out.at[at], out_h.at[at], sems.at[n]))
        copies[-1].start()
    for copy in copies:
        copy.wait()


def call(kernel, operands, outs, scratch=(), limit=8, cost=None, aliases=None):
    specs = [pl.BlockSpec(memory_space=space) for space, _ in operands]
    return pl.pallas_call(
        kernel,
        out_shape=[space(shape.shape, shape.dtype) for space, shape in outs],
        in_specs=specs,
        out_specs=[pl.BlockSpec(memory_space=space) for space, _ in outs],
        scratch_shapes=list(scratch),
        compiler_params=pltpu.CompilerParams(vmem_limit_bytes=limit * MIB),
        cost_estimate=cost,
        input_output_aliases=aliases or {},
    )(*[pltpu.with_memory_space_constraint(array, space) for space, array in operands])


def body(queries, new_kv, cache_pool, lengths, anchor, out_weight):
    steps, slots, width = queries.shape
    heads = width // HDIM
    rows = steps * heads
    insts = lax.axis_size("inst")
    cores = lax.axis_size("tp")
    kvw = cache_pool.shape[1]
    depth, columns = out_weight.shape
    half = columns // cores
    ops = insts // 2
    stride = slots + PAD
    hbm, vmem, smem = pltpu.HBM, pltpu.VMEM, pltpu.SMEM
    dma = pltpu.SemaphoreType.DMA

    def bf16(*shape):
        return jax.ShapeDtypeStruct(shape, jnp.bfloat16)

    def f32(*shape):
        return jax.ShapeDtypeStruct(shape, jnp.float32)

    table, lists, pool, spread, fresh, own_q, sent_q, *sends = call(
        functools.partial(plan_kernel, ops, stride),
        [
            (hbm, anchor),
            (hbm, lengths),
            (hbm, queries),
            (hbm, new_kv.reshape(steps * slots, kvw)),
            (hbm, cache_pool),
        ],
        [
            (smem, jax.ShapeDtypeStruct((2, insts), jnp.int32)),
            (smem, jax.ShapeDtypeStruct((2, slots), jnp.int32)),
            (vmem, bf16(*cache_pool.shape)),
            (vmem, f32(rows * stride, HDIM)),
            (vmem, bf16(steps * slots, kvw)),
            (vmem, bf16(ops, rows, HDIM)),
            (vmem, bf16(ops - 1, rows, HDIM)),
        ]
        + [(vmem, bf16(WIN, kvw))] * ops,
        [
            smem(anchor.shape, jnp.int32),
            smem(lengths.shape, jnp.int32),
            smem((insts,), jnp.int32),
            vmem(queries.shape, jnp.bfloat16),
            dma((5,)),
        ],
    )
    swap = [(c, cores - 1 - c) for c in range(cores)]
    peer_q = lax.ppermute(sent_q, "tp", swap)

    blocks = [None] * ops
    for i in reversed(range(ops)):
        pairs = []
        for a in range(insts):
            for c in range(cores):
                pairs.append((a * cores + c, (a ^ table_place(insts, ops, 2 * i + c)) * cores + c))
        blocks[i] = lax.ppermute(sends[i], ("inst", "tp"), pairs)

    attn, peer_w, own_w = call(
        functools.partial(stay_kernel, stride, steps, 8),
        [
            (smem, lists),
            (vmem, spread),
            (vmem, pool),
            (vmem, fresh),
            (hbm, out_weight),
        ],
        [(vmem, f32(rows * stride, HDIM))] + [(vmem, bf16(depth, half))] * 2,
        [
            vmem((rows * stride, HDIM), jnp.float32),
            vmem((rows * stride, HDIM), jnp.float32),
            dma((2,)),
        ],
        cost=pl.CostEstimate(
            flops=4 * slots * rows * WIN * HDIM, bytes_accessed=20 * MIB, transcendentals=0
        ),
    )
    tokens = steps * slots
    partial, own, spot = call(
        functools.partial(base_kernel, ops, stride),
        [(smem, table), (vmem, attn), (vmem, peer_w), (vmem, own_w)],
        [(vmem, bf16(tokens, half)), (vmem, f32(tokens, half)), (vmem, bf16(tokens, 2 * ops * steps))],
        [vmem((tokens, width), jnp.bfloat16)],
        cost=pl.CostEstimate(
            flops=4 * tokens * width * half, bytes_accessed=10 * MIB, transcendentals=0
        ),
    )

    found, sent, partial = call(
        functools.partial(move_kernel, ops, steps, slots),
        [(vmem, partial), (smem, table), (vmem, own_q), (vmem, peer_q), (vmem, fresh)]
        + [(vmem, block) for block in blocks],
        [
            (vmem, bf16(ops, rows, HDIM)),
            (vmem, bf16(ops - 1, rows, HDIM)),
            (vmem, bf16(tokens, half)),
        ],
        aliases={0: 2},
    )
    others = lax.ppermute(partial, "tp", swap)
    arrived = lax.ppermute(sent, "tp", swap)
    moved = 2 * ops * steps
    partial_m, lhs_m = call(
        functools.partial(project_kernel, ops, steps),
        [(vmem, peer_w), (vmem, found), (vmem, arrived)],
        [(vmem, bf16(moved, half)), (vmem, bf16(moved, width))],
        [vmem((2 * ops * rows, HDIM), jnp.float32)],
    )
    others_m = lax.ppermute(partial_m, "tp", swap)
    (own_m,) = call(
        own_kernel,
        [(vmem, lhs_m), (vmem, own_w)],
        [(vmem, f32(moved, half))],
        cost=pl.CostEstimate(
            flops=2 * moved * width * half, bytes_accessed=6 * MIB, transcendentals=0
        ),
    )
    (result,) = call(
        functools.partial(final_kernel, 4),
        [(vmem, spot), (vmem, own), (vmem, others), (vmem, own_m), (vmem, others_m)],
        [(hbm, bf16(tokens, half))],
        [vmem((tokens, half), jnp.bfloat16), dma((4,))],
    )
    return result.reshape(steps, slots, half)


def solution(mesh):
    placed = (
        P(None, ("groups", "inst"), "tp"),
        P(None, ("groups", "inst"), None),
        P(("groups", "inst"), None),
        P("groups", None),
        P("groups", None),
        P("tp", None),
    )
    return jax.shard_map(
        body,
        mesh=mesh,
        in_specs=placed,
        out_specs=P(None, ("groups", "inst"), "tp"),
        check_vma=False,
    )
```

```python
import functools
import math

import jax
import jax.numpy as jnp
from jax import lax
from jax.experimental import pallas as pl
from jax.experimental.pallas import tpu as pltpu
from jax.sharding import PartitionSpec as P

HDIM = 128
BLK = 128
MAXB = 2
WIN = MAXB * BLK
PAD = 8
FEW = 16
MIB = 1024 * 1024


def partner(insts, ops, i, core):
    return jnp.int32(1) if i == ops - 1 else insts - 2 - 2 * i + core


def start_copies(pairs, sems):
    copies = [pltpu.make_async_copy(a, b, sems.at[n]) for n, (a, b) in enumerate(pairs)]
    for copy in copies:
        copy.start()
    return copies


def plan_kernel(
    ops, asked, stride, anchor_h, lengths_h, queries_h, fresh_h, pool_h,
    table, lists, pool, spread, fresh, own_q, sent_q, asked_f, *refs,
):
    sends, (anchor, lengths, offs, queries, keys, values, few, sems) = refs[:ops], refs[ops:]
    insts, slots = anchor.shape
    steps, _, width = queries.shape
    heads = width // HDIM
    rows = steps * heads
    blocks = pool.shape[0] // BLK
    own, core = lax.axis_index("inst"), lax.axis_index("tp")
    loads = start_copies(
        [
            (anchor_h, anchor),
            (lengths_h, lengths),
            (queries_h, queries),
            (fresh_h, fresh),
            (pool_h, pool),
        ],
        sems,
    )
    loads[0].wait()
    loads[1].wait()
    for m in range(insts):
        table[0, m] = slots
        table[1, m] = 1
        table[2, m] = 1
        offs[m] = 0
    longer = blocks - slots
    start, found = jnp.int32(0), jnp.int32(0)
    for j in range(slots):
        source, count = anchor[own, j], lengths[own, j]
        dest = (2 * own - source) & (insts - 1)
        table[0, own ^ source] = j
        table[1, own ^ source] = lengths[source, j]
        table[2, own ^ dest] = count
        offs[own ^ dest] = start
        place = jnp.where(count > 1, found, longer + j - found)
        lists[0, place] = j
        lists[1, place] = start
        start = start + count
        found = found + count - 1
    loads[2].wait()
    for s in range(steps):
        for h in range(heads):
            spread[pl.ds((s * heads + h) * stride, slots), :] = queries[
                s, :, h * HDIM : (h + 1) * HDIM
            ].astype(jnp.float32)
    for i in range(ops):
        j = table[0, partner(insts, ops, i, core)]
        own_q[i] = spread[pl.ds(j, rows, stride=stride), :].astype(jnp.bfloat16)
    for i in range(ops - 1):
        j = table[0, partner(insts, ops, i, 1 - core)]
        sent_q[i] = spread[pl.ds(j, rows, stride=stride), :].astype(jnp.bfloat16)
    loads[3].wait()
    keys[0 : steps * slots, :] = fresh[:, :HDIM].astype(jnp.float32)
    values[0 : steps * slots, :] = fresh[:, HDIM:].astype(jnp.float32)
    few[...] = jnp.zeros_like(few)
    for n, i in enumerate(asked):
        j = table[0, partner(insts, ops, i, core)]
        for u in range(steps):
            few[u : u + 1, :] = keys[pl.ds(u * slots + j, 1), :]
            few[FEW + u : FEW + u + 1, :] = values[pl.ds(u * slots + j, 1), :]
        asked_f[n] = few[...].astype(jnp.bfloat16)
    loads[4].wait()
    for i in range(ops):
        at = offs[partner(insts, ops, i, core)]
        for b in range(MAXB):
            row = pl.multiple_of(jnp.minimum(at + b, blocks - 1) * BLK, BLK)
            sends[i][b * BLK : (b + 1) * BLK, :] = pool[pl.ds(row, BLK), :]


def ask_kernel(asked, own_q, peer_q, asked_f, *refs):
    outs = refs[-len(asked) :]
    rows = own_q.shape[1]
    for n, i in enumerate(asked):
        outs[n][0:rows, :] = own_q[i]
        outs[n][rows : 2 * rows, :] = peer_q[i]
        outs[n][2 * rows :, :] = asked_f[n]


def answer_kernel(ops, asked, steps, table, *refs):
    count = len(asked)
    questions, windows, outs = refs[:count], refs[count : 2 * count], refs[2 * count :]
    rows = outs[0].shape[0]
    heads = rows // 2 // steps
    insts = table.shape[1]
    core = lax.axis_index("tp")
    step = lax.broadcasted_iota(jnp.int32, (rows, HDIM), 0) // heads % steps
    col = lax.broadcasted_iota(jnp.int32, (rows, HDIM), 1)
    within = lax.broadcasted_iota(jnp.int32, (rows, WIN), 1)
    empty = jnp.zeros((HDIM - FEW, HDIM), jnp.bfloat16)
    scores, recents, lates = [], [], []
    for n, i in enumerate(asked):
        limit = table[2, partner(insts, ops, i, core)] * BLK
        query = questions[n][0:rows, :]
        score = contract_last(query, windows[n][:, :HDIM])
        scores.append(jnp.where(within < limit, score, -jnp.inf))
        keys = jnp.concatenate([questions[n][rows : rows + FEW, :], empty])
        lates.append(jnp.concatenate([questions[n][rows + FEW :, :], empty]))
        recents.append(jnp.where(col <= step, contract_last(query, keys), -jnp.inf))
    done = attend_all(scores, recents, [window[:, HDIM:] for window in windows])
    for n, (mixed, weight) in enumerate(done):
        out = mixed + jnp.dot(
            weight.astype(jnp.bfloat16), lates[n], preferred_element_type=jnp.float32
        )
        outs[n][...] = out.astype(jnp.bfloat16)


def contract_last(a, b):
    return lax.dot_general(a, b, (((1,), (1,)), ((), ())), preferred_element_type=jnp.float32)


def widest(score):
    return functools.reduce(
        jnp.maximum, [score[:, k : k + HDIM] for k in range(0, score.shape[1], HDIM)]
    )


def attend_all(scores, recents, values):
    scale = math.log2(math.e) / math.sqrt(HDIM)
    weights = []
    for score, recent in zip(scores, recents):
        top = jnp.max(jnp.maximum(widest(score), recent), axis=1, keepdims=True)
        cached = jnp.exp2((score - top) * scale)
        late = jnp.exp2((recent - top) * scale)
        folded = sum([cached[:, k : k + HDIM] for k in range(0, cached.shape[1], HDIM)], late)
        share = 1.0 / jnp.sum(folded, axis=1, keepdims=True)
        weights.append((cached.astype(jnp.bfloat16), late * share, share))
    return [
        (jnp.dot(cached, value, preferred_element_type=jnp.float32) * share, late)
        for (cached, late, share), value in zip(weights, values)
    ]


def stay_requests(stride, rows, group, first, count, size, lists, spread, pool, recent, attn, late):
    group = math.gcd(group, count)

    def some(g, _):
        places = [first + g * group + u for u in range(group)]
        picked = [pl.ds(lists[0, at], rows, stride=stride) for at in places]
        windows = [pl.ds(pl.multiple_of(lists[1, at] * BLK, BLK), size) for at in places]
        queries = [spread[at, :].astype(jnp.bfloat16) for at in picked]
        recents = [recent[at, :] for at in picked]
        scores = [contract_last(q, pool[w, :HDIM]) for q, w in zip(queries, windows)]
        done = attend_all(scores, recents, [pool[w, HDIM:] for w in windows])
        for at, (mixed, weight) in zip(picked, done):
            attn[at, :] = mixed
            late[at, :] = weight
        return 0

    lax.fori_loop(0, count // group, some, 0)


def stay_kernel(
    stride, steps, group, after, lists, spread, pool, fresh, weight_h,
    attn, peer_w, own_w, recent, late, sems,
):
    slots = lists.shape[1]
    rows = spread.shape[0] // stride
    heads = rows // steps
    half = peer_w.shape[1]
    core = lax.axis_index("tp")
    own_cols = pl.ds(pl.multiple_of(core * half, HDIM), half)
    peer_cols = pl.ds(pl.multiple_of((1 - core) * half, HDIM), half)
    loads = start_copies(
        [(weight_h.at[:, peer_cols], peer_w), (weight_h.at[:, own_cols], own_w)], sems
    )
    slot = lax.broadcasted_iota(jnp.int32, (slots, steps * slots), 0)
    col = lax.broadcasted_iota(jnp.int32, (slots, steps * slots), 1)
    for i in range(rows):
        at = pl.ds(i * stride, slots)
        score = contract_last(spread[at, :].astype(jnp.bfloat16), fresh[:, :HDIM])
        mine = (col % slots == slot) & (col // slots <= i // heads)
        recent[at, :] = jnp.where(mine, score, -jnp.inf)
    longer = pool.shape[0] // BLK - slots
    state = (lists, spread, pool, recent, attn, late)
    stay_requests(stride, rows, group, 0, longer, WIN, *state)
    stay_requests(stride, rows, group, longer, slots - longer, BLK, *state)
    for i in range(rows):
        at = pl.ds(i * stride, slots)
        attn[at, :] = attn[at, :] + jnp.dot(
            late[at, :].astype(jnp.bfloat16), fresh[:, HDIM:], preferred_element_type=jnp.float32
        )
    for load in loads:
        load.wait()


def move_kernel(ops, asked, steps, slots, group, after, table, own_q, peer_q, fresh, *refs):
    blocks, (found, sent) = refs[:ops], refs[ops:]
    rows = own_q.shape[1]
    heads = rows // steps
    insts = table.shape[1]
    core = lax.axis_index("tp")
    shape = (2 * rows, steps * slots)
    step = lax.broadcasted_iota(jnp.int32, shape, 0) // heads % steps
    col = lax.broadcasted_iota(jnp.int32, shape, 1)
    owner = jnp.where(col // slots <= step, col % slots, -1)
    within = lax.broadcasted_iota(jnp.int32, (2 * rows, WIN), 1)
    for i in asked:
        found[i] = blocks[i][0:rows, :].astype(jnp.float32)
        sent[i] = blocks[i][rows : 2 * rows, :]
    moved = [i for i in range(ops) if i not in asked]
    for first in range(0, len(moved), group):
        batch = moved[first : first + group]
        queries, recents, scores = [], [], []
        for i in batch:
            query = own_q[i]
            if i < ops - 1:
                query = jnp.concatenate([query, peer_q[i]])
            queries.append(query)
        for i, query in zip(batch, queries):
            m = partner(insts, ops, i, core)
            score = contract_last(query, blocks[i][:, :HDIM])
            limit = table[1, m] * BLK
            scores.append(jnp.where(within[: query.shape[0]] < limit, score, -jnp.inf))
        for i, query in zip(batch, queries):
            recent = contract_last(query, fresh[:, :HDIM])
            j = table[0, partner(insts, ops, i, core)]
            recents.append(jnp.where(owner[: query.shape[0]] == j, recent, -jnp.inf))
        done = attend_all(scores, recents, [blocks[i][:, HDIM:] for i in batch])
        for i, (mixed, weight) in zip(batch, done):
            out = mixed + jnp.dot(
                weight.astype(jnp.bfloat16), fresh[:, HDIM:], preferred_element_type=jnp.float32
            )
            found[i] = out[:rows]
            if i < ops - 1:
                sent[i] = out[rows:].astype(jnp.bfloat16)


def project_kernel(ops, stride, chunks, table, attn, found, arrived, weight, partial, lhs, merged):
    rows = found.shape[1]
    insts = table.shape[1]
    slots = stride - PAD
    steps = lhs.shape[0] // slots
    heads = rows // steps
    core = lax.axis_index("tp")
    for i in range(ops):
        j = table[0, partner(insts, ops, i, core)]
        merged[pl.ds(j, rows, stride=stride), :] = found[i]
    for i in range(ops - 1):
        j = table[0, partner(insts, ops, i, 1 - core)]
        merged[pl.ds(j, rows, stride=stride), :] = arrived[i].astype(jnp.float32)
    for s in range(steps):
        for h in range(heads):
            lhs[s * slots : (s + 1) * slots, h * HDIM : (h + 1) * HDIM] = merged[
                pl.ds((s * heads + h) * stride, slots), :
            ].astype(jnp.bfloat16)
    tile = partial.shape[1] // chunks
    for n in range(chunks):
        cols = slice(n * tile, (n + 1) * tile)
        partial[:, cols] = jnp.dot(
            lhs[...], weight[:, cols], preferred_element_type=jnp.float32
        ).astype(jnp.bfloat16)


def own_kernel(chunks, lhs, weight, out):
    tile = out.shape[1] // chunks
    for n in range(chunks):
        cols = slice(n * tile, (n + 1) * tile)
        out[:, cols] = jnp.dot(lhs[...], weight[:, cols], preferred_element_type=jnp.float32)


def add_kernel(chunks, own, others, out_h, out, sems):
    part = out.shape[0] // chunks
    copies = []
    for n in range(chunks):
        at = pl.ds(n * part, part)
        out[at, :] = (own[at, :] + others[at, :].astype(jnp.float32)).astype(jnp.bfloat16)
        copies.append(pltpu.make_async_copy(out.at[at], out_h.at[at], sems.at[n]))
        copies[-1].start()
    for copy in copies:
        copy.wait()


def call(kernel, operands, outs, scratch=(), limit=8, cost=None, aliases=None):
    specs = [pl.BlockSpec(memory_space=space) for space, _ in operands]
    return pl.pallas_call(
        kernel,
        out_shape=[space(shape.shape, shape.dtype) for space, shape in outs],
        in_specs=specs,
        out_specs=[pl.BlockSpec(memory_space=space) for space, _ in outs],
        scratch_shapes=list(scratch),
        compiler_params=pltpu.CompilerParams(vmem_limit_bytes=limit * MIB),
        cost_estimate=cost,
        input_output_aliases=aliases or {},
    )(*[pltpu.with_memory_space_constraint(array, space) for space, array in operands])


def body(queries, new_kv, cache_pool, lengths, anchor, out_weight):
    steps, slots, width = queries.shape
    heads = width // HDIM
    rows = steps * heads
    insts = lax.axis_size("inst")
    cores = lax.axis_size("tp")
    kvw = cache_pool.shape[1]
    depth, columns = out_weight.shape
    half = columns // cores
    ops = insts // 2
    stride = slots + PAD
    hbm, vmem, smem = pltpu.HBM, pltpu.VMEM, pltpu.SMEM
    dma = pltpu.SemaphoreType.DMA

    def bf16(*shape):
        return jax.ShapeDtypeStruct(shape, jnp.bfloat16)

    def f32(*shape):
        return jax.ShapeDtypeStruct(shape, jnp.float32)

    asked = (1,)
    table, lists, pool, spread, fresh, own_q, sent_q, asked_f, *sends = call(
        functools.partial(plan_kernel, ops, asked, stride),
        [
            (hbm, anchor),
            (hbm, lengths),
            (hbm, queries),
            (hbm, new_kv.reshape(steps * slots, kvw)),
            (hbm, cache_pool),
        ],
        [
            (smem, jax.ShapeDtypeStruct((3, insts), jnp.int32)),
            (smem, jax.ShapeDtypeStruct((2, slots), jnp.int32)),
            (vmem, bf16(*cache_pool.shape)),
            (vmem, f32(rows * stride, HDIM)),
            (vmem, bf16(steps * slots, kvw)),
            (vmem, bf16(ops, rows, HDIM)),
            (vmem, bf16(ops - 1, rows, HDIM)),
            (vmem, bf16(len(asked), 2 * FEW, HDIM)),
        ]
        + [(vmem, bf16(WIN, kvw))] * ops,
        [
            smem(anchor.shape, jnp.int32),
            smem(lengths.shape, jnp.int32),
            smem((insts,), jnp.int32),
            vmem(queries.shape, jnp.bfloat16),
            vmem((steps * slots + PAD, HDIM), jnp.float32),
            vmem((steps * slots + PAD, HDIM), jnp.float32),
            vmem((2 * FEW, HDIM), jnp.float32),
            dma((5,)),
        ],
    )
    swap = [(c, cores - 1 - c) for c in range(cores)]
    peer_q = lax.ppermute(sent_q, "tp", swap)

    def exchange(i, array):
        pairs = []
        for a in range(insts):
            for c in range(cores):
                m = 1 if i == ops - 1 else insts - 2 - 2 * i + c
                pairs.append((a * cores + c, (a ^ m) * cores + c))
        return lax.ppermute(array, ("inst", "tp"), pairs)

    kept = [i for i in range(ops) if i not in asked]
    handed = call(
        functools.partial(ask_kernel, asked),
        [(vmem, own_q), (vmem, peer_q), (vmem, asked_f)] + [(vmem, sends[i]) for i in kept],
        [(vmem, bf16(WIN, kvw))] * len(kept)
        + [(vmem, bf16(2 * rows + 2 * FEW, HDIM))] * len(asked),
        aliases={3 + n: n for n in range(len(kept))},
    )
    blocks = [None] * ops
    for i, block in reversed(list(zip(kept, handed))):
        blocks[i] = exchange(i, block)
    asking = [exchange(i, question) for i, question in zip(asked, handed[len(kept) :])]
    answers = call(
        functools.partial(answer_kernel, ops, asked, steps),
        [(smem, table)]
        + [(vmem, question) for question in asking]
        + [(vmem, sends[i]) for i in asked],
        [(vmem, bf16(2 * rows, HDIM))] * len(asked),
    )
    for i, answer in zip(asked, answers):
        blocks[i] = exchange(i, answer)
    attn, peer_w, own_w = call(
        functools.partial(stay_kernel, stride, steps, 8),
        [
            (vmem, answers[0]),
            (smem, lists),
            (vmem, spread),
            (vmem, pool),
            (vmem, fresh),
            (hbm, out_weight),
        ],
        [(vmem, f32(rows * stride, HDIM))] + [(vmem, bf16(depth, half))] * 2,
        [
            vmem((rows * stride, HDIM), jnp.float32),
            vmem((rows * stride, HDIM), jnp.float32),
            dma((2,)),
        ],
        cost=pl.CostEstimate(
            flops=200 * slots * rows * WIN * HDIM, bytes_accessed=20 * MIB, transcendentals=0
        ),
    )

    found, sent = call(
        functools.partial(move_kernel, ops, asked, steps, slots, 4),
        [(vmem, own_w), (smem, table), (vmem, own_q), (vmem, peer_q), (vmem, fresh)]
        + [(vmem, block) for block in blocks],
        [(vmem, f32(ops, rows, HDIM)), (vmem, bf16(ops - 1, rows, HDIM))],
    )
    arrived = lax.ppermute(sent, "tp", swap)
    chunks = half // WIN
    partial, lhs, _ = call(
        functools.partial(project_kernel, ops, stride, chunks),
        [(smem, table), (vmem, attn), (vmem, found), (vmem, arrived), (vmem, peer_w)],
        [
            (vmem, bf16(steps * slots, half)),
            (vmem, bf16(steps * slots, width)),
            (vmem, f32(rows * stride, HDIM)),
        ],
        aliases={1: 2},
    )
    others = lax.ppermute(partial, "tp", swap)
    (own,) = call(
        functools.partial(own_kernel, chunks),
        [(vmem, lhs), (vmem, own_w)],
        [(vmem, f32(steps * slots, half))],
        cost=pl.CostEstimate(
            flops=2 * steps * slots * width * half, bytes_accessed=6 * MIB, transcendentals=0
        ),
    )
    (result,) = call(
        functools.partial(add_kernel, 4),
        [(vmem, own), (vmem, others)],
        [(hbm, bf16(steps * slots, half))],
        [vmem((steps * slots, half), jnp.bfloat16), dma((4,))],
    )
    return result.reshape(steps, slots, half)


def solution(mesh):
    placed = (
        P(None, ("groups", "inst"), "tp"),
        P(None, ("groups", "inst"), None),
        P(("groups", "inst"), None),
        P("groups", None),
        P("groups", None),
        P("tp", None),
    )
    return jax.shard_map(
        body,
        mesh=mesh,
        in_specs=placed,
        out_specs=P(None, ("groups", "inst"), "tp"),
        check_vma=False,
    )
```

```python
import functools
import math

import jax
import jax.numpy as jnp
from jax import lax
from jax.experimental import pallas as pl
from jax.experimental.pallas import tpu as pltpu
from jax.sharding import PartitionSpec as P

HDIM = 128
BLK = 128
MAXB = 2
WIN = MAXB * BLK
PAD = 8
FEW = 16
MIB = 1024 * 1024


def partner(insts, ops, i, core):
    return jnp.int32(1) if i == ops - 1 else insts - 2 - 2 * i + core


def start_copies(pairs, sems):
    copies = [pltpu.make_async_copy(a, b, sems.at[n]) for n, (a, b) in enumerate(pairs)]
    for copy in copies:
        copy.start()
    return copies


def plan_kernel(
    ops, asked, stride, anchor_h, lengths_h, queries_h, fresh_h, pool_h,
    table, lists, pool, spread, fresh, own_q, sent_q, asked_f, *refs,
):
    sends, (anchor, lengths, offs, queries, keys, values, few, sems) = refs[:ops], refs[ops:]
    insts, slots = anchor.shape
    steps, _, width = queries.shape
    heads = width // HDIM
    rows = steps * heads
    blocks = pool.shape[0] // BLK
    own, core = lax.axis_index("inst"), lax.axis_index("tp")
    loads = start_copies(
        [
            (anchor_h, anchor),
            (lengths_h, lengths),
            (queries_h, queries),
            (fresh_h, fresh),
            (pool_h, pool),
        ],
        sems,
    )
    loads[0].wait()
    loads[1].wait()
    for m in range(insts):
        table[0, m] = slots
        table[1, m] = 1
        table[2, m] = 1
        offs[m] = 0
    longer = blocks - slots
    start, found = jnp.int32(0), jnp.int32(0)
    for j in range(slots):
        source, count = anchor[own, j], lengths[own, j]
        dest = (2 * own - source) & (insts - 1)
        table[0, own ^ source] = j
        table[1, own ^ source] = lengths[source, j]
        table[2, own ^ dest] = count
        offs[own ^ dest] = start
        place = jnp.where(count > 1, found, longer + j - found)
        lists[0, place] = j
        lists[1, place] = start
        start = start + count
        found = found + count - 1
    loads[2].wait()
    for s in range(steps):
        for h in range(heads):
            spread[pl.ds((s * heads + h) * stride, slots), :] = queries[
                s, :, h * HDIM : (h + 1) * HDIM
            ].astype(jnp.float32)
    for i in range(ops):
        j = table[0, partner(insts, ops, i, core)]
        own_q[i] = spread[pl.ds(j, rows, stride=stride), :].astype(jnp.bfloat16)
    for i in range(ops - 1):
        j = table[0, partner(insts, ops, i, 1 - core)]
        sent_q[i] = spread[pl.ds(j, rows, stride=stride), :].astype(jnp.bfloat16)
    loads[3].wait()
    keys[0 : steps * slots, :] = fresh[:, :HDIM].astype(jnp.float32)
    values[0 : steps * slots, :] = fresh[:, HDIM:].astype(jnp.float32)
    few[...] = jnp.zeros_like(few)
    for n, i in enumerate(asked):
        j = table[0, partner(insts, ops, i, core)]
        for u in range(steps):
            few[u : u + 1, :] = keys[pl.ds(u * slots + j, 1), :]
            few[FEW + u : FEW + u + 1, :] = values[pl.ds(u * slots + j, 1), :]
        asked_f[n] = few[...].astype(jnp.bfloat16)
    loads[4].wait()
    for i in range(ops):
        at = offs[partner(insts, ops, i, core)]
        for b in range(MAXB):
            row = pl.multiple_of(jnp.minimum(at + b, blocks - 1) * BLK, BLK)
            sends[i][b * BLK : (b + 1) * BLK, :] = pool[pl.ds(row, BLK), :]


def ask_kernel(asked, own_q, peer_q, asked_f, *refs):
    outs = refs[-len(asked) :]
    rows = own_q.shape[1]
    for n, i in enumerate(asked):
        outs[n][0:rows, :] = own_q[i]
        outs[n][rows : 2 * rows, :] = peer_q[i]
        outs[n][2 * rows :, :] = asked_f[n]


def answer_kernel(ops, asked, steps, after, table, *refs):
    count = len(asked)
    questions, windows, outs = refs[:count], refs[count : 2 * count], refs[2 * count :]
    rows = outs[0].shape[0]
    heads = rows // 2 // steps
    insts = table.shape[1]
    core = lax.axis_index("tp")
    step = lax.broadcasted_iota(jnp.int32, (rows, HDIM), 0) // heads % steps
    col = lax.broadcasted_iota(jnp.int32, (rows, HDIM), 1)
    within = lax.broadcasted_iota(jnp.int32, (rows, WIN), 1)
    empty = jnp.zeros((HDIM - FEW, HDIM), jnp.bfloat16)
    scores, recents, lates = [], [], []
    for n, i in enumerate(asked):
        limit = table[2, partner(insts, ops, i, core)] * BLK
        query = questions[n][0:rows, :]
        score = contract_last(query, windows[n][:, :HDIM])
        scores.append(jnp.where(within < limit, score, -jnp.inf))
        keys = jnp.concatenate([questions[n][rows : rows + FEW, :], empty])
        lates.append(jnp.concatenate([questions[n][rows + FEW :, :], empty]))
        recents.append(jnp.where(col <= step, contract_last(query, keys), -jnp.inf))
    done = attend_all(scores, recents, [window[:, HDIM:] for window in windows])
    for n, (mixed, weight) in enumerate(done):
        out = mixed + jnp.dot(
            weight.astype(jnp.bfloat16), lates[n], preferred_element_type=jnp.float32
        )
        outs[n][...] = out.astype(jnp.bfloat16)


def contract_last(a, b):
    return lax.dot_general(a, b, (((1,), (1,)), ((), ())), preferred_element_type=jnp.float32)


def widest(score):
    return functools.reduce(
        jnp.maximum, [score[:, k : k + HDIM] for k in range(0, score.shape[1], HDIM)]
    )


def attend_all(scores, recents, values):
    scale = math.log2(math.e) / math.sqrt(HDIM)
    weights = []
    for score, recent in zip(scores, recents):
        top = jnp.max(jnp.maximum(widest(score), recent), axis=1, keepdims=True)
        cached = jnp.exp2((score - top) * scale)
        late = jnp.exp2((recent - top) * scale)
        folded = sum([cached[:, k : k + HDIM] for k in range(0, cached.shape[1], HDIM)], late)
        share = 1.0 / jnp.sum(folded, axis=1, keepdims=True)
        weights.append((cached.astype(jnp.bfloat16), late * share, share))
    return [
        (jnp.dot(cached, value, preferred_element_type=jnp.float32) * share, late)
        for (cached, late, share), value in zip(weights, values)
    ]


def stay_requests(stride, rows, group, first, count, size, lists, spread, pool, recent, attn, late):
    group = math.gcd(group, count)

    def some(g, _):
        places = [first + g * group + u for u in range(group)]
        picked = [pl.ds(lists[0, at], rows, stride=stride) for at in places]
        windows = [pl.ds(pl.multiple_of(lists[1, at] * BLK, BLK), size) for at in places]
        queries = [spread[at, :].astype(jnp.bfloat16) for at in picked]
        recents = [recent[at, :] for at in picked]
        scores = [contract_last(q, pool[w, :HDIM]) for q, w in zip(queries, windows)]
        done = attend_all(scores, recents, [pool[w, HDIM:] for w in windows])
        for at, (mixed, weight) in zip(picked, done):
            attn[at, :] = mixed
            late[at, :] = weight
        return 0

    lax.fori_loop(0, count // group, some, 0)


def long_kernel(
    stride, steps, group, after, lists, spread, pool, fresh, weight_h,
    attn, late, recent, peer_w, sems,
):
    slots = lists.shape[1]
    rows = spread.shape[0] // stride
    heads = rows // steps
    half = peer_w.shape[1]
    peer = (1 - lax.axis_index("tp")) * half
    load = start_copies([(weight_h.at[:, pl.ds(pl.multiple_of(peer, HDIM), half)], peer_w)], sems)
    slot = lax.broadcasted_iota(jnp.int32, (slots, steps * slots), 0)
    col = lax.broadcasted_iota(jnp.int32, (slots, steps * slots), 1)
    for i in range(rows):
        at = pl.ds(i * stride, slots)
        score = contract_last(spread[at, :].astype(jnp.bfloat16), fresh[:, :HDIM])
        mine = (col % slots == slot) & (col // slots <= i // heads)
        recent[at, :] = jnp.where(mine, score, -jnp.inf)
    longer = pool.shape[0] // BLK - slots
    stay_requests(stride, rows, group, 0, longer, WIN, lists, spread, pool, recent, attn, late)
    load[0].wait()


def short_kernel(
    stride, group, after, lists, spread, pool, fresh, weight_h, recent, attn_in, late_in,
    attn, late, own_w, sems,
):
    slots = lists.shape[1]
    rows = spread.shape[0] // stride
    half = own_w.shape[1]
    own = lax.axis_index("tp") * half
    load = start_copies([(weight_h.at[:, pl.ds(pl.multiple_of(own, HDIM), half)], own_w)], sems)
    longer = pool.shape[0] // BLK - slots
    stay_requests(
        stride, rows, group, longer, slots - longer, BLK, lists, spread, pool, recent, attn, late
    )
    for i in range(rows):
        at = pl.ds(i * stride, slots)
        attn[at, :] = attn[at, :] + jnp.dot(
            late[at, :].astype(jnp.bfloat16), fresh[:, HDIM:], preferred_element_type=jnp.float32
        )
    load[0].wait()


def move_kernel(ops, asked, steps, slots, group, after, table, own_q, peer_q, fresh, *refs):
    blocks, (found, sent) = refs[:ops], refs[ops:]
    rows = own_q.shape[1]
    heads = rows // steps
    insts = table.shape[1]
    core = lax.axis_index("tp")
    shape = (2 * rows, steps * slots)
    step = lax.broadcasted_iota(jnp.int32, shape, 0) // heads % steps
    col = lax.broadcasted_iota(jnp.int32, shape, 1)
    owner = jnp.where(col // slots <= step, col % slots, -1)
    within = lax.broadcasted_iota(jnp.int32, (2 * rows, WIN), 1)
    for i in asked:
        found[i] = blocks[i][0:rows, :].astype(jnp.float32)
        sent[i] = blocks[i][rows : 2 * rows, :]
    moved = [i for i in range(ops) if i not in asked]
    for first in range(0, len(moved), group):
        batch = moved[first : first + group]
        queries, recents, scores = [], [], []
        for i in batch:
            query = own_q[i]
            if i < ops - 1:
                query = jnp.concatenate([query, peer_q[i]])
            queries.append(query)
        for i, query in zip(batch, queries):
            m = partner(insts, ops, i, core)
            score = contract_last(query, blocks[i][:, :HDIM])
            limit = table[1, m] * BLK
            scores.append(jnp.where(within[: query.shape[0]] < limit, score, -jnp.inf))
        for i, query in zip(batch, queries):
            recent = contract_last(query, fresh[:, :HDIM])
            j = table[0, partner(insts, ops, i, core)]
            recents.append(jnp.where(owner[: query.shape[0]] == j, recent, -jnp.inf))
        done = attend_all(scores, recents, [blocks[i][:, HDIM:] for i in batch])
        for i, (mixed, weight) in zip(batch, done):
            out = mixed + jnp.dot(
                weight.astype(jnp.bfloat16), fresh[:, HDIM:], preferred_element_type=jnp.float32
            )
            found[i] = out[:rows]
            if i < ops - 1:
                sent[i] = out[rows:].astype(jnp.bfloat16)


def project_kernel(ops, stride, chunks, table, attn, found, arrived, weight, partial, lhs, merged):
    rows = found.shape[1]
    insts = table.shape[1]
    slots = stride - PAD
    steps = lhs.shape[0] // slots
    heads = rows // steps
    core = lax.axis_index("tp")
    for i in range(ops):
        j = table[0, partner(insts, ops, i, core)]
        merged[pl.ds(j, rows, stride=stride), :] = found[i]
    for i in range(ops - 1):
        j = table[0, partner(insts, ops, i, 1 - core)]
        merged[pl.ds(j, rows, stride=stride), :] = arrived[i].astype(jnp.float32)
    for s in range(steps):
        for h in range(heads):
            lhs[s * slots : (s + 1) * slots, h * HDIM : (h + 1) * HDIM] = merged[
                pl.ds((s * heads + h) * stride, slots), :
            ].astype(jnp.bfloat16)
    tile = partial.shape[1] // chunks
    for n in range(chunks):
        cols = slice(n * tile, (n + 1) * tile)
        partial[:, cols] = jnp.dot(
            lhs[...], weight[:, cols], preferred_element_type=jnp.float32
        ).astype(jnp.bfloat16)


def own_kernel(chunks, lhs, weight, out):
    tile = out.shape[1] // chunks
    for n in range(chunks):
        cols = slice(n * tile, (n + 1) * tile)
        out[:, cols] = jnp.dot(lhs[...], weight[:, cols], preferred_element_type=jnp.float32)


def add_kernel(chunks, own, others, out_h, out, sems):
    part = out.shape[0] // chunks
    copies = []
    for n in range(chunks):
        at = pl.ds(n * part, part)
        out[at, :] = (own[at, :] + others[at, :].astype(jnp.float32)).astype(jnp.bfloat16)
        copies.append(pltpu.make_async_copy(out.at[at], out_h.at[at], sems.at[n]))
        copies[-1].start()
    for copy in copies:
        copy.wait()


def call(kernel, operands, outs, scratch=(), limit=8, cost=None, aliases=None):
    specs = [pl.BlockSpec(memory_space=space) for space, _ in operands]
    return pl.pallas_call(
        kernel,
        out_shape=[space(shape.shape, shape.dtype) for space, shape in outs],
        in_specs=specs,
        out_specs=[pl.BlockSpec(memory_space=space) for space, _ in outs],
        scratch_shapes=list(scratch),
        compiler_params=pltpu.CompilerParams(vmem_limit_bytes=limit * MIB),
        cost_estimate=cost,
        input_output_aliases=aliases or {},
    )(*[pltpu.with_memory_space_constraint(array, space) for space, array in operands])


def body(queries, new_kv, cache_pool, lengths, anchor, out_weight):
    steps, slots, width = queries.shape
    heads = width // HDIM
    rows = steps * heads
    insts = lax.axis_size("inst")
    cores = lax.axis_size("tp")
    kvw = cache_pool.shape[1]
    depth, columns = out_weight.shape
    half = columns // cores
    ops = insts // 2
    stride = slots + PAD
    hbm, vmem, smem = pltpu.HBM, pltpu.VMEM, pltpu.SMEM
    dma = pltpu.SemaphoreType.DMA

    def bf16(*shape):
        return jax.ShapeDtypeStruct(shape, jnp.bfloat16)

    def f32(*shape):
        return jax.ShapeDtypeStruct(shape, jnp.float32)

    asked = (1,)
    table, lists, pool, spread, fresh, own_q, sent_q, asked_f, *sends = call(
        functools.partial(plan_kernel, ops, asked, stride),
        [
            (hbm, anchor),
            (hbm, lengths),
            (hbm, queries),
            (hbm, new_kv.reshape(steps * slots, kvw)),
            (hbm, cache_pool),
        ],
        [
            (smem, jax.ShapeDtypeStruct((3, insts), jnp.int32)),
            (smem, jax.ShapeDtypeStruct((2, slots), jnp.int32)),
            (vmem, bf16(*cache_pool.shape)),
            (vmem, f32(rows * stride, HDIM)),
            (vmem, bf16(steps * slots, kvw)),
            (vmem, bf16(ops, rows, HDIM)),
            (vmem, bf16(ops - 1, rows, HDIM)),
            (vmem, bf16(len(asked), 2 * FEW, HDIM)),
        ]
        + [(vmem, bf16(WIN, kvw))] * ops,
        [
            smem(anchor.shape, jnp.int32),
            smem(lengths.shape, jnp.int32),
            smem((insts,), jnp.int32),
            vmem(queries.shape, jnp.bfloat16),
            vmem((steps * slots + PAD, HDIM), jnp.float32),
            vmem((steps * slots + PAD, HDIM), jnp.float32),
            vmem((2 * FEW, HDIM), jnp.float32),
            dma((5,)),
        ],
    )
    swap = [(c, cores - 1 - c) for c in range(cores)]
    peer_q = lax.ppermute(sent_q, "tp", swap)

    def exchange(i, array):
        pairs = []
        for a in range(insts):
            for c in range(cores):
                m = 1 if i == ops - 1 else insts - 2 - 2 * i + c
                pairs.append((a * cores + c, (a ^ m) * cores + c))
        return lax.ppermute(array, ("inst", "tp"), pairs)

    kept = [i for i in range(ops) if i not in asked]
    *handed, questions = call(
        functools.partial(ask_kernel, asked),
        [(vmem, own_q), (vmem, peer_q), (vmem, asked_f)] + [(vmem, sends[i]) for i in kept],
        [(vmem, bf16(WIN, kvw))] * len(kept)
        + [(vmem, bf16(2 * rows + 2 * FEW, HDIM))] * len(asked),
        aliases={3 + n: n for n in range(len(kept))},
    )
    questions = [questions]
    blocks = [None] * ops
    for i, block in zip(kept, handed):
        blocks[i] = exchange(i, block)
    asking = [exchange(i, question) for i, question in zip(asked, questions)]
    half_cost = pl.CostEstimate(
        flops=100 * slots * rows * WIN * HDIM, bytes_accessed=10 * MIB, transcendentals=0
    )
    attn, late, recent, peer_w = call(
        functools.partial(long_kernel, stride, steps, 8),
        [
            (vmem, questions[0]),
            (smem, lists),
            (vmem, spread),
            (vmem, pool),
            (vmem, fresh),
            (hbm, out_weight),
        ],
        [(vmem, f32(rows * stride, HDIM))] * 3 + [(vmem, bf16(depth, half))],
        [dma((1,))],
        cost=half_cost,
    )
    answers = call(
        functools.partial(answer_kernel, ops, asked, steps),
        [(vmem, attn), (smem, table)]
        + [(vmem, question) for question in asking]
        + [(vmem, sends[i]) for i in asked],
        [(vmem, bf16(2 * rows, HDIM))] * len(asked),
    )
    for i, answer in zip(asked, answers):
        blocks[i] = exchange(i, answer)
    attn, late, own_w = call(
        functools.partial(short_kernel, stride, 8),
        [
            (vmem, answers[0]),
            (smem, lists),
            (vmem, spread),
            (vmem, pool),
            (vmem, fresh),
            (hbm, out_weight),
            (vmem, recent),
            (vmem, attn),
            (vmem, late),
        ],
        [(vmem, f32(rows * stride, HDIM))] * 2 + [(vmem, bf16(depth, half))],
        [dma((1,))],
        cost=half_cost,
        aliases={7: 0, 8: 1},
    )

    found, sent = call(
        functools.partial(move_kernel, ops, asked, steps, slots, 4),
        [(vmem, own_w), (smem, table), (vmem, own_q), (vmem, peer_q), (vmem, fresh)]
        + [(vmem, block) for block in blocks],
        [(vmem, f32(ops, rows, HDIM)), (vmem, bf16(ops - 1, rows, HDIM))],
    )
    arrived = lax.ppermute(sent, "tp", swap)
    chunks = half // WIN
    partial, lhs, _ = call(
        functools.partial(project_kernel, ops, stride, chunks),
        [(smem, table), (vmem, attn), (vmem, found), (vmem, arrived), (vmem, peer_w)],
        [
            (vmem, bf16(steps * slots, half)),
            (vmem, bf16(steps * slots, width)),
            (vmem, f32(rows * stride, HDIM)),
        ],
        aliases={1: 2},
    )
    others = lax.ppermute(partial, "tp", swap)
    (own,) = call(
        functools.partial(own_kernel, chunks),
        [(vmem, lhs), (vmem, own_w)],
        [(vmem, f32(steps * slots, half))],
        cost=pl.CostEstimate(
            flops=2 * steps * slots * width * half, bytes_accessed=6 * MIB, transcendentals=0
        ),
    )
    (result,) = call(
        functools.partial(add_kernel, 4),
        [(vmem, own), (vmem, others)],
        [(hbm, bf16(steps * slots, half))],
        [vmem((steps * slots, half), jnp.bfloat16), dma((4,))],
    )
    return result.reshape(steps, slots, half)


def solution(mesh):
    placed = (
        P(None, ("groups", "inst"), "tp"),
        P(None, ("groups", "inst"), None),
        P(("groups", "inst"), None),
        P("groups", None),
        P("groups", None),
        P("tp", None),
    )
    return jax.shard_map(
        body,
        mesh=mesh,
        in_specs=placed,
        out_specs=P(None, ("groups", "inst"), "tp"),
        check_vma=False,
    )
```

```python
import functools
import math

import jax
import jax.numpy as jnp
from jax import lax
from jax.experimental import pallas as pl
from jax.experimental.pallas import tpu as pltpu
from jax.sharding import PartitionSpec as P

HDIM = 128
BLK = 128
MAXB = 2
WIN = MAXB * BLK
PAD = 8
FEW = 16
MIB = 1024 * 1024


def partner(insts, ops, i, core):
    return jnp.int32(1) if i == ops - 1 else insts - 2 - 2 * i + core


def start_copies(pairs, sems):
    copies = [pltpu.make_async_copy(a, b, sems.at[n]) for n, (a, b) in enumerate(pairs)]
    for copy in copies:
        copy.start()
    return copies


def plan_kernel(
    ops, asked, stride, anchor_h, lengths_h, queries_h, fresh_h, pool_h,
    table, lists, pool, spread, fresh, own_q, sent_q, asked_f, *refs,
):
    sends, (anchor, lengths, offs, queries, keys, values, few, sems) = refs[:ops], refs[ops:]
    insts, slots = anchor.shape
    steps, _, width = queries.shape
    heads = width // HDIM
    rows = steps * heads
    blocks = pool.shape[0] // BLK
    own, core = lax.axis_index("inst"), lax.axis_index("tp")
    loads = start_copies(
        [
            (anchor_h, anchor),
            (lengths_h, lengths),
            (queries_h, queries),
            (fresh_h, fresh),
            (pool_h, pool),
        ],
        sems,
    )
    loads[0].wait()
    loads[1].wait()
    for m in range(insts):
        table[0, m] = slots
        table[1, m] = 1
        table[2, m] = 1
        offs[m] = 0
    longer = blocks - slots
    start, found = jnp.int32(0), jnp.int32(0)
    for j in range(slots):
        source, count = anchor[own, j], lengths[own, j]
        dest = (2 * own - source) & (insts - 1)
        table[0, own ^ source] = j
        table[1, own ^ source] = lengths[source, j]
        table[2, own ^ dest] = count
        offs[own ^ dest] = start
        place = jnp.where(count > 1, found, longer + j - found)
        lists[0, place] = j
        lists[1, place] = start
        start = start + count
        found = found + count - 1
    loads[2].wait()
    for s in range(steps):
        for h in range(heads):
            spread[pl.ds((s * heads + h) * stride, slots), :] = queries[
                s, :, h * HDIM : (h + 1) * HDIM
            ].astype(jnp.float32)
    for i in range(ops):
        j = table[0, partner(insts, ops, i, core)]
        own_q[i] = spread[pl.ds(j, rows, stride=stride), :].astype(jnp.bfloat16)
    for i in range(ops - 1):
        j = table[0, partner(insts, ops, i, 1 - core)]
        sent_q[i] = spread[pl.ds(j, rows, stride=stride), :].astype(jnp.bfloat16)
    loads[3].wait()
    keys[0 : steps * slots, :] = fresh[:, :HDIM].astype(jnp.float32)
    values[0 : steps * slots, :] = fresh[:, HDIM:].astype(jnp.float32)
    few[...] = jnp.zeros_like(few)
    for n, i in enumerate(asked):
        j = table[0, partner(insts, ops, i, core)]
        for u in range(steps):
            few[u : u + 1, :] = keys[pl.ds(u * slots + j, 1), :]
            few[FEW + u : FEW + u + 1, :] = values[pl.ds(u * slots + j, 1), :]
        asked_f[n] = few[...].astype(jnp.bfloat16)
    loads[4].wait()
    for i in range(ops):
        at = offs[partner(insts, ops, i, core)]
        for b in range(MAXB):
            row = pl.multiple_of(jnp.minimum(at + b, blocks - 1) * BLK, BLK)
            sends[i][b * BLK : (b + 1) * BLK, :] = pool[pl.ds(row, BLK), :]


def ask_kernel(asked, own_q, peer_q, asked_f, *refs):
    outs = refs[-len(asked) :]
    rows = own_q.shape[1]
    for n, i in enumerate(asked):
        outs[n][0:rows, :] = own_q[i]
        outs[n][rows : 2 * rows, :] = peer_q[i]
        outs[n][2 * rows :, :] = asked_f[n]


def answer_kernel(ops, asked, steps, table, *refs):
    count = len(asked)
    questions, windows, outs = refs[:count], refs[count : 2 * count], refs[2 * count :]
    rows = outs[0].shape[0]
    heads = rows // 2 // steps
    insts = table.shape[1]
    core = lax.axis_index("tp")
    step = lax.broadcasted_iota(jnp.int32, (rows, HDIM), 0) // heads % steps
    col = lax.broadcasted_iota(jnp.int32, (rows, HDIM), 1)
    within = lax.broadcasted_iota(jnp.int32, (rows, WIN), 1)
    empty = jnp.zeros((HDIM - FEW, HDIM), jnp.bfloat16)
    scores, recents, lates = [], [], []
    for n, i in enumerate(asked):
        limit = table[2, partner(insts, ops, i, core)] * BLK
        query = questions[n][0:rows, :]
        score = contract_last(query, windows[n][:, :HDIM])
        scores.append(jnp.where(within < limit, score, -jnp.inf))
        keys = jnp.concatenate([questions[n][rows : rows + FEW, :], empty])
        lates.append(jnp.concatenate([questions[n][rows + FEW :, :], empty]))
        recents.append(jnp.where(col <= step, contract_last(query, keys), -jnp.inf))
    done = attend_all(scores, recents, [window[:, HDIM:] for window in windows])
    for n, (mixed, weight) in enumerate(done):
        out = mixed + jnp.dot(
            weight.astype(jnp.bfloat16), lates[n], preferred_element_type=jnp.float32
        )
        outs[n][...] = out.astype(jnp.bfloat16)


def contract_last(a, b):
    return lax.dot_general(a, b, (((1,), (1,)), ((), ())), preferred_element_type=jnp.float32)


def widest(score):
    return functools.reduce(
        jnp.maximum, [score[:, k : k + HDIM] for k in range(0, score.shape[1], HDIM)]
    )


def attend_all(scores, recents, values):
    scale = math.log2(math.e) / math.sqrt(HDIM)
    weights = []
    for score, recent in zip(scores, recents):
        top = jnp.max(jnp.maximum(widest(score), recent), axis=1, keepdims=True)
        cached = jnp.exp2((score - top) * scale)
        late = jnp.exp2((recent - top) * scale)
        folded = sum([cached[:, k : k + HDIM] for k in range(0, cached.shape[1], HDIM)], late)
        share = 1.0 / jnp.sum(folded, axis=1, keepdims=True)
        weights.append((cached.astype(jnp.bfloat16), late * share, share))
    return [
        (jnp.dot(cached, value, preferred_element_type=jnp.float32) * share, late)
        for (cached, late, share), value in zip(weights, values)
    ]


def stay_requests(stride, rows, group, first, count, size, lists, spread, pool, recent, attn, late):
    group = math.gcd(group, count)

    def some(g, _):
        places = [first + g * group + u for u in range(group)]
        picked = [pl.ds(lists[0, at], rows, stride=stride) for at in places]
        windows = [pl.ds(pl.multiple_of(lists[1, at] * BLK, BLK), size) for at in places]
        queries = [spread[at, :].astype(jnp.bfloat16) for at in picked]
        recents = [recent[at, :] for at in picked]
        scores = [contract_last(q, pool[w, :HDIM]) for q, w in zip(queries, windows)]
        done = attend_all(scores, recents, [pool[w, HDIM:] for w in windows])
        for at, (mixed, weight) in zip(picked, done):
            attn[at, :] = mixed
            late[at, :] = weight
        return 0

    lax.fori_loop(0, count // group, some, 0)


def stay_kernel(
    stride, steps, group, after, lists, spread, pool, fresh, weight_h,
    attn, peer_w, own_w, recent, late, sems,
):
    slots = lists.shape[1]
    rows = spread.shape[0] // stride
    heads = rows // steps
    half = peer_w.shape[1]
    core = lax.axis_index("tp")
    own_cols = pl.ds(pl.multiple_of(core * half, HDIM), half)
    peer_cols = pl.ds(pl.multiple_of((1 - core) * half, HDIM), half)
    loads = start_copies(
        [(weight_h.at[:, peer_cols], peer_w), (weight_h.at[:, own_cols], own_w)], sems
    )
    slot = lax.broadcasted_iota(jnp.int32, (slots, steps * slots), 0)
    col = lax.broadcasted_iota(jnp.int32, (slots, steps * slots), 1)
    for i in range(rows):
        at = pl.ds(i * stride, slots)
        score = contract_last(spread[at, :].astype(jnp.bfloat16), fresh[:, :HDIM])
        mine = (col % slots == slot) & (col // slots <= i // heads)
        recent[at, :] = jnp.where(mine, score, -jnp.inf)
    longer = pool.shape[0] // BLK - slots
    state = (lists, spread, pool, recent, attn, late)
    stay_requests(stride, rows, group, 0, longer, WIN, *state)
    stay_requests(stride, rows, group, longer, slots - longer, BLK, *state)
    for i in range(rows):
        at = pl.ds(i * stride, slots)
        attn[at, :] = attn[at, :] + jnp.dot(
            late[at, :].astype(jnp.bfloat16), fresh[:, HDIM:], preferred_element_type=jnp.float32
        )
    for load in loads:
        load.wait()


def move_kernel(ops, asked, steps, slots, group, after, table, own_q, peer_q, fresh, *refs):
    blocks, (found, sent) = refs[:ops], refs[ops:]
    rows = own_q.shape[1]
    heads = rows // steps
    insts = table.shape[1]
    core = lax.axis_index("tp")
    shape = (2 * rows, steps * slots)
    step = lax.broadcasted_iota(jnp.int32, shape, 0) // heads % steps
    col = lax.broadcasted_iota(jnp.int32, shape, 1)
    owner = jnp.where(col // slots <= step, col % slots, -1)
    within = lax.broadcasted_iota(jnp.int32, (2 * rows, WIN), 1)
    for i in asked:
        found[i] = blocks[i][0:rows, :].astype(jnp.float32)
        sent[i] = blocks[i][rows : 2 * rows, :]
    moved = [i for i in range(ops) if i not in asked]
    for first in range(0, len(moved), group):
        batch = moved[first : first + group]
        queries, recents, scores = [], [], []
        for i in batch:
            query = own_q[i]
            if i < ops - 1:
                query = jnp.concatenate([query, peer_q[i]])
            queries.append(query)
        for i, query in zip(batch, queries):
            m = partner(insts, ops, i, core)
            score = contract_last(query, blocks[i][:, :HDIM])
            limit = table[1, m] * BLK
            scores.append(jnp.where(within[: query.shape[0]] < limit, score, -jnp.inf))
        for i, query in zip(batch, queries):
            recent = contract_last(query, fresh[:, :HDIM])
            j = table[0, partner(insts, ops, i, core)]
            recents.append(jnp.where(owner[: query.shape[0]] == j, recent, -jnp.inf))
        done = attend_all(scores, recents, [blocks[i][:, HDIM:] for i in batch])
        for i, (mixed, weight) in zip(batch, done):
            out = mixed + jnp.dot(
                weight.astype(jnp.bfloat16), fresh[:, HDIM:], preferred_element_type=jnp.float32
            )
            found[i] = out[:rows]
            if i < ops - 1:
                sent[i] = out[rows:].astype(jnp.bfloat16)


def project_kernel(ops, stride, chunks, table, attn, found, arrived, weight, partial, lhs, merged):
    rows = found.shape[1]
    insts = table.shape[1]
    slots = stride - PAD
    steps = lhs.shape[0] // slots
    heads = rows // steps
    core = lax.axis_index("tp")
    for i in range(ops):
        j = table[0, partner(insts, ops, i, core)]
        merged[pl.ds(j, rows, stride=stride), :] = found[i]
    for i in range(ops - 1):
        j = table[0, partner(insts, ops, i, 1 - core)]
        merged[pl.ds(j, rows, stride=stride), :] = arrived[i].astype(jnp.float32)
    for s in range(steps):
        for h in range(heads):
            lhs[s * slots : (s + 1) * slots, h * HDIM : (h + 1) * HDIM] = merged[
                pl.ds((s * heads + h) * stride, slots), :
            ].astype(jnp.bfloat16)
    tile = partial.shape[1] // chunks
    for n in range(chunks):
        cols = slice(n * tile, (n + 1) * tile)
        partial[:, cols] = jnp.dot(
            lhs[...], weight[:, cols], preferred_element_type=jnp.float32
        ).astype(jnp.bfloat16)


def own_kernel(chunks, lhs, weight, out):
    tile = out.shape[1] // chunks
    for n in range(chunks):
        cols = slice(n * tile, (n + 1) * tile)
        out[:, cols] = jnp.dot(lhs[...], weight[:, cols], preferred_element_type=jnp.float32)


def add_kernel(chunks, own, others, out_h, out, sems):
    part = out.shape[0] // chunks
    copies = []
    for n in range(chunks):
        at = pl.ds(n * part, part)
        out[at, :] = (own[at, :] + others[at, :].astype(jnp.float32)).astype(jnp.bfloat16)
        copies.append(pltpu.make_async_copy(out.at[at], out_h.at[at], sems.at[n]))
        copies[-1].start()
    for copy in copies:
        copy.wait()


def call(kernel, operands, outs, scratch=(), limit=8, cost=None, aliases=None):
    specs = [pl.BlockSpec(memory_space=space) for space, _ in operands]
    return pl.pallas_call(
        kernel,
        out_shape=[space(shape.shape, shape.dtype) for space, shape in outs],
        in_specs=specs,
        out_specs=[pl.BlockSpec(memory_space=space) for space, _ in outs],
        scratch_shapes=list(scratch),
        compiler_params=pltpu.CompilerParams(vmem_limit_bytes=limit * MIB),
        cost_estimate=cost,
        input_output_aliases=aliases or {},
    )(*[pltpu.with_memory_space_constraint(array, space) for space, array in operands])


def body(queries, new_kv, cache_pool, lengths, anchor, out_weight):
    steps, slots, width = queries.shape
    heads = width // HDIM
    rows = steps * heads
    insts = lax.axis_size("inst")
    cores = lax.axis_size("tp")
    kvw = cache_pool.shape[1]
    depth, columns = out_weight.shape
    half = columns // cores
    ops = insts // 2
    stride = slots + PAD
    hbm, vmem, smem = pltpu.HBM, pltpu.VMEM, pltpu.SMEM
    dma = pltpu.SemaphoreType.DMA

    def bf16(*shape):
        return jax.ShapeDtypeStruct(shape, jnp.bfloat16)

    def f32(*shape):
        return jax.ShapeDtypeStruct(shape, jnp.float32)

    asked = (1,)
    table, lists, pool, spread, fresh, own_q, sent_q, asked_f, *sends = call(
        functools.partial(plan_kernel, ops, asked, stride),
        [
            (hbm, anchor),
            (hbm, lengths),
            (hbm, queries),
            (hbm, new_kv.reshape(steps * slots, kvw)),
            (hbm, cache_pool),
        ],
        [
            (smem, jax.ShapeDtypeStruct((3, insts), jnp.int32)),
            (smem, jax.ShapeDtypeStruct((2, slots), jnp.int32)),
            (vmem, bf16(*cache_pool.shape)),
            (vmem, f32(rows * stride, HDIM)),
            (vmem, bf16(steps * slots, kvw)),
            (vmem, bf16(ops, rows, HDIM)),
            (vmem, bf16(ops - 1, rows, HDIM)),
            (vmem, bf16(len(asked), 2 * FEW, HDIM)),
        ]
        + [(vmem, bf16(WIN, kvw))] * ops,
        [
            smem(anchor.shape, jnp.int32),
            smem(lengths.shape, jnp.int32),
            smem((insts,), jnp.int32),
            vmem(queries.shape, jnp.bfloat16),
            vmem((steps * slots + PAD, HDIM), jnp.float32),
            vmem((steps * slots + PAD, HDIM), jnp.float32),
            vmem((2 * FEW, HDIM), jnp.float32),
            dma((5,)),
        ],
    )
    swap = [(c, cores - 1 - c) for c in range(cores)]
    peer_q = lax.ppermute(sent_q, "tp", swap)

    def exchange(i, array):
        pairs = []
        for a in range(insts):
            for c in range(cores):
                m = 1 if i == ops - 1 else insts - 2 - 2 * i + c
                pairs.append((a * cores + c, (a ^ m) * cores + c))
        return lax.ppermute(array, ("inst", "tp"), pairs)

    kept = [i for i in range(ops) if i not in asked]
    handed = call(
        functools.partial(ask_kernel, asked),
        [(vmem, own_q), (vmem, peer_q), (vmem, asked_f)] + [(vmem, sends[i]) for i in kept],
        [(vmem, bf16(WIN, kvw))] * len(kept)
        + [(vmem, bf16(2 * rows + 2 * FEW, HDIM))] * len(asked),
        aliases={3 + n: n for n in range(len(kept))},
    )
    blocks = [None] * ops
    for i, block in zip(kept, handed):
        blocks[i] = exchange(i, block)
    asking = [exchange(i, question) for i, question in zip(asked, handed[len(kept) :])]
    answers = call(
        functools.partial(answer_kernel, ops, asked, steps),
        [(smem, table)]
        + [(vmem, question) for question in asking]
        + [(vmem, sends[i]) for i in asked],
        [(vmem, bf16(2 * rows, HDIM))] * len(asked),
    )
    for i, answer in zip(asked, answers):
        blocks[i] = exchange(i, answer)
    attn, peer_w, own_w = call(
        functools.partial(stay_kernel, stride, steps, 8),
        [
            (vmem, answers[0]),
            (smem, lists),
            (vmem, spread),
            (vmem, pool),
            (vmem, fresh),
            (hbm, out_weight),
        ],
        [(vmem, f32(rows * stride, HDIM))] + [(vmem, bf16(depth, half))] * 2,
        [
            vmem((rows * stride, HDIM), jnp.float32),
            vmem((rows * stride, HDIM), jnp.float32),
            dma((2,)),
        ],
        cost=pl.CostEstimate(
            flops=200 * slots * rows * WIN * HDIM, bytes_accessed=20 * MIB, transcendentals=0
        ),
    )

    found, sent = call(
        functools.partial(move_kernel, ops, asked, steps, slots, 4),
        [(vmem, own_w), (smem, table), (vmem, own_q), (vmem, peer_q), (vmem, fresh)]
        + [(vmem, block) for block in blocks],
        [(vmem, f32(ops, rows, HDIM)), (vmem, bf16(ops - 1, rows, HDIM))],
    )
    arrived = lax.ppermute(sent, "tp", swap)
    chunks = half // WIN
    partial, lhs, _ = call(
        functools.partial(project_kernel, ops, stride, chunks),
        [(smem, table), (vmem, attn), (vmem, found), (vmem, arrived), (vmem, peer_w)],
        [
            (vmem, bf16(steps * slots, half)),
            (vmem, bf16(steps * slots, width)),
            (vmem, f32(rows * stride, HDIM)),
        ],
        aliases={1: 2},
    )
    others = lax.ppermute(partial, "tp", swap)
    (own,) = call(
        functools.partial(own_kernel, chunks),
        [(vmem, lhs), (vmem, own_w)],
        [(vmem, f32(steps * slots, half))],
        cost=pl.CostEstimate(
            flops=2 * steps * slots * width * half, bytes_accessed=6 * MIB, transcendentals=0
        ),
    )
    (result,) = call(
        functools.partial(add_kernel, 4),
        [(vmem, own), (vmem, others)],
        [(hbm, bf16(steps * slots, half))],
        [vmem((steps * slots, half), jnp.bfloat16), dma((4,))],
    )
    return result.reshape(steps, slots, half)


def solution(mesh):
    placed = (
        P(None, ("groups", "inst"), "tp"),
        P(None, ("groups", "inst"), None),
        P(("groups", "inst"), None),
        P("groups", None),
        P("groups", None),
        P("tp", None),
    )
    return jax.shard_map(
        body,
        mesh=mesh,
        in_specs=placed,
        out_specs=P(None, ("groups", "inst"), "tp"),
        check_vma=False,
    )
```

```python
import functools
import math

import jax
import jax.numpy as jnp
from jax import lax
from jax.experimental import pallas as pl
from jax.experimental.pallas import tpu as pltpu
from jax.sharding import PartitionSpec as P

HDIM = 128
BLK = 128
MAXB = 2
WIN = MAXB * BLK
PAD = 8
PARTS = 4
MIB = 1024 * 1024


def partner(insts, ops, i, core):
    return jnp.int32(1) if i == ops - 1 else insts - 2 - 2 * i + core


def start_copies(pairs, sems):
    copies = [pltpu.make_async_copy(a, b, sems.at[n]) for n, (a, b) in enumerate(pairs)]
    for copy in copies:
        copy.start()
    return copies


def plan_kernel(ops, anchor_h, lengths_h, pool_h, table, lists, pool, *refs):
    sends, (anchor, lengths, offs, sems) = refs[:ops], refs[ops:]
    insts, slots = anchor.shape
    blocks = pool.shape[0] // BLK
    own, core = lax.axis_index("inst"), lax.axis_index("tp")
    part = pool.shape[0] // PARTS
    loads = start_copies(
        [(anchor_h, anchor), (lengths_h, lengths)]
        + [
            (pool_h.at[pl.ds(n * part, part)], pool.at[pl.ds(n * part, part)])
            for n in range(PARTS)
        ],
        sems,
    )
    loads[0].wait()
    loads[1].wait()
    for m in range(insts):
        table[0, m] = slots
        table[1, m] = 1
        offs[m] = 0
    longer = blocks - slots
    start, found = jnp.int32(0), jnp.int32(0)
    for j in range(slots):
        source, count = anchor[own, j], lengths[own, j]
        dest = (2 * own - source) & (insts - 1)
        table[0, own ^ source] = j
        table[1, own ^ source] = lengths[source, j]
        offs[own ^ dest] = start
        place = jnp.where(count > 1, found, longer + j - found)
        lists[0, place] = j
        lists[1, place] = start
        start = start + count
        found = found + count - 1
    for load in loads[2:]:
        load.wait()
    for i in range(ops):
        at = offs[partner(insts, ops, i, core)]
        for b in range(MAXB):
            row = pl.multiple_of(jnp.minimum(at + b, blocks - 1) * BLK, BLK)
            sends[i][b * BLK : (b + 1) * BLK, :] = pool[pl.ds(row, BLK), :]


def query_kernel(
    stride, ops, table, queries_h, fresh_h, spread, fresh, own_q, sent_q, queries, sems
):
    steps, slots, width = queries.shape
    insts = table.shape[1]
    heads = width // HDIM
    rows = steps * heads
    core = lax.axis_index("tp")
    loads = start_copies([(queries_h, queries), (fresh_h, fresh)], sems)
    loads[0].wait()
    for s in range(steps):
        for h in range(heads):
            spread[pl.ds((s * heads + h) * stride, slots), :] = queries[
                s, :, h * HDIM : (h + 1) * HDIM
            ].astype(jnp.float32)
    for i in range(ops):
        j = table[0, partner(insts, ops, i, core)]
        own_q[i] = spread[pl.ds(j, rows, stride=stride), :].astype(jnp.bfloat16)
    for i in range(ops - 1):
        j = table[0, partner(insts, ops, i, 1 - core)]
        sent_q[i] = spread[pl.ds(j, rows, stride=stride), :].astype(jnp.bfloat16)
    loads[1].wait()


def contract_last(a, b):
    return lax.dot_general(a, b, (((1,), (1,)), ((), ())), preferred_element_type=jnp.float32)


def widest(score):
    return functools.reduce(
        jnp.maximum, [score[:, k : k + HDIM] for k in range(0, score.shape[1], HDIM)]
    )


def attend_all(scores, recents, values):
    scale = math.log2(math.e) / math.sqrt(HDIM)
    weights = []
    for score, recent in zip(scores, recents):
        top = jnp.max(jnp.maximum(widest(score), recent), axis=1, keepdims=True)
        cached = jnp.exp2((score - top) * scale)
        late = jnp.exp2((recent - top) * scale)
        folded = sum([cached[:, k : k + HDIM] for k in range(0, cached.shape[1], HDIM)], late)
        share = 1.0 / jnp.sum(folded, axis=1, keepdims=True)
        weights.append((cached.astype(jnp.bfloat16), late * share, share))
    return [
        (jnp.dot(cached, value, preferred_element_type=jnp.float32) * share, late)
        for (cached, late, share), value in zip(weights, values)
    ]


def stay_requests(stride, rows, group, first, count, size, lists, spread, pool, recent, attn, late):
    group = math.gcd(group, count)

    def some(g, _):
        places = [first + g * group + u for u in range(group)]
        picked = [pl.ds(lists[0, at], rows, stride=stride) for at in places]
        windows = [pl.ds(pl.multiple_of(lists[1, at] * BLK, BLK), size) for at in places]
        queries = [spread[at, :].astype(jnp.bfloat16) for at in picked]
        recents = [recent[at, :] for at in picked]
        scores = [contract_last(q, pool[w, :HDIM]) for q, w in zip(queries, windows)]
        done = attend_all(scores, recents, [pool[w, HDIM:] for w in windows])
        for at, (mixed, weight) in zip(picked, done):
            attn[at, :] = mixed
            late[at, :] = weight
        return 0

    lax.fori_loop(0, count // group, some, 0)


def stay_kernel(
    stride, steps, group, lists, spread, pool, fresh, weight_h,
    attn, peer_w, own_w, recent, late, sems,
):
    slots = lists.shape[1]
    rows = spread.shape[0] // stride
    heads = rows // steps
    half = peer_w.shape[1]
    core = lax.axis_index("tp")
    own_cols = pl.ds(pl.multiple_of(core * half, HDIM), half)
    peer_cols = pl.ds(pl.multiple_of((1 - core) * half, HDIM), half)
    loads = start_copies(
        [(weight_h.at[:, peer_cols], peer_w), (weight_h.at[:, own_cols], own_w)], sems
    )
    slot = lax.broadcasted_iota(jnp.int32, (slots, steps * slots), 0)
    col = lax.broadcasted_iota(jnp.int32, (slots, steps * slots), 1)
    for i in range(rows):
        at = pl.ds(i * stride, slots)
        score = contract_last(spread[at, :].astype(jnp.bfloat16), fresh[:, :HDIM])
        mine = (col % slots == slot) & (col // slots <= i // heads)
        recent[at, :] = jnp.where(mine, score, -jnp.inf)
    longer = pool.shape[0] // BLK - slots
    state = (lists, spread, pool, recent, attn, late)
    stay_requests(stride, rows, group, 0, longer, WIN, *state)
    stay_requests(stride, rows, group, longer, slots - longer, BLK, *state)
    for i in range(rows):
        at = pl.ds(i * stride, slots)
        attn[at, :] = attn[at, :] + jnp.dot(
            late[at, :].astype(jnp.bfloat16), fresh[:, HDIM:], preferred_element_type=jnp.float32
        )
    for load in loads:
        load.wait()


def recent_kernel(ops, steps, slots, after, table, own_q, peer_q, fresh, query, recent):
    rows = own_q.shape[1]
    heads = rows // steps
    insts = table.shape[1]
    core = lax.axis_index("tp")
    shape = (2 * rows, steps * slots)
    step = lax.broadcasted_iota(jnp.int32, shape, 0) // heads % steps
    col = lax.broadcasted_iota(jnp.int32, shape, 1)
    owner = jnp.where(col // slots <= step, col % slots, -1)
    for i in range(ops):
        count = 2 * rows if i < ops - 1 else rows
        query[i, 0:rows, :] = own_q[i]
        if i < ops - 1:
            query[i, rows:, :] = peer_q[i]
        score = contract_last(query[i, 0:count, :], fresh[:, :HDIM])
        j = table[0, partner(insts, ops, i, core)]
        recent[i, 0:count, :] = jnp.where(owner[:count] == j, score, -jnp.inf)


def move_kernel(ops, table, query, recent, fresh, *refs):
    blocks, (found, sent) = refs[:ops], refs[ops:]
    rows = found.shape[1]
    insts = table.shape[1]
    core = lax.axis_index("tp")
    within = lax.broadcasted_iota(jnp.int32, (2 * rows, WIN), 1)
    for first in range(0, ops, 4):
        batch = range(first, min(first + 4, ops))
        counts = [2 * rows if i < ops - 1 else rows for i in batch]
        scores = []
        for i, count in zip(batch, counts):
            score = contract_last(query[i, 0:count, :], blocks[i][:, :HDIM])
            limit = table[1, partner(insts, ops, i, core)] * BLK
            scores.append(jnp.where(within[:count] < limit, score, -jnp.inf))
        recents = [recent[i, 0:count, :] for i, count in zip(batch, counts)]
        done = attend_all(scores, recents, [blocks[i][:, HDIM:] for i in batch])
        for i, (mixed, weight) in zip(batch, done):
            out = mixed + jnp.dot(
                weight.astype(jnp.bfloat16), fresh[:, HDIM:], preferred_element_type=jnp.float32
            )
            found[i] = out[:rows]
            if i < ops - 1:
                sent[i] = out[rows:].astype(jnp.bfloat16)


def project_kernel(ops, stride, chunks, table, attn, found, arrived, weight, partial, lhs, merged):
    rows = found.shape[1]
    insts = table.shape[1]
    slots = stride - PAD
    steps = lhs.shape[0] // slots
    heads = rows // steps
    core = lax.axis_index("tp")
    for i in range(ops):
        j = table[0, partner(insts, ops, i, core)]
        merged[pl.ds(j, rows, stride=stride), :] = found[i]
    for i in range(ops - 1):
        j = table[0, partner(insts, ops, i, 1 - core)]
        merged[pl.ds(j, rows, stride=stride), :] = arrived[i].astype(jnp.float32)
    for s in range(steps):
        for h in range(heads):
            lhs[s * slots : (s + 1) * slots, h * HDIM : (h + 1) * HDIM] = merged[
                pl.ds((s * heads + h) * stride, slots), :
            ].astype(jnp.bfloat16)
    tile = partial.shape[1] // chunks
    for n in range(chunks):
        cols = slice(n * tile, (n + 1) * tile)
        partial[:, cols] = jnp.dot(
            lhs[...], weight[:, cols], preferred_element_type=jnp.float32
        ).astype(jnp.bfloat16)


def own_kernel(chunks, lhs, weight, out):
    tile = out.shape[1] // chunks
    for n in range(chunks):
        cols = slice(n * tile, (n + 1) * tile)
        out[:, cols] = jnp.dot(lhs[...], weight[:, cols], preferred_element_type=jnp.float32)


def add_kernel(chunks, own, others, out_h, out, sems):
    part = out.shape[0] // chunks
    copies = []
    for n in range(chunks):
        at = pl.ds(n * part, part)
        out[at, :] = (own[at, :] + others[at, :].astype(jnp.float32)).astype(jnp.bfloat16)
        copies.append(pltpu.make_async_copy(out.at[at], out_h.at[at], sems.at[n]))
        copies[-1].start()
    for copy in copies:
        copy.wait()


def call(kernel, operands, outs, scratch=(), limit=8, cost=None, aliases=None):
    specs = [pl.BlockSpec(memory_space=space) for space, _ in operands]
    return pl.pallas_call(
        kernel,
        out_shape=[space(shape.shape, shape.dtype) for space, shape in outs],
        in_specs=specs,
        out_specs=[pl.BlockSpec(memory_space=space) for space, _ in outs],
        scratch_shapes=list(scratch),
        compiler_params=pltpu.CompilerParams(vmem_limit_bytes=limit * MIB),
        cost_estimate=cost,
        input_output_aliases=aliases or {},
    )(*[pltpu.with_memory_space_constraint(array, space) for space, array in operands])


def body(queries, new_kv, cache_pool, lengths, anchor, out_weight):
    steps, slots, width = queries.shape
    heads = width // HDIM
    rows = steps * heads
    insts = lax.axis_size("inst")
    cores = lax.axis_size("tp")
    kvw = cache_pool.shape[1]
    depth, columns = out_weight.shape
    half = columns // cores
    ops = insts // 2
    stride = slots + PAD
    hbm, vmem, smem = pltpu.HBM, pltpu.VMEM, pltpu.SMEM
    dma = pltpu.SemaphoreType.DMA

    def bf16(*shape):
        return jax.ShapeDtypeStruct(shape, jnp.bfloat16)

    def f32(*shape):
        return jax.ShapeDtypeStruct(shape, jnp.float32)

    table, lists, pool, *sends = call(
        functools.partial(plan_kernel, ops),
        [(hbm, anchor), (hbm, lengths), (hbm, cache_pool)],
        [
            (smem, jax.ShapeDtypeStruct((2, insts), jnp.int32)),
            (smem, jax.ShapeDtypeStruct((2, slots), jnp.int32)),
            (vmem, bf16(*cache_pool.shape)),
        ]
        + [(vmem, bf16(WIN, kvw))] * ops,
        [
            smem(anchor.shape, jnp.int32),
            smem(lengths.shape, jnp.int32),
            smem((insts,), jnp.int32),
            dma((2 + PARTS,)),
        ],
    )
    blocks = [None] * ops
    for i in reversed(range(ops)):
        pairs = []
        for a in range(insts):
            for c in range(cores):
                m = 1 if i == ops - 1 else insts - 2 - 2 * i + c
                pairs.append((a * cores + c, (a ^ m) * cores + c))
        blocks[i] = lax.ppermute(sends[i], ("inst", "tp"), pairs)

    spread, fresh, own_q, sent_q = call(
        functools.partial(query_kernel, stride, ops),
        [(smem, table), (hbm, queries), (hbm, new_kv.reshape(steps * slots, kvw))],
        [
            (vmem, f32(rows * stride, HDIM)),
            (vmem, bf16(steps * slots, kvw)),
            (vmem, bf16(ops, rows, HDIM)),
            (vmem, bf16(ops - 1, rows, HDIM)),
        ],
        [vmem(queries.shape, jnp.bfloat16), dma((2,))],
        cost=pl.CostEstimate(flops=0, bytes_accessed=MIB, transcendentals=0),
    )
    swap = [(c, cores - 1 - c) for c in range(cores)]
    peer_q = lax.ppermute(sent_q, "tp", swap)

    attn, peer_w, own_w = call(
        functools.partial(stay_kernel, stride, steps, 8),
        [(smem, lists), (vmem, spread), (vmem, pool), (vmem, fresh), (hbm, out_weight)],
        [(vmem, f32(rows * stride, HDIM))] + [(vmem, bf16(depth, half))] * 2,
        [
            vmem((rows * stride, HDIM), jnp.float32),
            vmem((rows * stride, HDIM), jnp.float32),
            dma((2,)),
        ],
        cost=pl.CostEstimate(
            flops=4 * slots * rows * WIN * HDIM, bytes_accessed=20 * MIB, transcendentals=0
        ),
    )
    query, recent = call(
        functools.partial(recent_kernel, ops, steps, slots),
        [(vmem, own_w), (smem, table), (vmem, own_q), (vmem, peer_q), (vmem, fresh)],
        [(vmem, bf16(ops, 2 * rows, HDIM)), (vmem, f32(ops, 2 * rows, steps * slots))],
    )
    found, sent = call(
        functools.partial(move_kernel, ops),
        [(smem, table), (vmem, query), (vmem, recent), (vmem, fresh)]
        + [(vmem, block) for block in blocks],
        [(vmem, f32(ops, rows, HDIM)), (vmem, bf16(ops - 1, rows, HDIM))],
    )
    arrived = lax.ppermute(sent, "tp", swap)
    chunks = half // WIN
    partial, lhs, _ = call(
        functools.partial(project_kernel, ops, stride, chunks),
        [(smem, table), (vmem, attn), (vmem, found), (vmem, arrived), (vmem, peer_w)],
        [
            (vmem, bf16(steps * slots, half)),
            (vmem, bf16(steps * slots, width)),
            (vmem, f32(rows * stride, HDIM)),
        ],
        aliases={1: 2},
    )
    others = lax.ppermute(partial, "tp", swap)
    (own,) = call(
        functools.partial(own_kernel, chunks),
        [(vmem, lhs), (vmem, own_w)],
        [(vmem, f32(steps * slots, half))],
        cost=pl.CostEstimate(
            flops=2 * steps * slots * width * half, bytes_accessed=6 * MIB, transcendentals=0
        ),
    )
    (result,) = call(
        functools.partial(add_kernel, 4),
        [(vmem, own), (vmem, others)],
        [(hbm, bf16(steps * slots, half))],
        [vmem((steps * slots, half), jnp.bfloat16), dma((4,))],
    )
    return result.reshape(steps, slots, half)


def solution(mesh):
    placed = (
        P(None, ("groups", "inst"), "tp"),
        P(None, ("groups", "inst"), None),
        P(("groups", "inst"), None),
        P("groups", None),
        P("groups", None),
        P("tp", None),
    )
    return jax.shard_map(
        body,
        mesh=mesh,
        in_specs=placed,
        out_specs=P(None, ("groups", "inst"), "tp"),
        check_vma=False,
    )
```

```python
import functools
import math

import jax
import jax.numpy as jnp
from jax import lax
from jax.experimental import pallas as pl
from jax.experimental.pallas import tpu as pltpu
from jax.sharding import PartitionSpec as P

HDIM = 128
BLK = 128
MAXB = 2
WIN = MAXB * BLK
PAD = 8
PARTS = 4
MIB = 1024 * 1024


def partner(insts, ops, i, core):
    return jnp.int32(1) if i == ops - 1 else insts - 2 - 2 * i + core


def start_copies(pairs, sems):
    copies = [pltpu.make_async_copy(a, b, sems.at[n]) for n, (a, b) in enumerate(pairs)]
    for copy in copies:
        copy.start()
    return copies


def plan_kernel(ops, anchor_h, lengths_h, pool_h, table, lists, pool, *refs):
    sends, (anchor, lengths, offs, sems) = refs[:ops], refs[ops:]
    insts, slots = anchor.shape
    blocks = pool.shape[0] // BLK
    own, core = lax.axis_index("inst"), lax.axis_index("tp")
    part = pool.shape[0] // PARTS
    loads = start_copies(
        [(anchor_h, anchor), (lengths_h, lengths)]
        + [
            (pool_h.at[pl.ds(n * part, part)], pool.at[pl.ds(n * part, part)])
            for n in range(PARTS)
        ],
        sems,
    )
    loads[0].wait()
    loads[1].wait()
    for m in range(insts):
        table[0, m] = slots
        table[1, m] = 1
        offs[m] = 0
    longer = blocks - slots
    start, found = jnp.int32(0), jnp.int32(0)
    for j in range(slots):
        source, count = anchor[own, j], lengths[own, j]
        dest = (2 * own - source) & (insts - 1)
        table[0, own ^ source] = j
        table[1, own ^ source] = lengths[source, j]
        offs[own ^ dest] = start
        place = jnp.where(count > 1, found, longer + j - found)
        lists[0, place] = j
        lists[1, place] = start
        start = start + count
        found = found + count - 1
    for load in loads[2:]:
        load.wait()
    for i in range(ops):
        at = offs[partner(insts, ops, i, core)]
        for b in range(MAXB):
            row = pl.multiple_of(jnp.minimum(at + b, blocks - 1) * BLK, BLK)
            sends[i][b * BLK : (b + 1) * BLK, :] = pool[pl.ds(row, BLK), :]


def query_kernel(
    stride, ops, table, queries_h, fresh_h, spread, fresh, own_q, sent_q, queries, sems
):
    steps, slots, width = queries.shape
    insts = table.shape[1]
    heads = width // HDIM
    rows = steps * heads
    core = lax.axis_index("tp")
    loads = start_copies([(queries_h, queries), (fresh_h, fresh)], sems)
    loads[0].wait()
    for s in range(steps):
        for h in range(heads):
            spread[pl.ds((s * heads + h) * stride, slots), :] = queries[
                s, :, h * HDIM : (h + 1) * HDIM
            ].astype(jnp.float32)
    for i in range(ops):
        j = table[0, partner(insts, ops, i, core)]
        own_q[i] = spread[pl.ds(j, rows, stride=stride), :].astype(jnp.bfloat16)
    for i in range(ops - 1):
        j = table[0, partner(insts, ops, i, 1 - core)]
        sent_q[i] = spread[pl.ds(j, rows, stride=stride), :].astype(jnp.bfloat16)
    loads[1].wait()


def contract_last(a, b):
    return lax.dot_general(a, b, (((1,), (1,)), ((), ())), preferred_element_type=jnp.float32)


def widest(score):
    return functools.reduce(
        jnp.maximum, [score[:, k : k + HDIM] for k in range(0, score.shape[1], HDIM)]
    )


def attend_all(scores, recents, values):
    scale = math.log2(math.e) / math.sqrt(HDIM)
    weights = []
    for score, recent in zip(scores, recents):
        top = jnp.max(jnp.maximum(widest(score), recent), axis=1, keepdims=True)
        cached = jnp.exp2((score - top) * scale)
        late = jnp.exp2((recent - top) * scale)
        folded = sum([cached[:, k : k + HDIM] for k in range(0, cached.shape[1], HDIM)], late)
        share = 1.0 / jnp.sum(folded, axis=1, keepdims=True)
        weights.append((cached.astype(jnp.bfloat16), late * share, share))
    return [
        (jnp.dot(cached, value, preferred_element_type=jnp.float32) * share, late)
        for (cached, late, share), value in zip(weights, values)
    ]


def stay_requests(stride, rows, group, first, count, size, lists, spread, pool, recent, attn, late):
    group = math.gcd(group, count)

    def some(g, _):
        places = [first + g * group + u for u in range(group)]
        picked = [pl.ds(lists[0, at], rows, stride=stride) for at in places]
        windows = [pl.ds(pl.multiple_of(lists[1, at] * BLK, BLK), size) for at in places]
        queries = [spread[at, :].astype(jnp.bfloat16) for at in picked]
        recents = [recent[at, :] for at in picked]
        scores = [contract_last(q, pool[w, :HDIM]) for q, w in zip(queries, windows)]
        done = attend_all(scores, recents, [pool[w, HDIM:] for w in windows])
        for at, (mixed, weight) in zip(picked, done):
            attn[at, :] = mixed
            late[at, :] = weight
        return 0

    lax.fori_loop(0, count // group, some, 0)


def stay_kernel(
    stride, steps, group, lists, spread, pool, fresh, weight_h,
    attn, peer_w, own_w, recent, late, sems,
):
    slots = lists.shape[1]
    rows = spread.shape[0] // stride
    heads = rows // steps
    half = peer_w.shape[1]
    core = lax.axis_index("tp")
    own_cols = pl.ds(pl.multiple_of(core * half, HDIM), half)
    peer_cols = pl.ds(pl.multiple_of((1 - core) * half, HDIM), half)
    loads = start_copies(
        [(weight_h.at[:, peer_cols], peer_w), (weight_h.at[:, own_cols], own_w)], sems
    )
    slot = lax.broadcasted_iota(jnp.int32, (slots, steps * slots), 0)
    col = lax.broadcasted_iota(jnp.int32, (slots, steps * slots), 1)
    for i in range(rows):
        at = pl.ds(i * stride, slots)
        score = contract_last(spread[at, :].astype(jnp.bfloat16), fresh[:, :HDIM])
        mine = (col % slots == slot) & (col // slots <= i // heads)
        recent[at, :] = jnp.where(mine, score, -jnp.inf)
    longer = pool.shape[0] // BLK - slots
    state = (lists, spread, pool, recent, attn, late)
    stay_requests(stride, rows, group, 0, longer, WIN, *state)
    stay_requests(stride, rows, group, longer, slots - longer, BLK, *state)
    for i in range(rows):
        at = pl.ds(i * stride, slots)
        attn[at, :] = attn[at, :] + jnp.dot(
            late[at, :].astype(jnp.bfloat16), fresh[:, HDIM:], preferred_element_type=jnp.float32
        )
    for load in loads:
        load.wait()


def recent_kernel(ops, steps, slots, after, table, own_q, peer_q, fresh, query, recent):
    rows = own_q.shape[1]
    heads = rows // steps
    insts = table.shape[1]
    core = lax.axis_index("tp")
    shape = (2 * rows, steps * slots)
    step = lax.broadcasted_iota(jnp.int32, shape, 0) // heads % steps
    col = lax.broadcasted_iota(jnp.int32, shape, 1)
    owner = jnp.where(col // slots <= step, col % slots, -1)
    for i in range(ops):
        count = 2 * rows if i < ops - 1 else rows
        query[i, 0:rows, :] = own_q[i]
        if i < ops - 1:
            query[i, rows:, :] = peer_q[i]
        score = contract_last(query[i, 0:count, :], fresh[:, :HDIM])
        j = table[0, partner(insts, ops, i, core)]
        recent[i, 0:count, :] = jnp.where(owner[:count] == j, score, -jnp.inf)


def move_kernel(ops, table, query, recent, fresh, *refs):
    blocks, (found, sent) = refs[:ops], refs[ops:]
    rows = found.shape[1]
    insts = table.shape[1]
    core = lax.axis_index("tp")
    within = lax.broadcasted_iota(jnp.int32, (2 * rows, WIN), 1)
    for first in range(0, ops, 4):
        batch = range(first, min(first + 4, ops))
        counts = [2 * rows if i < ops - 1 else rows for i in batch]
        scores = []
        for i, count in zip(batch, counts):
            score = contract_last(query[i, 0:count, :], blocks[i][:, :HDIM])
            limit = table[1, partner(insts, ops, i, core)] * BLK
            scores.append(jnp.where(within[:count] < limit, score, -jnp.inf))
        recents = [recent[i, 0:count, :] for i, count in zip(batch, counts)]
        done = attend_all(scores, recents, [blocks[i][:, HDIM:] for i in batch])
        for i, (mixed, weight) in zip(batch, done):
            out = mixed + jnp.dot(
                weight.astype(jnp.bfloat16), fresh[:, HDIM:], preferred_element_type=jnp.float32
            )
            found[i] = out[:rows]
            if i < ops - 1:
                sent[i] = out[rows:].astype(jnp.bfloat16)


def spots(insts, ops, core, slots, shape):
    row = lax.broadcasted_iota(jnp.int32, shape, 0)
    col = lax.broadcasted_iota(jnp.int32, shape, 1)
    same = row // slots == col // ops

    def of(table):
        hit = row < 0
        for i in range(ops - 1):
            j = table[0, partner(insts, ops, i, core)]
            hit = hit | ((col % ops == i) & (row % slots == j))
        return jnp.where(hit & same, 1.0, 0.0).astype(jnp.bfloat16)

    return of


def dot_tiles(lhs, weight, out):
    tile = math.gcd(WIN, out.shape[1])
    for n in range(0, out.shape[1], tile):
        out[:, n : n + tile] = jnp.dot(
            lhs[...], weight[:, n : n + tile], preferred_element_type=jnp.float32
        ).astype(out.dtype)


def project_kernel(
    ops, stride, table, attn, found, weight, partial, lhs, spot_in, spot_out, merged
):
    rows = found.shape[1]
    insts = table.shape[1]
    slots = stride - PAD
    steps = lhs.shape[0] // slots
    heads = rows // steps
    core = lax.axis_index("tp")
    merged[...] = attn[...]
    for i in range(ops):
        j = table[0, partner(insts, ops, i, core)]
        merged[pl.ds(j, rows, stride=stride), :] = found[i]
    for i in range(ops - 1):
        j = table[0, partner(insts, ops, i, 1 - core)]
        merged[pl.ds(j, rows, stride=stride), :] = jnp.zeros((rows, HDIM), jnp.float32)
    for s in range(steps):
        for h in range(heads):
            lhs[s * slots : (s + 1) * slots, h * HDIM : (h + 1) * HDIM] = merged[
                pl.ds((s * heads + h) * stride, slots), :
            ].astype(jnp.bfloat16)
    dot_tiles(lhs, weight, partial)
    spot_in[...] = spots(insts, ops, 1 - core, slots, spot_in.shape)(table)
    spot_out[...] = spots(insts, ops, core, slots, spot_out.shape)(table)


def late_kernel(ops, steps, arrived, weight, partial, lhs, spread):
    rows = arrived.shape[1]
    heads = rows // steps
    count = steps * ops
    spread[...] = jnp.zeros_like(spread)
    for i in range(ops - 1):
        value = arrived[i].astype(jnp.float32)
        for s in range(steps):
            spread[pl.ds(s * ops + i, heads, stride=count), :] = value[s * heads : (s + 1) * heads]
    for h in range(heads):
        lhs[:, h * HDIM : (h + 1) * HDIM] = spread[h * count : (h + 1) * count, :].astype(
            jnp.bfloat16
        )
    dot_tiles(lhs, weight, partial)


def own_kernel(lhs, late, spot, weight, out, full):
    tile = math.gcd(WIN, full.shape[1])
    for n in range(0, full.shape[1], tile):
        cols = slice(n, n + tile)
        placed = jnp.dot(spot[...], late[:, cols], preferred_element_type=jnp.float32)
        full[:, cols] = lhs[:, cols] + placed.astype(jnp.bfloat16)
    dot_tiles(full, weight, out)


def add_kernel(chunks, spot, own, others, late, out_h, out, sems):
    part = out.shape[0] // chunks
    copies = []
    for n in range(chunks):
        at = pl.ds(n * part, part)
        placed = jnp.dot(spot[at, :], late[...], preferred_element_type=jnp.float32)
        out[at, :] = (own[at, :] + others[at, :].astype(jnp.float32) + placed).astype(jnp.bfloat16)
        copies.append(pltpu.make_async_copy(out.at[at], out_h.at[at], sems.at[n]))
        copies[-1].start()
    for copy in copies:
        copy.wait()


def call(kernel, operands, outs, scratch=(), limit=8, cost=None, aliases=None):
    specs = [pl.BlockSpec(memory_space=space) for space, _ in operands]
    return pl.pallas_call(
        kernel,
        out_shape=[space(shape.shape, shape.dtype) for space, shape in outs],
        in_specs=specs,
        out_specs=[pl.BlockSpec(memory_space=space) for space, _ in outs],
        scratch_shapes=list(scratch),
        compiler_params=pltpu.CompilerParams(vmem_limit_bytes=limit * MIB),
        cost_estimate=cost,
        input_output_aliases=aliases or {},
    )(*[pltpu.with_memory_space_constraint(array, space) for space, array in operands])


def body(queries, new_kv, cache_pool, lengths, anchor, out_weight):
    steps, slots, width = queries.shape
    heads = width // HDIM
    rows = steps * heads
    insts = lax.axis_size("inst")
    cores = lax.axis_size("tp")
    kvw = cache_pool.shape[1]
    depth, columns = out_weight.shape
    half = columns // cores
    ops = insts // 2
    stride = slots + PAD
    hbm, vmem, smem = pltpu.HBM, pltpu.VMEM, pltpu.SMEM
    dma = pltpu.SemaphoreType.DMA

    def bf16(*shape):
        return jax.ShapeDtypeStruct(shape, jnp.bfloat16)

    def f32(*shape):
        return jax.ShapeDtypeStruct(shape, jnp.float32)

    table, lists, pool, *sends = call(
        functools.partial(plan_kernel, ops),
        [(hbm, anchor), (hbm, lengths), (hbm, cache_pool)],
        [
            (smem, jax.ShapeDtypeStruct((2, insts), jnp.int32)),
            (smem, jax.ShapeDtypeStruct((2, slots), jnp.int32)),
            (vmem, bf16(*cache_pool.shape)),
        ]
        + [(vmem, bf16(WIN, kvw))] * ops,
        [
            smem(anchor.shape, jnp.int32),
            smem(lengths.shape, jnp.int32),
            smem((insts,), jnp.int32),
            dma((2 + PARTS,)),
        ],
    )
    blocks = [None] * ops
    for i in reversed(range(ops)):
        pairs = []
        for a in range(insts):
            for c in range(cores):
                m = 1 if i == ops - 1 else insts - 2 - 2 * i + c
                pairs.append((a * cores + c, (a ^ m) * cores + c))
        blocks[i] = lax.ppermute(sends[i], ("inst", "tp"), pairs)

    spread, fresh, own_q, sent_q = call(
        functools.partial(query_kernel, stride, ops),
        [(smem, table), (hbm, queries), (hbm, new_kv.reshape(steps * slots, kvw))],
        [
            (vmem, f32(rows * stride, HDIM)),
            (vmem, bf16(steps * slots, kvw)),
            (vmem, bf16(ops, rows, HDIM)),
            (vmem, bf16(ops - 1, rows, HDIM)),
        ],
        [vmem(queries.shape, jnp.bfloat16), dma((2,))],
        cost=pl.CostEstimate(flops=0, bytes_accessed=MIB, transcendentals=0),
    )
    swap = [(c, cores - 1 - c) for c in range(cores)]
    peer_q = lax.ppermute(sent_q, "tp", swap)

    attn, peer_w, own_w = call(
        functools.partial(stay_kernel, stride, steps, 8),
        [(smem, lists), (vmem, spread), (vmem, pool), (vmem, fresh), (hbm, out_weight)],
        [(vmem, f32(rows * stride, HDIM))] + [(vmem, bf16(depth, half))] * 2,
        [
            vmem((rows * stride, HDIM), jnp.float32),
            vmem((rows * stride, HDIM), jnp.float32),
            dma((2,)),
        ],
        cost=pl.CostEstimate(
            flops=4 * slots * rows * WIN * HDIM, bytes_accessed=20 * MIB, transcendentals=0
        ),
    )
    query, recent = call(
        functools.partial(recent_kernel, ops, steps, slots),
        [(vmem, own_w), (smem, table), (vmem, own_q), (vmem, peer_q), (vmem, fresh)],
        [(vmem, bf16(ops, 2 * rows, HDIM)), (vmem, f32(ops, 2 * rows, steps * slots))],
    )
    found, sent = call(
        functools.partial(move_kernel, ops),
        [(smem, table), (vmem, query), (vmem, recent), (vmem, fresh)]
        + [(vmem, block) for block in blocks],
        [(vmem, f32(ops, rows, HDIM)), (vmem, bf16(ops - 1, rows, HDIM))],
    )
    arrived = lax.ppermute(sent, "tp", swap)
    tokens, few = steps * slots, steps * ops
    partial, lhs, spot_in, spot_out = call(
        functools.partial(project_kernel, ops, stride),
        [(smem, table), (vmem, attn), (vmem, found), (vmem, peer_w)],
        [
            (vmem, bf16(tokens, half)),
            (vmem, bf16(tokens, width)),
            (vmem, bf16(tokens, few)),
            (vmem, bf16(tokens, few)),
        ],
        [vmem((rows * stride, HDIM), jnp.float32)],
        cost=pl.CostEstimate(
            flops=2 * tokens * width * half, bytes_accessed=6 * MIB, transcendentals=0
        ),
    )
    others = lax.ppermute(partial, "tp", swap)
    partial, late = call(
        functools.partial(late_kernel, ops, steps),
        [(vmem, arrived), (vmem, peer_w)],
        [(vmem, bf16(few, half)), (vmem, bf16(few, width))],
        [vmem((rows * ops, HDIM), jnp.float32)],
    )
    late_others = lax.ppermute(partial, "tp", swap)
    (own,) = call(
        own_kernel,
        [(vmem, lhs), (vmem, late), (vmem, spot_in), (vmem, own_w)],
        [(vmem, f32(tokens, half))],
        [vmem((tokens, width), jnp.bfloat16)],
        cost=pl.CostEstimate(
            flops=100 * tokens * width * half, bytes_accessed=6 * MIB, transcendentals=0
        ),
    )
    (result,) = call(
        functools.partial(add_kernel, 4),
        [(vmem, spot_out), (vmem, own), (vmem, others), (vmem, late_others)],
        [(hbm, bf16(tokens, half))],
        [vmem((tokens, half), jnp.bfloat16), dma((4,))],
    )
    return result.reshape(steps, slots, half)


def solution(mesh):
    placed = (
        P(None, ("groups", "inst"), "tp"),
        P(None, ("groups", "inst"), None),
        P(("groups", "inst"), None),
        P("groups", None),
        P("groups", None),
        P("tp", None),
    )
    return jax.shard_map(
        body,
        mesh=mesh,
        in_specs=placed,
        out_specs=P(None, ("groups", "inst"), "tp"),
        check_vma=False,
    )
```
